128 devices in a mesh: row: 8 (over x, y_hi), col: 16 (over y_lo, z, core).
Axes of the slice: x: 4, y: 4 (y_hi: 2, y_lo: 2; y = y_hi * 2 + y_lo), z: 4, core: 2. Of those that a mesh axis runs over, the one named last changes fastest.
Arguments:
- feature_grid: bfloat16 [64, 4, 64, 1536], P('row', None, 'col'), may hold values from -40 to 40
- depthwise_kernel: bfloat16 [7, 7, 1536], replicated, may hold values from -0.875 to 0.875
- depthwise_bias: float32 [1536], replicated, may hold values from -3 to 3
- layer_norm_gain: float32 [1536], replicated, may hold values from 0.1 to 1.9
- layer_norm_shift: float32 [1536], replicated, may hold values from -3 to 3
- expansion_weight: bfloat16 [1536, 6144], P(None, 'col'), may hold values from -0.15625 to 0.15625
- expansion_bias: float32 [6144], P('col'), may hold values from -3 to 3
- reduction_weight: bfloat16 [6144, 1536], P('col'), may hold values from -0.078125 to 0.078125
- reduction_bias: float32 [1536], replicated, may hold values from -3 to 3
- layer_branch_scale: float32 [1536], replicated, may hold values from 0.5 to 2
- projector_weight: bfloat16 [1536, 8192], P(None, ('row', 'col')), may hold values from -8 to 8
- projector_bias: bfloat16 [8192], P(('row', 'col')), may hold values from -3 to 3
- input_norm_gain: bfloat16 [8192], P(('row', 'col')), may hold values from 0.099609375 to 1.8984375
- key_value_weight: bfloat16 [8192, 2048], P(('row', 'col')), may hold values from -0.0625 to 0.0625
- key_value_bias: float32 [2048], replicated, may hold values from -3 to 3
- adapter_down_weight: bfloat16 [8192, 128], P(('row', 'col')), may hold values from -0.0625 to 0.0625
- adapter_up_weight: bfloat16 [2, 64, 1024], replicated, may hold values from -0.75 to 0.75
- image_start_positions: int32 [4], replicated, may hold values from 1 to 14336, as said below
- key_value_cotangent: bfloat16 [256, 64, 2048], P(('row', 'col')), may hold values from -0.046875 to 0.046875
Outputs:
- keys_and_values: bfloat16 [256, 64, 2048], P(('row', 'col'))
- down_grad: float32 [8192, 128], P(('row', 'col'))
- up_grad: float32 [2, 64, 1024], replicated
The draws below stay inside these ranges and needn't reach their ends.
Inputs may be any that keep to these rules, and one draw needn't show every extreme that they name: `image_start_positions`: strictly increasing; text positions stand before each image, so the images' position ranges never meet.
All inputs are finite; a program needn't handle non-finite values.
Results may differ from the reference program's by a relative error of at most 0.022.
Values may be sent and summed in bfloat16 or wider, within the bound.
A program may use at most 192 MiB of HBM per device.

```python
import math
import jax
import jax.numpy as jnp
from jax import lax

ENC_C = 1536
ENC_HIDDEN = 6144
LANGUAGE_WIDTH = 8192
KV_HEADS = 8
HEAD_DIM = 128
ADAPTER_RANK = 64
IMAGES = 4
KEY_VALUE_WIDTH = 1024
GH = 64
GW = 64
SEQ_ROWS = 256
TOKENS = 16384
N_ROW = 8
N_COL = 16


def draw_feature_grid(key, part):
    key = jax.random.fold_in(key, 7)
    keys = jax.random.split(key, 4)
    array_dimensions = (GH, IMAGES, GW, ENC_C)
    values = jnp.clip(jax.random.normal(keys[0], array_dimensions, jnp.float32), -4.0, 4.0)
    spread = math.log(10.0)
    pixel_scale = jnp.exp(spread * (jax.random.uniform(keys[2], (GH, IMAGES, GW, 1), jnp.float32) - 0.5))
    channel_scale = jnp.exp(spread * (jax.random.uniform(keys[3], (1, 1, 1, ENC_C), jnp.float32) - 0.5))
    return jnp.clip(values * pixel_scale * channel_scale, -40.0, 40.0).astype(jnp.bfloat16)


def draw_projector_weight(key, part):
    key = jax.random.fold_in(key, 19)
    keys = jax.random.split(key, 2)
    array_dimensions = (ENC_C, LANGUAGE_WIDTH)
    values = jnp.clip(jax.random.normal(keys[0], array_dimensions, jnp.float32), -4.0, 4.0)
    trend = math.log(3.0)
    spread = math.log(10.0)
    feature = jnp.arange(LANGUAGE_WIDTH, dtype=jnp.int32)
    group_width = LANGUAGE_WIDTH // N_ROW
    overall = feature.astype(jnp.float32) / LANGUAGE_WIDTH
    within = (feature % group_width).astype(jnp.float32) / group_width
    scale = jnp.exp(0.5 * trend * (overall + within) + spread * (jax.random.uniform(keys[1], (LANGUAGE_WIDTH,), jnp.float32) - 0.5))
    return jnp.clip(values * scale / math.sqrt(ENC_C) * 4.0, -8.0, 8.0).astype(jnp.bfloat16)


def draw_image_start_positions(key, part):
    key = jax.random.fold_in(key, 31)
    text_gaps = jax.random.randint(key, (IMAGES,), 1, 513, dtype=jnp.int32)
    is_last = jnp.arange(IMAGES, dtype=jnp.int32) == IMAGES - 1
    earlier = jnp.sum(jnp.where(is_last, 0, text_gaps))
    text_gaps = jnp.where(is_last, 512 * IMAGES - earlier, text_gaps).astype(jnp.int32)
    return jnp.cumsum(text_gaps).astype(jnp.int32) + jnp.arange(IMAGES, dtype=jnp.int32) * (GH * GW)


def block_levels(own_key, extent, cuts, low, largest):
    def one(position, shards_of):
        steps = jax.random.uniform(jax.random.fold_in(jax.random.fold_in(own_key, 6), position), (shards_of,), jnp.float32, low / len(cuts), largest / len(cuts))
        return jnp.repeat(jnp.exp(steps), extent[position] // shards_of).reshape((-1,) + (1,) * (len(extent) - position - 1))

    factor_of = one(*cuts[0])
    for cut in cuts[1:]:
        factor_of = factor_of * one(*cut)
    return factor_of


def gaussian(key, extent, deviation, limit, cuts=(), kind=jnp.bfloat16):
    loudness = block_levels(key, extent, cuts, -0.22, 0.18) if cuts else 1.0
    drawn = jax.random.normal(key, extent, jnp.float32) * deviation * loudness
    return jnp.minimum(jnp.maximum(drawn, -limit), limit).astype(kind)


def setup_inputs(seed: int = 0) -> dict:
    seeds = jax.random.split(jax.random.key(seed), 20)
    feature_grid = draw_feature_grid(jax.random.fold_in(seeds[19], 71), 0)
    depthwise_kernel = gaussian(seeds[1], (7, 7, ENC_C), 49 ** -0.5, 0.875)
    depthwise_bias = gaussian(seeds[2], (ENC_C,), 0.5, 3.0, (), jnp.float32)
    layer_norm_gain = jnp.clip(1.0 + 0.18 * jax.random.normal(seeds[3], (ENC_C,), jnp.float32), 0.1, 1.9)
    layer_norm_shift = gaussian(seeds[4], (ENC_C,), 0.5, 3.0, (), jnp.float32)
    expansion_weight = gaussian(seeds[5], (ENC_C, ENC_HIDDEN), ENC_C ** -0.5, 0.15625, ((1, 16),))
    expansion_bias = gaussian(seeds[6], (ENC_HIDDEN,), 0.5, 3.0, ((0, 16),), jnp.float32)
    reduction_weight = gaussian(seeds[7], (ENC_HIDDEN, ENC_C), ENC_HIDDEN ** -0.5, 0.078125, ((0, 16),))
    reduction_bias = gaussian(seeds[8], (ENC_C,), 0.5, 3.0, (), jnp.float32)
    layer_branch_scale = jnp.clip(jnp.exp(jax.random.uniform(seeds[9], (ENC_C,), jnp.float32, math.log(0.5), math.log(2.0))), 0.5, 2.0)
    projector_weight = draw_projector_weight(jax.random.fold_in(seeds[19], 71), 0)
    projector_bias = gaussian(seeds[11], (LANGUAGE_WIDTH,), 0.5, 3.0, ((0, 128),))
    input_norm_gain = jnp.clip(1.0 + 0.18 * jax.random.normal(seeds[12], (LANGUAGE_WIDTH,), jnp.float32), 0.099609375, 1.8984375).astype(jnp.bfloat16)
    key_value_weight = gaussian(seeds[13], (LANGUAGE_WIDTH, 2 * KEY_VALUE_WIDTH), LANGUAGE_WIDTH ** -0.5, 0.0625, ((0, 128),))
    key_value_bias = gaussian(seeds[14], (2 * KEY_VALUE_WIDTH,), 0.5, 3.0, (), jnp.float32)
    adapter_down_weight = gaussian(seeds[15], (LANGUAGE_WIDTH, 2 * ADAPTER_RANK), LANGUAGE_WIDTH ** -0.5, 0.0625, ((0, 128),))
    adapter_up_weight = gaussian(seeds[16], (2, ADAPTER_RANK, KEY_VALUE_WIDTH), ADAPTER_RANK ** -0.5, 0.75)
    image_start_positions = draw_image_start_positions(jax.random.fold_in(seeds[19], 71), 0)
    key_value_cotangent = gaussian(seeds[18], (SEQ_ROWS, GW, 2 * KEY_VALUE_WIDTH), TOKENS ** -0.5, 0.046875, ((0, 128),))
    return dict(feature_grid=feature_grid, depthwise_kernel=depthwise_kernel, depthwise_bias=depthwise_bias, layer_norm_gain=layer_norm_gain, layer_norm_shift=layer_norm_shift, expansion_weight=expansion_weight, expansion_bias=expansion_bias, reduction_weight=reduction_weight, reduction_bias=reduction_bias, layer_branch_scale=layer_branch_scale, projector_weight=projector_weight, projector_bias=projector_bias, input_norm_gain=input_norm_gain, key_value_weight=key_value_weight, key_value_bias=key_value_bias, adapter_down_weight=adapter_down_weight, adapter_up_weight=adapter_up_weight, image_start_positions=image_start_positions, key_value_cotangent=key_value_cotangent)


adapter_scale = 0.5
rope_theta = 1000000.0

def depth_conv(padded, kernel, bias):
    out_rows = padded.shape[0] - 6
    out_cols = padded.shape[2] - 6
    accum = jnp.zeros((out_rows, padded.shape[1], out_cols, padded.shape[3]), jnp.float32) + bias
    for vertical in range(7):
        for horizontal in range(7):
            window = padded[vertical:vertical + out_rows, :, horizontal:horizontal + out_cols, :].astype(jnp.float32)
            accum = accum + window * kernel[vertical, horizontal].astype(jnp.float32)
    return accum

def channel_norm(values, gain, shift):
    center = lax.optimization_barrier(jnp.mean(values, axis=-1, keepdims=True))
    centered = values - center
    variance = lax.optimization_barrier(jnp.mean(centered * centered, axis=-1, keepdims=True))
    return centered * lax.rsqrt(variance + 1e-06) * gain + shift

def project_rows(tokens, weight, bias):
    flat_tokens = tokens.reshape(-1, tokens.shape[-1])
    result = jnp.dot(flat_tokens, weight, preferred_element_type=jnp.float32) + bias.astype(jnp.float32)
    return result.reshape(tokens.shape[:-1] + (weight.shape[1],))

def rms_scale(projected, squares, gain):
    return (projected * lax.rsqrt(squares[..., None] / LANGUAGE_WIDTH + 1e-06) * gain.astype(jnp.float32)).astype(jnp.bfloat16)

def linear_summands(normalized_rows, key_value_weight, adapter_down_weight):
    flattened_normed = normalized_rows.reshape(-1, normalized_rows.shape[-1])
    key_value_summand = jnp.dot(flattened_normed, key_value_weight, preferred_element_type=jnp.float32)
    adapter_summand = jnp.dot(flattened_normed, adapter_down_weight, preferred_element_type=jnp.float32)
    leading_dimensions = normalized_rows.shape[:-1]
    return (key_value_summand.reshape(leading_dimensions + (key_value_weight.shape[1],)), adapter_summand.reshape(leading_dimensions + (adapter_down_weight.shape[1],)))

def rotation(token_positions):
    half_dim = HEAD_DIM // 2
    freq_steps = jnp.arange(half_dim, dtype=jnp.float32)
    inverse = jnp.exp(freq_steps * (-2.0 * math.log(rope_theta) / HEAD_DIM))
    angle = token_positions.astype(jnp.float32)[..., None, None] * inverse
    return (jnp.cos(angle), jnp.sin(angle))

def rotate(values, cosine, sine_part, sign):
    shaped = values.reshape(values.shape[:-1] + (KV_HEADS, HEAD_DIM))
    half_dim = HEAD_DIM // 2
    leading = shaped[..., :half_dim]
    trailing = shaped[..., half_dim:]
    turned = jnp.concatenate([leading * cosine - sign * trailing * sine_part, trailing * cosine + sign * leading * sine_part], axis=-1)
    return turned.reshape(values.shape)

def finalize(key_value_sum, adapter_total_sum, key_value_bias, adapter_up_weight, token_positions, key_value_cotangent):
    seq_count, width_cols = (key_value_sum.shape[0], key_value_sum.shape[1])
    adapter_in = adapter_total_sum.astype(jnp.bfloat16)
    flattened_input = adapter_in.reshape(-1, 2 * ADAPTER_RANK)
    reduced_key = jnp.dot(flattened_input[:, :ADAPTER_RANK], adapter_up_weight[0], preferred_element_type=jnp.float32)
    reduced_value = jnp.dot(flattened_input[:, ADAPTER_RANK:], adapter_up_weight[1], preferred_element_type=jnp.float32)
    reduced_rank_part = jnp.concatenate([reduced_key, reduced_value], axis=1).reshape(seq_count, width_cols, 2 * KEY_VALUE_WIDTH)
    linear_map = key_value_sum + key_value_bias + adapter_scale * reduced_rank_part
    cosine, sine_part = rotation(token_positions)
    rotated_keys = rotate(linear_map[..., :KEY_VALUE_WIDTH], cosine, sine_part, 1.0)
    keys_and_values = jnp.concatenate([rotated_keys, linear_map[..., KEY_VALUE_WIDTH:]], axis=-1).astype(jnp.bfloat16)
    incoming = key_value_cotangent.astype(jnp.float32)
    key_back = rotate(incoming[..., :KEY_VALUE_WIDTH], cosine, sine_part, -1.0)
    linear_grad = jnp.concatenate([key_back, incoming[..., KEY_VALUE_WIDTH:]], axis=-1).astype(jnp.bfloat16)
    flattened_gradient = linear_grad.reshape(-1, 2 * KEY_VALUE_WIDTH)
    key_gradient = jnp.dot(flattened_gradient[:, :KEY_VALUE_WIDTH], adapter_up_weight[0].T, preferred_element_type=jnp.float32)
    value_gradient = jnp.dot(flattened_gradient[:, KEY_VALUE_WIDTH:], adapter_up_weight[1].T, preferred_element_type=jnp.float32)
    adapter_gradient = (adapter_scale * jnp.concatenate([key_gradient, value_gradient], axis=1)).astype(jnp.bfloat16)
    adapter_gradient = adapter_gradient.reshape(seq_count, width_cols, 2 * ADAPTER_RANK)
    key_up_weight = jnp.dot(flattened_input[:, :ADAPTER_RANK].T, flattened_gradient[:, :KEY_VALUE_WIDTH], preferred_element_type=jnp.float32)
    value_up_weight = jnp.dot(flattened_input[:, ADAPTER_RANK:].T, flattened_gradient[:, KEY_VALUE_WIDTH:], preferred_element_type=jnp.float32)
    up_weight_local = adapter_scale * jnp.stack([key_up_weight, value_up_weight])
    return (keys_and_values, adapter_gradient, up_weight_local)

def reference(feature_grid, depthwise_kernel, depthwise_bias, layer_norm_gain, layer_norm_shift, expansion_weight, expansion_bias, reduction_weight, reduction_bias, layer_branch_scale, projector_weight, projector_bias, input_norm_gain, key_value_weight, key_value_bias, adapter_down_weight, adapter_up_weight, image_start_positions, key_value_cotangent):
    padded = jnp.pad(feature_grid, ((3, 3), (0, 0), (3, 3), (0, 0)))
    normed = channel_norm(depth_conv(padded, depthwise_kernel, depthwise_bias), layer_norm_gain, layer_norm_shift).astype(jnp.bfloat16)
    tokens = normed.reshape(-1, ENC_C)
    block_size = ENC_HIDDEN // N_COL

    def add_block(index, accum):
        start_unit = (index * block_size).astype(jnp.int32)
        w_in = lax.dynamic_slice_in_dim(expansion_weight, start_unit, block_size, 1)
        b_in = lax.dynamic_slice_in_dim(expansion_bias, start_unit, block_size, 0)
        w_out = lax.dynamic_slice_in_dim(reduction_weight, start_unit, block_size, 0)
        hidden = jax.nn.gelu(jnp.dot(tokens, w_in, preferred_element_type=jnp.float32) + b_in, approximate=False).astype(jnp.bfloat16)
        block_term = jnp.dot(hidden, w_out, preferred_element_type=jnp.float32).astype(jnp.bfloat16)
        return accum + lax.optimization_barrier(block_term).astype(jnp.float32)
    branch_sum = lax.fori_loop(0, N_COL, add_block, jnp.zeros((tokens.shape[0], ENC_C), jnp.float32))
    encoded = (feature_grid.astype(jnp.float32) + layer_branch_scale * (branch_sum.reshape(feature_grid.shape) + reduction_bias)).astype(jnp.bfloat16)
    cotangent_rows = key_value_cotangent.reshape(GH, IMAGES, GW, 2 * KEY_VALUE_WIDTH)
    column_index = jnp.arange(GW, dtype=jnp.int32)

    def layer_row(carry, inputs):
        down_total, up_total = carry
        row_tokens, row_gradient, row_index = inputs
        token_positions = image_start_positions[:, None] + row_index * GW + column_index[None, :]
        projected = project_rows(row_tokens, projector_weight, projector_bias)
        normalized_rows = rms_scale(projected, lax.optimization_barrier(jnp.sum(projected * projected, axis=-1)), input_norm_gain)
        key_value_sum, adapter_total_sum = linear_summands(normalized_rows, key_value_weight, adapter_down_weight)
        keys_and_values, adapter_gradient, up_weight_local = finalize(key_value_sum, adapter_total_sum, key_value_bias, adapter_up_weight, token_positions, row_gradient)
        down_total = down_total + jnp.dot(normalized_rows.reshape(-1, LANGUAGE_WIDTH).T, adapter_gradient.reshape(-1, 2 * ADAPTER_RANK), preferred_element_type=jnp.float32)
        return ((down_total, up_total + up_weight_local), keys_and_values)
    start_carry = (jnp.zeros((LANGUAGE_WIDTH, 2 * ADAPTER_RANK), jnp.float32), jnp.zeros((2, ADAPTER_RANK, KEY_VALUE_WIDTH), jnp.float32))
    (down_grad, up_grad), keys_and_values = lax.scan(layer_row, start_carry, (encoded, cotangent_rows, jnp.arange(GH, dtype=jnp.int32)))
    return (keys_and_values.reshape(SEQ_ROWS, GW, 2 * KEY_VALUE_WIDTH), down_grad, up_grad)
```

```python
import functools
import math

import jax
import jax.numpy as jnp
from jax import lax
from jax.experimental import pallas as pl
from jax.experimental.pallas import tpu as pltpu
from jax.sharding import PartitionSpec as P

LANGUAGE_WIDTH = 8192
HEAD_DIM = 128
IMAGES = 4
CHANNELS = 1536
BLOCKS = 12
EXT = 1664
ROPE_THETA = 1000000.0
MESH = pl.DeviceIdType.MESH
BF = jnp.bfloat16
F32 = jnp.float32
COPIES = 160
SLOT_OF = {0: 0, 3: 1, 1: 2, 2: 3}
OFFSET = (0, -1, 1, 2)


def dot(a, b):
    return jnp.dot(a, b, preferred_element_type=F32)


def dot_tn(a, b):
    return lax.dot_general(a, b, (((0,), (0,)), ((), ())), preferred_element_type=F32)


def dot_nt(a, b):
    return lax.dot_general(a, b, (((1,), (1,)), ((), ())), preferred_element_type=F32)


def kernel(
    x_ref, taps_ref, vec_ref, w1_ref, w2_ref, b1_ref, pt_ref, gb_ref, gain_ref,
    up_ref, cos_ref, sin_ref, cot_ref, kvb_ref, perm_ref, seq_ref,
    kv_ref, down_ref, upg_ref,
    pad, conv, tok, wa, wb, ba, feat, acc, part, rs_in, stage_t, stage_b, seq_in,
    pb, quad, red_in, red_bias, mf, ext, lin, grad,
    ein, e_in1, e_in2, e_all, send, recv, lsem,
):
    row = lax.axis_index("row")
    col = lax.axis_index("col")
    x = row // 2
    y = (row % 2) * 2 + col // 8
    z = (col % 8) // 2
    core = col % 2
    ylo = y % 2
    plane = y * 4 + z
    pair = x * 2 + core

    def device(dx, dy, dz, dk):
        xx, yy, zz, kk = (x + dx + 4) % 4, (y + dy + 4) % 4, (z + dz + 4) % 4, (core + dk) % 2
        return (xx * 2 + yy // 2, (yy % 2) * 8 + zz * 2 + kk)

    ids = [0]

    def push(src, dst, target):
        n = ids[0]
        ids[0] += 1
        copy = pltpu.make_async_remote_copy(
            src_ref=src, dst_ref=dst, send_sem=send.at[n], recv_sem=recv.at[n],
            device_id=target, device_id_type=MESH,
        )
        copy.start()
        return copy

    planes = [(dy, dz) for dy in range(4) for dz in range(4) if (dy, dz) != (0, 0)]
    up_dev = ((row + 7) % 8, col)
    dn_dev = ((row + 1) % 8, col)
    lt_dev = (row, (col + 15) % 16)
    rt_dev = (row, (col + 1) % 16)
    other = device(0, 0, 0, 1)
    yflip = 1 - 2 * ylo

    partners = [up_dev, dn_dev, lt_dev, rt_dev]
    for dx in range(4):
        for dk in range(2):
            if (dx, dk) != (0, 0):
                partners.append(device(dx, 0, 0, dk))
    for dy, dz in planes:
        partners.append(device(0, dy, dz, 0))
    partners.append(device(0, yflip, 0, 1))
    barrier = pltpu.get_barrier_semaphore()
    for partner in partners:
        pl.semaphore_signal(barrier, inc=1, device_id=partner, device_id_type=MESH)
    copies0 = [
        pltpu.make_async_copy(x_ref, pad.at[3:7, 16:48], lsem.at[0]),
        pltpu.make_async_copy(w1_ref, wa.at[0], lsem.at[1]),
        pltpu.make_async_copy(w2_ref, wb.at[0], lsem.at[2]),
        pltpu.make_async_copy(b1_ref, ba.at[0], lsem.at[3]),
        pltpu.make_async_copy(pt_ref, pb.at[0, :, 0:EXT], lsem.at[4]),
        pltpu.make_async_copy(gb_ref.at[pair], pb.at[0, :, EXT:2048], lsem.at[5]),
    ]
    for copy in copies0:
        copy.start()
    pl.semaphore_wait(barrier, len(partners))

    h_up = push(x_ref.at[:, 0:16], pad.at[3:7, 48:64], up_dev)
    h_dn = push(x_ref.at[:, 16:32], pad.at[3:7, 0:16], dn_dev)
    h_rt = push(x_ref.at[1:4], pad.at[0:3, 16:48], rt_dev)
    h_lt = push(x_ref.at[0:3], pad.at[7:10, 16:48], lt_dev)
    gb_copies = []
    pt_copies = []
    for dx in (1, 3, 2):
        pt_copies.append(push(pt_ref, pb.at[2 * dx, :, 0:EXT], device(dx, 0, 0, 0)))
    for dx in range(4):
        for dk in range(2):
            if (dx, dk) != (0, 0):
                target_pair = ((x + dx) % 4) * 2 + (core + dk) % 2
                gb_copies.append(
                    push(gb_ref.at[target_pair], pb.at[2 * dx + dk, :, EXT:2048], device(dx, 0, 0, dk))
                )
    fwd_copies = [push(pt_ref, pb.at[1, :, 0:EXT], other)]
    w_core = [
        push(w1_ref, wa.at[1], other), push(w2_ref, wb.at[1], other), push(b1_ref, ba.at[1], other),
    ]
    w_y = [
        push(w1_ref, wa.at[2], device(0, 1, 0, 0)),
        push(w2_ref, wb.at[2], device(0, 3, 0, 0)),
        push(b1_ref, ba.at[2], device(0, 1, 0, 0)),
    ]

    cosine = cos_ref[...]
    sine = sin_ref[...]
    for head in range(8):
        lanes = slice(head * 128, head * 128 + 128)
        value = cot_ref[:, lanes].astype(F32)
        grad[:, lanes] = (value * cosine - pltpu.roll(value, 64, 1) * sine).astype(BF)
    grad[:, 1024:2048] = cot_ref[:, 1024:2048]
    adapter_grad = dot_nt(grad[...], up_ref[...]).astype(BF).astype(F32)
    for copy in copies0:
        copy.wait()
    for n in range(3):
        lanes = slice(n * 512, n * 512 + 512)
        feat[:, lanes] = dot(perm_ref[...], x_ref[:, :, lanes].reshape(128, 512))

    h_up.wait()
    h_dn.wait()

    @pl.when(row == 0)
    def _():
        pad[3:7, 0:16] = jnp.zeros((4, 16, CHANNELS), BF)

    @pl.when(row == 7)
    def _():
        pad[3:7, 48:64] = jnp.zeros((4, 16, CHANNELS), BF)

    corners = [
        push(pad.at[4:7, 0:16], pad.at[0:3, 0:16], rt_dev),
        push(pad.at[4:7, 48:64], pad.at[0:3, 48:64], rt_dev),
        push(pad.at[3:6, 0:16], pad.at[7:10, 0:16], lt_dev),
        push(pad.at[3:6, 48:64], pad.at[7:10, 48:64], lt_dev),
    ]

    for n, dx in enumerate((1, 3, 2)):
        pt_copies[n].wait()
        fwd_copies.append(push(pb.at[2 * dx, :, 0:EXT], pb.at[2 * dx + 1, :, 0:EXT], other))
    for copy in gb_copies:
        copy.wait()
    for copy in fwd_copies:
        copy.wait()

    def products(i, carry):
        left = pb[:, :, pl.ds(pl.multiple_of(i * 128, 128), 128)].reshape(512, 128)
        for t in range(3):
            block = pair * 3 + t
            shift = i + block - 17
            around = jnp.where(shift >= 13, shift - 13, shift)
            start = jnp.where(block < 17, 13 + t, around) * 128
            right = pb[:, :, pl.ds(pl.multiple_of(start, 128), 128)].reshape(512, 128)
            value = dot_tn(left, right).astype(BF)
            quad[pl.ds(i * 8, 8), :, t * 128:t * 128 + 128] = value.reshape(8, 16, 128)
        return carry

    lax.fori_loop(0, 13, products, 0)
    red_copies = []
    for n, (dy, dz) in enumerate(planes):
        target_plane = ((y + dy) % 4) * 4 + (z + dz) % 4
        target = device(0, dy, dz, 0)
        red_copies.append(push(quad.at[pl.ds(target_plane * 6, 6)], red_in.at[n], target))
        red_copies.append(push(quad.at[96:97], red_bias.at[n], target))

    h_rt.wait()
    h_lt.wait()
    for copy in corners:
        copy.wait()

    @pl.when(col == 0)
    def _():
        pad[0:3] = jnp.zeros((3, 64, CHANNELS), BF)

    @pl.when(col == 15)
    def _():
        pad[7:10] = jnp.zeros((3, 64, CHANNELS), BF)

    def conv_lanes(n, carry):
        lanes = pl.ds(pl.multiple_of(n * 128, 128), 128)
        sums = [jnp.zeros((32, 128), F32) + vec_ref[0:1, lanes] for _ in range(4)]
        for wp in range(10):
            full = pad[wp, :, lanes].astype(F32)
            moved = pltpu.roll(full, 60, 0)
            for a in range(7):
                start = 4 * (a + 1)
                window = full[start:start + 32] if a % 2 else moved[start - 4:start + 28]
                for w in range(max(0, wp - 6), min(3, wp) + 1):
                    tap = a * 7 + wp - w
                    sums[w] = sums[w] + window * taps_ref[tap:tap + 1, lanes]
        for w in range(4):
            conv[w, :, lanes] = sums[w]
        return carry

    lax.fori_loop(0, BLOCKS, conv_lanes, 0)

    def norm_rows(n, carry):
        w = n // 2
        rows = pl.ds(pl.multiple_of((n % 2) * 16, 16), 16)
        value = conv[w, rows, :]
        center = jnp.sum(value, axis=-1, keepdims=True) * (1.0 / CHANNELS)
        centered = value - center
        variance = jnp.sum(centered * centered, axis=-1, keepdims=True) * (1.0 / CHANNELS)
        value = centered * lax.rsqrt(variance + 1e-06) * vec_ref[1:2, :] + vec_ref[2:3, :]
        part[0, w, rows, :] = value.astype(BF)
        return carry

    lax.fori_loop(0, 8, norm_rows, 0)
    for n in range(3):
        lanes = slice(n * 512, n * 512 + 512)
        tok[0, :, lanes] = dot(perm_ref[...], part[0, :, :, lanes].reshape(128, 512)).astype(BF)
    t_next = push(tok.at[0], tok.at[1], device(0, 0, 1, 0))
    t_prev = push(tok.at[0], tok.at[2], device(0, 0, 3, 0))

    def mlp(slot, count, weights, first):
        rows = 128 * count
        tokens = tok[slot:slot + count].reshape(rows, CHANNELS)
        for index, s in enumerate(weights):
            pre = dot(tokens, wa[s]) + ba[s, 0:1, :]
            hidden = (0.5 * pre * (1.0 + lax.erf(pre * (0.5 ** 0.5)))).astype(BF)
            for n in range(3):
                lanes = slice(n * 512, n * 512 + 512)
                term = dot(hidden, wb[s, :, lanes])
                if first and index == 0:
                    acc[0:rows, lanes] = term
                else:
                    acc[0:rows, lanes] += term

    def scatter(slot):
        sent = []
        for tau in (1, 3, 2):
            into = SLOT_OF[(OFFSET[slot] - tau) % 4]
            peer = SLOT_OF[(-tau) % 4] - 1
            sent.append(
                push(part.at[slot, (z + tau) % 4], rs_in.at[peer, into], device(0, 0, tau, 0))
            )
        return sent

    scale = vec_ref[3:4, :]
    mlp(0, 1, (0,), True)
    for copy in w_core:
        copy.wait()
    mlp(0, 1, (1,), False)
    for copy in w_y:
        copy.wait()
    w_fwd = [
        push(wa.at[2], wa.at[3], other), push(wb.at[2], wb.at[3], other), push(ba.at[2], ba.at[3], other),
    ]
    t_next.wait()
    t_far0 = push(tok.at[1, 0:64], tok.at[3, 0:64], device(0, 0, 1, 0))
    t_prev.wait()
    t_far1 = push(tok.at[2, 64:128], tok.at[3, 64:128], device(0, 0, 3, 0))
    mlp(0, 1, (2,), False)
    for copy in w_fwd:
        copy.wait()
    mlp(0, 1, (3,), False)
    part[0] = (acc[0:128, :] * scale + (feat[...] + scale * vec_ref[4:5, :])).astype(BF).reshape(4, 32, CHANNELS)
    scatters = scatter(0)

    for copy in red_copies:
        copy.wait()
    mine = quad.at[pl.ds(plane * 6, 6)]

    def reduce_block(g, carry):
        total = quad[plane * 6 + g].astype(F32)
        for n in range(15):
            total = total + red_in[n, g].astype(F32)
        mf[pair, plane * 6 + g] = total.astype(BF)
        return carry

    lax.fori_loop(0, 6, reduce_block, 0)
    total = quad[96].astype(F32)
    for n in range(15):
        total = total + red_bias[n, 0].astype(F32)
    mf[pair, 96] = total.astype(BF)
    block = mf.at[pair, pl.ds(plane * 6, 6)]
    all_copies = [push(block, block, device(0, dy, dz, 0)) for dy, dz in planes]

    mlp(1, 2, (0, 1, 2, 3), True)
    for slot in (1, 2):
        part[slot] = (acc[128 * slot - 128:128 * slot, :] * scale).astype(BF).reshape(4, 32, CHANNELS)
        scatters += scatter(slot)
    for copy in all_copies:
        copy.wait()
    m_next = push(mf.at[pair], mf.at[pair], device(1, 0, 0, 0))
    m_prev = push(mf.at[pair], mf.at[pair], device(3, 0, 0, 0))
    m_core = [push(mf.at[pair], mf.at[pair], other)]
    t_far0.wait()
    t_far1.wait()
    mlp(3, 1, (0, 1, 2, 3), True)
    part[3] = (acc[0:128, :] * scale).astype(BF).reshape(4, 32, CHANNELS)
    scatters += scatter(3)
    for copy in scatters:
        copy.wait()

    for slot in range(4):
        for n in range(3):
            lanes = slice(n * 512, n * 512 + 512)
            value = part[slot, z, :, lanes].astype(F32)
            for peer in range(3):
                value = value + rs_in[peer, slot, :, lanes].astype(F32)
            for q in range(4):
                stage_t[q, (z + OFFSET[slot] + 4) % 4, :, lanes] = value[8 * q:8 * q + 8]
    for q in range(4):
        stage_b[q] = stage_t[q].reshape(32, CHANNELS).astype(BF)
    my_q = ylo * 2 + core
    seq_copies = []
    for dy in range(2):
        for dk in range(2):
            if (dy, dk) != (0, 0):
                q = ((ylo + dy) % 2) * 2 + (core + dk) % 2
                seq_copies.append(push(stage_b.at[q], seq_in.at[my_q], device(0, dy * yflip, 0, dk)))
    seq_in[my_q] = stage_b[my_q]

    x_prev = ((x + 3) % 4) * 2 + core
    x_next = ((x + 1) % 4) * 2 + core
    x_far = ((x + 2) % 4) * 2 + core
    m_next.wait()
    far0 = push(mf.at[x_prev, 0:48], mf.at[x_prev, 0:48], device(1, 0, 0, 0))
    m_core.append(push(mf.at[x_prev], mf.at[x_prev], other))
    m_prev.wait()
    far1 = push(mf.at[x_next, 48:97], mf.at[x_next, 48:97], device(3, 0, 0, 0))
    m_core.append(push(mf.at[x_next], mf.at[x_next], other))
    for copy in seq_copies:
        copy.wait()
    for n in range(3):
        lanes = slice(n * 512, n * 512 + 512)
        tok[0, :, lanes] = dot(seq_ref[...], seq_in[:, :, lanes].reshape(128, 512)).astype(BF)
    for b in range(19):
        if b % 13 == 12:
            ext[:, b * 128:b * 128 + 128] = jnp.where(
                lax.broadcasted_iota(jnp.int32, (128, 128), 1) == 0, 1.0, 0.0
            )
        else:
            lanes = slice((b % 13) * 128, (b % 13) * 128 + 128)
            ext[:, b * 128:b * 128 + 128] = tok[0, :, lanes].astype(F32)
    far0.wait()
    far1.wait()
    m_core.append(push(mf.at[x_far], mf.at[x_far], other))
    for copy in m_core:
        copy.wait()

    encoded = tok[0]

    def squares_of(i, total):
        cells = tok[0, :, pl.ds(pl.multiple_of(i * 128, 128), 128)]
        groups = pl.ds(i * 8, 8)

        def other_block(d):
            return ext[:, pl.ds(pl.multiple_of((i + d) * 128, 128), 128)]

        total = total + dot(cells, mf[5, groups, :, 256:384].reshape(128, 128)) * other_block(0)
        for j in (6, 7):
            value = 2.0 * dot(cells, mf[j, groups].reshape(128, 384))
            for t in range(3):
                total = total + value[:, t * 128:t * 128 + 128] * other_block((j - 6) * 3 + t + 1)
        return total

    total = lax.fori_loop(0, BLOCKS, squares_of, jnp.zeros((128, 128), F32))
    for d in range(7):
        j, t = (17 + d) // 3, (17 + d) % 3
        weight = mf[j, 96, :, t * 128:t * 128 + 128].astype(F32)[0:1]
        total = total + (1.0 if d == 0 else 2.0) * weight * ext[:, (12 + d) * 128:(13 + d) * 128]
    squares = jnp.maximum(jnp.sum(total, axis=-1, keepdims=True), 0.0)
    inverse = lax.rsqrt(squares * (1.0 / LANGUAGE_WIDTH) + 1e-06)
    for j in range(6):
        bias = mf[j, 96].astype(F32)[0:1]
        lin[:, j * 384:j * 384 + 384] = inverse * (dot(encoded, mf[j, 0:96].reshape(CHANNELS, 384)) + bias)
    adapter_in = lin[:, 2048:2176].astype(BF)
    for n in range(8):
        lanes = slice(n * 256, n * 256 + 256)
        value = lin[:, lanes] + kvb_ref[0:1, lanes] + dot(adapter_in, up_ref[:, lanes])
        if n < 4:
            for h in range(2):
                head = value[:, h * 128:h * 128 + 128]
                turned = head * cosine + pltpu.roll(head, 64, 1) * sine
                kv_ref[:, n * 256 + h * 128:n * 256 + h * 128 + 128] = turned.astype(BF)
        else:
            kv_ref[:, lanes] = value.astype(BF)

    weighted = (inverse * adapter_grad).astype(BF)
    for n in range(3):
        value = dot_tn(encoded[:, n * 512:n * 512 + 512], weighted)
        ein[n * 32:n * 32 + 32] = value.astype(BF).reshape(32, 16, 128)
    shifted = jnp.sum(weighted.astype(F32), axis=0, keepdims=True)
    ein[96] = jnp.where(lax.broadcasted_iota(jnp.int32, (16, 128), 0) == 0, shifted, 0.0).astype(BF)
    for n in range(16):
        value = dot_tn(adapter_in, grad[:, n * 128:n * 128 + 128])
        value = value[0:64] if n < 8 else value[64:128]
        ein[97 + 4 * n:101 + 4 * n] = (0.5 * value).astype(BF).reshape(4, 16, 128)
    ein[161:176] = jnp.zeros((15, 16, 128), BF)
    sums = []
    for n, (dy, dz) in enumerate(planes):
        target_plane = ((y + dy) % 4) * 4 + (z + dz) % 4
        sums.append(push(ein.at[pl.ds(target_plane * 11, 11)], e_in1.at[n], device(0, dy, dz, 0)))
    for copy in sums:
        copy.wait()
    value = ein[pl.ds(plane * 11, 11)].astype(F32)
    for n in range(15):
        value = value + e_in1[n].astype(F32)
    e_in2[pair] = value.astype(BF)
    sums = []
    for dx in range(4):
        for dk in range(2):
            if (dx, dk) != (0, 0):
                sums.append(push(e_in2.at[pair], e_in2.at[pair], device(dx, 0, 0, dk)))
    for copy in sums:
        copy.wait()
    value = e_in2[0].astype(F32)
    for n in range(1, 8):
        value = value + e_in2[n].astype(F32)
    mine = e_all.at[pl.ds(plane * 11, 11)]
    mine[...] = value.astype(BF)
    sums = [push(mine, mine, device(0, dy, dz, 0)) for dy, dz in planes]
    for copy in sums:
        copy.wait()
    down_ref[...] = dot(pt_ref[...], e_all[0:104].reshape(EXT, 128)) * gain_ref[...]
    for n in range(16):
        lanes = slice((n % 8) * 128, (n % 8) * 128 + 128)
        upg_ref[n // 8, :, lanes] = e_all[97 + 4 * n:101 + 4 * n].reshape(64, 128).astype(F32)


def orders():
    tile = [[0.0] * 128 for _ in range(128)]
    seq = [[0.0] * 128 for _ in range(128)]
    for w in range(4):
        for h in range(8):
            for i in range(4):
                tile[(h % 4) * 32 + (h // 4) * 16 + (i // 2) * 8 + w * 2 + i % 2][w * 32 + h * 4 + i] = 1.0
    for ys in range(2):
        for cs in range(2):
            for zs in range(4):
                for w in range(4):
                    for i in range(2):
                        here = (ys * 2 + cs) * 32 + zs * 8 + w * 2 + i
                        seq[i * 64 + ys * 32 + zs * 8 + cs * 4 + w][here] = 1.0
    return jnp.array(tile, BF), jnp.array(seq, BF)


def local(
    feature_grid, depthwise_kernel, depthwise_bias, layer_norm_gain, layer_norm_shift,
    expansion_weight, expansion_bias, reduction_weight, reduction_bias, layer_branch_scale,
    projector_weight, projector_bias, input_norm_gain, key_value_weight, key_value_bias,
    adapter_down_weight, adapter_up_weight, image_start_positions, key_value_cotangent,
):
    device_block = lax.axis_index("row") * 16 + lax.axis_index("col")
    seq_index = device_block * 2 + jnp.arange(2, dtype=jnp.int32)
    match = (seq_index % IMAGES)[:, None] == jnp.arange(IMAGES, dtype=jnp.int32)[None, :]
    offsets = jnp.sum(jnp.where(match, image_start_positions[None, :], 0), axis=1)
    positions = (offsets + seq_index // IMAGES * 64)[:, None] + jnp.arange(64, dtype=jnp.int32)[None, :]
    freq_steps = jnp.arange(HEAD_DIM // 2, dtype=F32)
    inverse = jnp.exp(freq_steps * (-2.0 * math.log(ROPE_THETA) / HEAD_DIM))
    angle = positions.astype(F32).reshape(128, 1) * inverse
    cosine, sine = jnp.cos(angle), jnp.sin(angle)
    cosine = jnp.concatenate([cosine, cosine], axis=1)
    sine = jnp.concatenate([-sine, sine], axis=1)

    cells = feature_grid.transpose(2, 0, 1, 3).reshape(4, 32, CHANNELS)
    taps = depthwise_kernel.reshape(49, CHANNELS).astype(F32)
    vectors = jnp.stack(
        [depthwise_bias, layer_norm_gain, layer_norm_shift, layer_branch_scale, reduction_bias]
        + [jnp.zeros_like(depthwise_bias)] * 3
    )
    b1 = jnp.broadcast_to(expansion_bias[None, :], (8, 384))
    pt = jnp.concatenate(
        [projector_weight.T, projector_bias[:, None], jnp.zeros((64, 127), BF)], axis=1
    )
    gain = input_norm_gain.astype(F32)[:, None]
    gb = jnp.concatenate([key_value_weight, adapter_down_weight], axis=1).astype(F32) * gain
    gb = jnp.pad(gb.astype(BF), ((0, 0), (0, 896))).reshape(64, 8, 384).transpose(1, 0, 2)
    half = (adapter_up_weight.astype(F32) * 0.5).astype(BF)
    zero = jnp.zeros((64, 1024), BF)
    up = jnp.concatenate(
        [jnp.concatenate([half[0], zero], axis=1), jnp.concatenate([zero, half[1]], axis=1)], axis=0
    )
    tile_order, seq_order = orders()
    vmem = pl.BlockSpec(memory_space=pltpu.VMEM)
    kv, down, upg = pl.pallas_call(
        kernel,
        out_shape=(
            jax.ShapeDtypeStruct((128, 2048), BF),
            jax.ShapeDtypeStruct((64, 128), F32),
            jax.ShapeDtypeStruct((2, 64, 1024), F32),
        ),
        in_specs=[vmem] * 16,
        out_specs=(vmem, vmem, vmem),
        scratch_shapes=[
            pltpu.VMEM((10, 64, CHANNELS), BF),
            pltpu.VMEM((4, 32, CHANNELS), F32),
            pltpu.VMEM((4, 128, CHANNELS), BF),
            pltpu.VMEM((4, CHANNELS, 384), BF),
            pltpu.VMEM((4, 384, CHANNELS), BF),
            pltpu.VMEM((4, 8, 384), F32),
            pltpu.VMEM((128, CHANNELS), F32),
            pltpu.VMEM((256, CHANNELS), F32),
            pltpu.VMEM((4, 4, 32, CHANNELS), BF),
            pltpu.VMEM((3, 4, 32, CHANNELS), BF),
            pltpu.VMEM((4, 4, 8, CHANNELS), F32),
            pltpu.VMEM((4, 32, CHANNELS), BF),
            pltpu.VMEM((4, 32, CHANNELS), BF),
            pltpu.VMEM((8, 64, 2048), BF),
            pltpu.VMEM((104, 16, 384), BF),
            pltpu.VMEM((15, 6, 16, 384), BF),
            pltpu.VMEM((15, 1, 16, 384), BF),
            pltpu.VMEM((8, 97, 16, 384), BF),
            pltpu.VMEM((128, 19 * 128), F32),
            pltpu.VMEM((128, 2304), F32),
            pltpu.VMEM((128, 2048), BF),
            pltpu.VMEM((176, 16, 128), BF),
            pltpu.VMEM((15, 11, 16, 128), BF),
            pltpu.VMEM((8, 11, 16, 128), BF),
            pltpu.VMEM((176, 16, 128), BF),
            pltpu.SemaphoreType.DMA((COPIES,)),
            pltpu.SemaphoreType.DMA((COPIES,)),
            pltpu.SemaphoreType.DMA((6,)),
        ],
        compiler_params=pltpu.CompilerParams(
            collective_id=0, has_side_effects=True, vmem_limit_bytes=62 << 20
        ),
        cost_estimate=pl.CostEstimate(flops=8_000_000_000, bytes_accessed=30_000_000, transcendentals=0),
    )(
        cells, taps, vectors, expansion_weight, reduction_weight, b1, pt, gb, gain,
        up, cosine, sine, key_value_cotangent.reshape(128, 2048), key_value_bias[None, :], tile_order, seq_order,
    )
    return kv.reshape(2, 64, 2048), down, upg


def solution(mesh):
    in_specs = (
        P("row", None, "col", None), P(), P(), P(), P(),
        P(None, "col"), P("col"), P("col", None), P(), P(),
        P(None, ("row", "col")), P(("row", "col")), P(("row", "col")), P(("row", "col"), None), P(),
        P(("row", "col"), None), P(), P(), P(("row", "col"), None, None),
    )
    out_specs = (P(("row", "col"), None, None), P(("row", "col"), None), P())
    return jax.shard_map(local, mesh=mesh, in_specs=in_specs, out_specs=out_specs, check_vma=False)
```

```python
import functools
import math

import jax
import jax.numpy as jnp
from jax import lax
from jax.experimental import pallas as pl
from jax.experimental.pallas import tpu as pltpu
from jax.sharding import PartitionSpec as P

LANGUAGE_WIDTH = 8192
HEAD_DIM = 128
IMAGES = 4
CHANNELS = 1536
BLOCKS = 12
EXT = 1664
ROPE_THETA = 1000000.0
MESH = pl.DeviceIdType.MESH
BF = jnp.bfloat16
F32 = jnp.float32
COPIES = 200
SLOT_OF = {0: 0, 3: 1, 1: 2, 2: 3}
OFFSET = (0, -1, 1, 2)


def dot(a, b):
    return jnp.dot(a, b, preferred_element_type=F32)


def dot_tn(a, b):
    return lax.dot_general(a, b, (((0,), (0,)), ((), ())), preferred_element_type=F32)


def dot_nt(a, b):
    return lax.dot_general(a, b, (((1,), (1,)), ((), ())), preferred_element_type=F32)


def kernel(
    x_ref, taps_ref, vec_ref, w1_ref, w2_ref, b1_ref, pt_ref, gb_ref, gain_ref,
    up_ref, cos_ref, sin_ref, cot_ref, kvb_ref, perm_ref, seq_ref,
    kv_ref, down_ref, upg_ref,
    pad, conv, tok, wa, wb, ba, feat, acc, part, rs_in, stage_t, stage_b, seq_in,
    pb, quad, red_z, red_mid, red_y, red_bias, mf, ext, lin, grad,
    ein, e_in1, e_in2, e_all, send, recv, lsem,
):
    row = lax.axis_index("row")
    col = lax.axis_index("col")
    x = row // 2
    y = (row % 2) * 2 + col // 8
    z = (col % 8) // 2
    core = col % 2
    ylo = y % 2
    plane = y * 4 + z
    pair = x * 2 + core

    def device(dx, dy, dz, dk):
        xx, yy, zz, kk = (x + dx + 4) % 4, (y + dy + 4) % 4, (z + dz + 4) % 4, (core + dk) % 2
        return (xx * 2 + yy // 2, (yy % 2) * 8 + zz * 2 + kk)

    ids = [0]

    def push(src, dst, target):
        n = ids[0]
        ids[0] += 1
        copy = pltpu.make_async_remote_copy(
            src_ref=src, dst_ref=dst, send_sem=send.at[n], recv_sem=recv.at[n],
            device_id=target, device_id_type=MESH,
        )
        copy.start()
        return copy

    planes = [(dy, dz) for dy in range(4) for dz in range(4) if (dy, dz) != (0, 0)]
    up_dev = ((row + 7) % 8, col)
    dn_dev = ((row + 1) % 8, col)
    lt_dev = (row, (col + 15) % 16)
    rt_dev = (row, (col + 1) % 16)
    other = device(0, 0, 0, 1)
    yflip = 1 - 2 * ylo

    partners = [up_dev, dn_dev, lt_dev, rt_dev]
    for dx in range(4):
        for dk in range(2):
            if (dx, dk) != (0, 0):
                partners.append(device(dx, 0, 0, dk))
    for dy, dz in planes:
        partners.append(device(0, dy, dz, 0))
    partners.append(device(0, yflip, 0, 1))
    barrier = pltpu.get_barrier_semaphore()
    for partner in partners:
        pl.semaphore_signal(barrier, inc=1, device_id=partner, device_id_type=MESH)
    copies0 = [
        pltpu.make_async_copy(x_ref, pad.at[3:7, 16:48], lsem.at[0]),
        pltpu.make_async_copy(w1_ref, wa.at[0], lsem.at[1]),
        pltpu.make_async_copy(w2_ref, wb.at[0], lsem.at[2]),
        pltpu.make_async_copy(b1_ref, ba.at[0], lsem.at[3]),
        pltpu.make_async_copy(pt_ref, pb.at[0, :, 0:EXT], lsem.at[4]),
        pltpu.make_async_copy(gb_ref.at[pair], pb.at[0, :, EXT:2048], lsem.at[5]),
    ]
    for copy in copies0:
        copy.start()
    pl.semaphore_wait(barrier, len(partners))

    h_up = push(x_ref.at[:, 0:16], pad.at[3:7, 48:64], up_dev)
    h_dn = push(x_ref.at[:, 16:32], pad.at[3:7, 0:16], dn_dev)
    h_rt = push(x_ref.at[1:4], pad.at[0:3, 16:48], rt_dev)
    h_lt = push(x_ref.at[0:3], pad.at[7:10, 16:48], lt_dev)
    gb_copies = []
    pt_copies = []
    for dx in (1, 3, 2):
        pt_copies.append(push(pt_ref, pb.at[2 * dx, :, 0:EXT], device(dx, 0, 0, 0)))
    for dx in range(4):
        for dk in range(2):
            if (dx, dk) != (0, 0):
                target_pair = ((x + dx) % 4) * 2 + (core + dk) % 2
                gb_copies.append(
                    push(gb_ref.at[target_pair], pb.at[2 * dx + dk, :, EXT:2048], device(dx, 0, 0, dk))
                )
    fwd_copies = [push(pt_ref, pb.at[1, :, 0:EXT], other)]
    w_core = [
        push(w1_ref, wa.at[1], other), push(w2_ref, wb.at[1], other), push(b1_ref, ba.at[1], other),
    ]
    w_y = [
        push(w1_ref, wa.at[2], device(0, 1, 0, 0)),
        push(w2_ref, wb.at[2], device(0, 3, 0, 0)),
        push(b1_ref, ba.at[2], device(0, 1, 0, 0)),
    ]

    cosine = cos_ref[...]
    sine = sin_ref[...]
    for head in range(8):
        lanes = slice(head * 128, head * 128 + 128)
        value = cot_ref[:, lanes].astype(F32)
        grad[:, lanes] = (value * cosine - pltpu.roll(value, 64, 1) * sine).astype(BF)
    grad[:, 1024:2048] = cot_ref[:, 1024:2048]
    adapter_grad = dot_nt(grad[...], up_ref[...]).astype(BF).astype(F32)
    for copy in copies0:
        copy.wait()
    for n in range(3):
        lanes = slice(n * 512, n * 512 + 512)
        feat[:, lanes] = dot(perm_ref[...], x_ref[:, :, lanes].reshape(128, 512))

    h_up.wait()
    h_dn.wait()

    @pl.when(row == 0)
    def _():
        pad[3:7, 0:16] = jnp.zeros((4, 16, CHANNELS), BF)

    @pl.when(row == 7)
    def _():
        pad[3:7, 48:64] = jnp.zeros((4, 16, CHANNELS), BF)

    corners = [
        push(pad.at[4:7, 0:16], pad.at[0:3, 0:16], rt_dev),
        push(pad.at[4:7, 48:64], pad.at[0:3, 48:64], rt_dev),
        push(pad.at[3:6, 0:16], pad.at[7:10, 0:16], lt_dev),
        push(pad.at[3:6, 48:64], pad.at[7:10, 48:64], lt_dev),
    ]

    for n, dx in enumerate((1, 3, 2)):
        pt_copies[n].wait()
        fwd_copies.append(push(pb.at[2 * dx, :, 0:EXT], pb.at[2 * dx + 1, :, 0:EXT], other))
    for copy in gb_copies:
        copy.wait()
    for copy in fwd_copies:
        copy.wait()

    def products(i, carry):
        left = pb[:, :, pl.ds(pl.multiple_of(i * 128, 128), 128)].reshape(512, 128)
        for t in range(3):
            block = pair * 3 + t
            shift = i + block - 17
            around = jnp.where(shift >= 13, shift - 13, shift)
            start = jnp.where(block < 17, 13 + t, around) * 128
            right = pb[:, :, pl.ds(pl.multiple_of(start, 128), 128)].reshape(512, 128)
            value = dot_tn(left, right).astype(BF).reshape(4, 2, 16, 128)
            for r in range(4):
                p = i * 4 + r
                quad[p // 12, p % 12, :, :, t * 128:t * 128 + 128] = value[r]
        return carry

    lax.fori_loop(0, 13, products, 0)
    red_copies = []
    for n, dz in enumerate((1, 3, 2)):
        target = device(0, 0, dz, 0)
        red_copies.append(push(quad.at[0:4, pl.ds(((z + dz) % 4) * 3, 3)], red_z.at[n], target))
        red_copies.append(push(quad.at[4, 0, 0], red_bias.at[n], target))

    h_rt.wait()
    h_lt.wait()
    for copy in corners:
        copy.wait()

    @pl.when(col == 0)
    def _():
        pad[0:3] = jnp.zeros((3, 64, CHANNELS), BF)

    @pl.when(col == 15)
    def _():
        pad[7:10] = jnp.zeros((3, 64, CHANNELS), BF)

    def conv_lanes(n, carry):
        lanes = pl.ds(pl.multiple_of(n * 128, 128), 128)
        sums = [jnp.zeros((32, 128), F32) + vec_ref[0:1, lanes] for _ in range(4)]
        for wp in range(10):
            full = pad[wp, :, lanes].astype(F32)
            moved = pltpu.roll(full, 60, 0)
            for a in range(7):
                start = 4 * (a + 1)
                window = full[start:start + 32] if a % 2 else moved[start - 4:start + 28]
                for w in range(max(0, wp - 6), min(3, wp) + 1):
                    tap = a * 7 + wp - w
                    sums[w] = sums[w] + window * taps_ref[tap:tap + 1, lanes]
        for w in range(4):
            conv[w, :, lanes] = sums[w]
        return carry

    lax.fori_loop(0, BLOCKS, conv_lanes, 0)

    def norm_rows(n, carry):
        w = n // 2
        rows = pl.ds(pl.multiple_of((n % 2) * 16, 16), 16)
        value = conv[w, rows, :]
        center = jnp.sum(value, axis=-1, keepdims=True) * (1.0 / CHANNELS)
        centered = value - center
        variance = jnp.sum(centered * centered, axis=-1, keepdims=True) * (1.0 / CHANNELS)
        value = centered * lax.rsqrt(variance + 1e-06) * vec_ref[1:2, :] + vec_ref[2:3, :]
        part[0, w, rows, :] = value.astype(BF)
        return carry

    lax.fori_loop(0, 8, norm_rows, 0)
    for n in range(3):
        lanes = slice(n * 512, n * 512 + 512)
        tok[0, :, lanes] = dot(perm_ref[...], part[0, :, :, lanes].reshape(128, 512)).astype(BF)
    t_next = push(tok.at[0], tok.at[1], device(0, 0, 1, 0))
    t_prev = push(tok.at[0], tok.at[2], device(0, 0, 3, 0))

    def mlp(slot, count, weights, first):
        rows = 128 * count
        tokens = tok[slot:slot + count].reshape(rows, CHANNELS)
        for index, s in enumerate(weights):
            pre = dot(tokens, wa[s]) + ba[s, 0:1, :]
            hidden = (0.5 * pre * (1.0 + lax.erf(pre * (0.5 ** 0.5)))).astype(BF)
            for n in range(3):
                lanes = slice(n * 512, n * 512 + 512)
                term = dot(hidden, wb[s, :, lanes])
                if first and index == 0:
                    acc[0:rows, lanes] = term
                else:
                    acc[0:rows, lanes] += term

    def scatter(slot):
        sent = []
        for tau in (1, 3, 2):
            into = SLOT_OF[(OFFSET[slot] - tau) % 4]
            peer = SLOT_OF[(-tau) % 4] - 1
            sent.append(
                push(part.at[slot, (z + tau) % 4], rs_in.at[peer, into], device(0, 0, tau, 0))
            )
        return sent

    scale = vec_ref[3:4, :]
    mlp(0, 1, (0,), True)
    for copy in w_core:
        copy.wait()
    mlp(0, 1, (1,), False)

    for copy in red_copies:
        copy.wait()

    def sum_z(n, carry):
        h, p = n // 3, n % 3
        total = quad[h, z * 3 + p].astype(F32)
        for m in range(3):
            total = total + red_z[m, h, p].astype(F32)
        red_mid[h, p] = total.astype(BF)
        return carry

    lax.fori_loop(0, 12, sum_z, 0)
    total = quad[4, 0, 0].astype(F32)
    for m in range(3):
        total = total + red_bias[m].astype(F32)
    red_bias[6] = total.astype(BF)
    red_copies = []
    for n, dy in enumerate((1, 3, 2)):
        target = device(0, dy, 0, 0)
        red_copies.append(push(red_mid.at[(y + dy) % 4], red_y.at[n], target))
        red_copies.append(push(red_bias.at[6], red_bias.at[3 + n], target))
    t_next.wait()
    t_far0 = push(tok.at[1, 0:64], tok.at[3, 0:64], device(0, 0, 1, 0))
    t_prev.wait()
    t_far1 = push(tok.at[2, 64:128], tok.at[3, 64:128], device(0, 0, 3, 0))
    for copy in red_copies:
        copy.wait()

    def sum_y(p, carry):
        total = red_mid[y, p].astype(F32)
        for m in range(3):
            total = total + red_y[m, p].astype(F32)
        mf[pair, pl.ds(plane * 6 + p * 2, 2)] = total.astype(BF)
        return carry

    lax.fori_loop(0, 3, sum_y, 0)
    total = red_bias[6].astype(F32)
    for m in range(3):
        total = total + red_bias[3 + m].astype(F32)
    mf[pair, 96] = total.astype(BF)
    block = mf.at[pair, pl.ds(plane * 6, 6)]
    all_z = [push(block, block, device(0, 0, dz, 0)) for dz in (1, 3, 2)]
    m_bias = [push(mf.at[pair, 96], mf.at[pair, 96], device(dx, 0, 0, 0)) for dx in (1, 3, 2)]
    for copy in w_y:
        copy.wait()
    w_fwd = [
        push(wa.at[2], wa.at[3], other), push(wb.at[2], wb.at[3], other), push(ba.at[2], ba.at[3], other),
    ]
    mlp(0, 1, (2,), False)
    for copy in w_fwd:
        copy.wait()
    mlp(0, 1, (3,), False)
    part[0] = (acc[0:128, :] * scale + (feat[...] + scale * vec_ref[4:5, :])).astype(BF).reshape(4, 32, CHANNELS)
    scatters = scatter(0)

    x_prev = ((x + 3) % 4) * 2 + core
    x_next = ((x + 1) % 4) * 2 + core
    x_far = ((x + 2) % 4) * 2 + core

    def piece(owner, dy, low=0, count=24):
        return mf.at[owner, pl.ds(((y + dy) % 4) * 24 + low, count)]

    m_core = []

    def send_piece(dy):
        sent = [
            push(piece(pair, dy), piece(pair, dy), device(1, 0, 0, 0)),
            push(piece(pair, dy), piece(pair, dy), device(3, 0, 0, 0)),
        ]
        m_core.append(push(piece(pair, dy), piece(pair, dy), other))
        return sent

    def relay_piece(dy, sent):
        sent[0].wait()
        far = [push(piece(x_prev, dy, 0, 12), piece(x_prev, dy, 0, 12), device(1, 0, 0, 0))]
        m_core.append(push(piece(x_prev, dy), piece(x_prev, dy), other))
        sent[1].wait()
        far.append(push(piece(x_next, dy, 12, 12), piece(x_next, dy, 12, 12), device(3, 0, 0, 0)))
        m_core.append(push(piece(x_next, dy), piece(x_next, dy), other))
        return far

    def finish_piece(dy, far):
        far[0].wait()
        far[1].wait()
        m_core.append(push(piece(x_far, dy), piece(x_far, dy), other))

    for copy in all_z:
        copy.wait()
    all_y = [push(piece(pair, 0), piece(pair, 0), device(0, dy, 0, 0)) for dy in (1, 3, 2)]
    sent_0 = send_piece(0)
    mlp(1, 2, (0, 1, 2, 3), True)
    for slot in (1, 2):
        part[slot] = (acc[128 * slot - 128:128 * slot, :] * scale).astype(BF).reshape(4, 32, CHANNELS)
        scatters += scatter(slot)
    all_y[0].wait()
    sent_3 = send_piece(3)
    far_0 = relay_piece(0, sent_0)
    t_far0.wait()
    t_far1.wait()
    mlp(3, 1, (0, 1, 2, 3), True)
    part[3] = (acc[0:128, :] * scale).astype(BF).reshape(4, 32, CHANNELS)
    scatters += scatter(3)
    all_y[1].wait()
    sent_1 = send_piece(1)
    all_y[2].wait()
    sent_2 = send_piece(2)
    finish_piece(0, far_0)
    far_3 = relay_piece(3, sent_3)
    for copy in scatters:
        copy.wait()

    for slot in range(4):
        for n in range(3):
            lanes = slice(n * 512, n * 512 + 512)
            value = part[slot, z, :, lanes].astype(F32)
            for peer in range(3):
                value = value + rs_in[peer, slot, :, lanes].astype(F32)
            for q in range(4):
                stage_t[q, (z + OFFSET[slot] + 4) % 4, :, lanes] = value[8 * q:8 * q + 8]
    for q in range(4):
        stage_b[q] = stage_t[q].reshape(32, CHANNELS).astype(BF)
    my_q = ylo * 2 + core
    seq_copies = []
    for dy in range(2):
        for dk in range(2):
            if (dy, dk) != (0, 0):
                q = ((ylo + dy) % 2) * 2 + (core + dk) % 2
                seq_copies.append(push(stage_b.at[q], seq_in.at[my_q], device(0, dy * yflip, 0, dk)))
    seq_in[my_q] = stage_b[my_q]

    for copy in seq_copies:
        copy.wait()
    for n in range(3):
        lanes = slice(n * 512, n * 512 + 512)
        tok[0, :, lanes] = dot(seq_ref[...], seq_in[:, :, lanes].reshape(128, 512)).astype(BF)
    for b in range(19):
        if b % 13 == 12:
            ext[:, b * 128:b * 128 + 128] = jnp.where(
                lax.broadcasted_iota(jnp.int32, (128, 128), 1) == 0, 1.0, 0.0
            )
        else:
            lanes = slice((b % 13) * 128, (b % 13) * 128 + 128)
            ext[:, b * 128:b * 128 + 128] = tok[0, :, lanes].astype(F32)
    far_1 = relay_piece(1, sent_1)
    finish_piece(3, far_3)
    far_2 = relay_piece(2, sent_2)
    finish_piece(1, far_1)
    for copy in m_bias:
        copy.wait()
    for owner in (pair, x_prev, x_next, x_far):
        m_core.append(push(mf.at[owner, 96], mf.at[owner, 96], other))
    finish_piece(2, far_2)
    for copy in m_core:
        copy.wait()

    encoded = tok[0]

    def squares_of(i, total):
        cells = tok[0, :, pl.ds(pl.multiple_of(i * 128, 128), 128)]
        groups = pl.ds(i * 8, 8)

        def other_block(d):
            return ext[:, pl.ds(pl.multiple_of((i + d) * 128, 128), 128)]

        total = total + dot(cells, mf[5, groups, :, 256:384].reshape(128, 128)) * other_block(0)
        for j in (6, 7):
            value = 2.0 * dot(cells, mf[j, groups].reshape(128, 384))
            for t in range(3):
                total = total + value[:, t * 128:t * 128 + 128] * other_block((j - 6) * 3 + t + 1)
        return total

    total = lax.fori_loop(0, BLOCKS, squares_of, jnp.zeros((128, 128), F32))
    for d in range(7):
        j, t = (17 + d) // 3, (17 + d) % 3
        weight = mf[j, 96, :, t * 128:t * 128 + 128].astype(F32)[0:1]
        total = total + (1.0 if d == 0 else 2.0) * weight * ext[:, (12 + d) * 128:(13 + d) * 128]
    squares = jnp.maximum(jnp.sum(total, axis=-1, keepdims=True), 0.0)
    inverse = lax.rsqrt(squares * (1.0 / LANGUAGE_WIDTH) + 1e-06)
    for j in range(6):
        bias = mf[j, 96].astype(F32)[0:1]
        lin[:, j * 384:j * 384 + 384] = inverse * (dot(encoded, mf[j, 0:96].reshape(CHANNELS, 384)) + bias)
    adapter_in = lin[:, 2048:2176].astype(BF)
    for n in range(8):
        lanes = slice(n * 256, n * 256 + 256)
        value = lin[:, lanes] + kvb_ref[0:1, lanes] + dot(adapter_in, up_ref[:, lanes])
        if n < 4:
            for h in range(2):
                head = value[:, h * 128:h * 128 + 128]
                turned = head * cosine + pltpu.roll(head, 64, 1) * sine
                kv_ref[:, n * 256 + h * 128:n * 256 + h * 128 + 128] = turned.astype(BF)
        else:
            kv_ref[:, lanes] = value.astype(BF)

    weighted = (inverse * adapter_grad).astype(BF)
    for n in range(3):
        value = dot_tn(encoded[:, n * 512:n * 512 + 512], weighted)
        ein[n * 32:n * 32 + 32] = value.astype(BF).reshape(32, 16, 128)
    shifted = jnp.sum(weighted.astype(F32), axis=0, keepdims=True)
    ein[96] = jnp.where(lax.broadcasted_iota(jnp.int32, (16, 128), 0) == 0, shifted, 0.0).astype(BF)
    for n in range(16):
        value = dot_tn(adapter_in, grad[:, n * 128:n * 128 + 128])
        value = value[0:64] if n < 8 else value[64:128]
        ein[97 + 4 * n:101 + 4 * n] = (0.5 * value).astype(BF).reshape(4, 16, 128)
    ein[161:176] = jnp.zeros((15, 16, 128), BF)
    sums = []
    for n, (dy, dz) in enumerate(planes):
        target_plane = ((y + dy) % 4) * 4 + (z + dz) % 4
        sums.append(push(ein.at[pl.ds(target_plane * 11, 11)], e_in1.at[n], device(0, dy, dz, 0)))
    for copy in sums:
        copy.wait()
    value = ein[pl.ds(plane * 11, 11)].astype(F32)
    for n in range(15):
        value = value + e_in1[n].astype(F32)
    e_in2[pair] = value.astype(BF)
    sums = []
    for dx in range(4):
        for dk in range(2):
            if (dx, dk) != (0, 0):
                sums.append(push(e_in2.at[pair], e_in2.at[pair], device(dx, 0, 0, dk)))
    for copy in sums:
        copy.wait()
    value = e_in2[0].astype(F32)
    for n in range(1, 8):
        value = value + e_in2[n].astype(F32)
    mine = e_all.at[pl.ds(plane * 11, 11)]
    mine[...] = value.astype(BF)
    sums = [push(mine, mine, device(0, dy, dz, 0)) for dy, dz in planes]
    for copy in sums:
        copy.wait()
    down_ref[...] = dot(pt_ref[...], e_all[0:104].reshape(EXT, 128)) * gain_ref[...]
    for n in range(16):
        lanes = slice((n % 8) * 128, (n % 8) * 128 + 128)
        upg_ref[n // 8, :, lanes] = e_all[97 + 4 * n:101 + 4 * n].reshape(64, 128).astype(F32)


def orders():
    tile = [[0.0] * 128 for _ in range(128)]
    seq = [[0.0] * 128 for _ in range(128)]
    for w in range(4):
        for h in range(8):
            for i in range(4):
                tile[(h % 4) * 32 + (h // 4) * 16 + (i // 2) * 8 + w * 2 + i % 2][w * 32 + h * 4 + i] = 1.0
    for ys in range(2):
        for cs in range(2):
            for zs in range(4):
                for w in range(4):
                    for i in range(2):
                        here = (ys * 2 + cs) * 32 + zs * 8 + w * 2 + i
                        seq[i * 64 + ys * 32 + zs * 8 + cs * 4 + w][here] = 1.0
    return jnp.array(tile, BF), jnp.array(seq, BF)


def local(
    feature_grid, depthwise_kernel, depthwise_bias, layer_norm_gain, layer_norm_shift,
    expansion_weight, expansion_bias, reduction_weight, reduction_bias, layer_branch_scale,
    projector_weight, projector_bias, input_norm_gain, key_value_weight, key_value_bias,
    adapter_down_weight, adapter_up_weight, image_start_positions, key_value_cotangent,
):
    device_block = lax.axis_index("row") * 16 + lax.axis_index("col")
    seq_index = device_block * 2 + jnp.arange(2, dtype=jnp.int32)
    match = (seq_index % IMAGES)[:, None] == jnp.arange(IMAGES, dtype=jnp.int32)[None, :]
    offsets = jnp.sum(jnp.where(match, image_start_positions[None, :], 0), axis=1)
    positions = (offsets + seq_index // IMAGES * 64)[:, None] + jnp.arange(64, dtype=jnp.int32)[None, :]
    freq_steps = jnp.arange(HEAD_DIM // 2, dtype=F32)
    inverse = jnp.exp(freq_steps * (-2.0 * math.log(ROPE_THETA) / HEAD_DIM))
    angle = positions.astype(F32).reshape(128, 1) * inverse
    cosine, sine = jnp.cos(angle), jnp.sin(angle)
    cosine = jnp.concatenate([cosine, cosine], axis=1)
    sine = jnp.concatenate([-sine, sine], axis=1)

    cells = feature_grid.transpose(2, 0, 1, 3).reshape(4, 32, CHANNELS)
    taps = depthwise_kernel.reshape(49, CHANNELS).astype(F32)
    vectors = jnp.stack(
        [depthwise_bias, layer_norm_gain, layer_norm_shift, layer_branch_scale, reduction_bias]
        + [jnp.zeros_like(depthwise_bias)] * 3
    )
    b1 = jnp.broadcast_to(expansion_bias[None, :], (8, 384))
    pt = jnp.concatenate(
        [projector_weight.T, projector_bias[:, None], jnp.zeros((64, 127), BF)], axis=1
    )
    gain = input_norm_gain.astype(F32)[:, None]
    gb = jnp.concatenate([key_value_weight, adapter_down_weight], axis=1).astype(F32) * gain
    gb = jnp.pad(gb.astype(BF), ((0, 0), (0, 896))).reshape(64, 8, 384).transpose(1, 0, 2)
    half = (adapter_up_weight.astype(F32) * 0.5).astype(BF)
    zero = jnp.zeros((64, 1024), BF)
    up = jnp.concatenate(
        [jnp.concatenate([half[0], zero], axis=1), jnp.concatenate([zero, half[1]], axis=1)], axis=0
    )
    tile_order, seq_order = orders()
    vmem = pl.BlockSpec(memory_space=pltpu.VMEM)
    kv, down, upg = pl.pallas_call(
        kernel,
        out_shape=(
            jax.ShapeDtypeStruct((128, 2048), BF),
            jax.ShapeDtypeStruct((64, 128), F32),
            jax.ShapeDtypeStruct((2, 64, 1024), F32),
        ),
        in_specs=[vmem] * 16,
        out_specs=(vmem, vmem, vmem),
        scratch_shapes=[
            pltpu.VMEM((10, 64, CHANNELS), BF),
            pltpu.VMEM((4, 32, CHANNELS), F32),
            pltpu.VMEM((4, 128, CHANNELS), BF),
            pltpu.VMEM((4, CHANNELS, 384), BF),
            pltpu.VMEM((4, 384, CHANNELS), BF),
            pltpu.VMEM((4, 8, 384), F32),
            pltpu.VMEM((128, CHANNELS), F32),
            pltpu.VMEM((256, CHANNELS), F32),
            pltpu.VMEM((4, 4, 32, CHANNELS), BF),
            pltpu.VMEM((3, 4, 32, CHANNELS), BF),
            pltpu.VMEM((4, 4, 8, CHANNELS), F32),
            pltpu.VMEM((4, 32, CHANNELS), BF),
            pltpu.VMEM((4, 32, CHANNELS), BF),
            pltpu.VMEM((8, 64, 2048), BF),
            pltpu.VMEM((5, 12, 2, 16, 384), BF),
            pltpu.VMEM((3, 4, 3, 2, 16, 384), BF),
            pltpu.VMEM((4, 3, 2, 16, 384), BF),
            pltpu.VMEM((3, 3, 2, 16, 384), BF),
            pltpu.VMEM((7, 16, 384), BF),
            pltpu.VMEM((8, 97, 16, 384), BF),
            pltpu.VMEM((128, 19 * 128), F32),
            pltpu.VMEM((128, 2304), F32),
            pltpu.VMEM((128, 2048), BF),
            pltpu.VMEM((176, 16, 128), BF),
            pltpu.VMEM((15, 11, 16, 128), BF),
            pltpu.VMEM((8, 11, 16, 128), BF),
            pltpu.VMEM((176, 16, 128), BF),
            pltpu.SemaphoreType.DMA((COPIES,)),
            pltpu.SemaphoreType.DMA((COPIES,)),
            pltpu.SemaphoreType.DMA((6,)),
        ],
        compiler_params=pltpu.CompilerParams(
            collective_id=0, has_side_effects=True, vmem_limit_bytes=62 << 20
        ),
        cost_estimate=pl.CostEstimate(flops=8_000_000_000, bytes_accessed=30_000_000, transcendentals=0),
    )(
        cells, taps, vectors, expansion_weight, reduction_weight, b1, pt, gb, gain,
        up, cosine, sine, key_value_cotangent.reshape(128, 2048), key_value_bias[None, :], tile_order, seq_order,
    )
    return kv.reshape(2, 64, 2048), down, upg


def solution(mesh):
    in_specs = (
        P("row", None, "col", None), P(), P(), P(), P(),
        P(None, "col"), P("col"), P("col", None), P(), P(),
        P(None, ("row", "col")), P(("row", "col")), P(("row", "col")), P(("row", "col"), None), P(),
        P(("row", "col"), None), P(), P(), P(("row", "col"), None, None),
    )
    out_specs = (P(("row", "col"), None, None), P(("row", "col"), None), P())
    return jax.shard_map(local, mesh=mesh, in_specs=in_specs, out_specs=out_specs, check_vma=False)
```

```python
import functools
import math

import jax
import jax.numpy as jnp
import numpy as np
from jax import lax
from jax.experimental import pallas as pl
from jax.experimental.pallas import tpu as pltpu
from jax.sharding import PartitionSpec as P

LANGUAGE_WIDTH = 8192
HEAD_DIM = 128
IMAGES = 4
CHANNELS = 1536
BLOCKS = 12
EXT = 1664
ROPE_THETA = 1000000.0
MESH = pl.DeviceIdType.MESH
BF = jnp.bfloat16
F32 = jnp.float32
COPIES = 200
SLOT_OF = {0: 0, 3: 1, 1: 2, 2: 3}
OFFSET = (0, -1, 1, 2)


def dot(a, b):
    return jnp.dot(a, b, preferred_element_type=F32)


def dot_tn(a, b):
    return lax.dot_general(a, b, (((0,), (0,)), ((), ())), preferred_element_type=F32)


def dot_nt(a, b):
    return lax.dot_general(a, b, (((1,), (1,)), ((), ())), preferred_element_type=F32)


def kernel(
    x_ref, depth_ref, dbias_ref, lgain_ref, lshift_ref, w1_ref, w2_ref, b1_ref, rbias_ref, scale_ref,
    proj_ref, pbias_ref, ngain_ref, kvw_ref, kvb_ref, downw_ref, upw_ref, start_ref, cot_ref,
    freq_ref, perm_ref, seq_ref,
    kv_ref, down_ref, upg_ref,
    pad, conv, tok, wa, wb, ba, feat, acc, part, rs_in, stage_t, stage_b, seq_in,
    pb, quad, red_z, red_mid, red_y, red_bias, mf, ext, lin, grad,
    ein, e_core, e_mid, e_in1, e_in2, e_all, pt_ref, gb_ref, up_ref, taps_ref, cos_ref, sin_ref,
    send, recv, lsem,
):
    row = lax.axis_index("row")
    col = lax.axis_index("col")
    x = row // 2
    y = (row % 2) * 2 + col // 8
    z = (col % 8) // 2
    core = col % 2
    ylo = y % 2
    plane = y * 4 + z
    pair = x * 2 + core

    def device(dx, dy, dz, dk):
        xx, yy, zz, kk = (x + dx + 4) % 4, (y + dy + 4) % 4, (z + dz + 4) % 4, (core + dk) % 2
        return (xx * 2 + yy // 2, (yy % 2) * 8 + zz * 2 + kk)

    ids = [0]

    def push(src, dst, target):
        n = ids[0]
        ids[0] += 1
        copy = pltpu.make_async_remote_copy(
            src_ref=src, dst_ref=dst, send_sem=send.at[n], recv_sem=recv.at[n],
            device_id=target, device_id_type=MESH,
        )
        copy.start()
        return copy

    planes = [(dy, dz) for dy in range(4) for dz in range(4) if (dy, dz) != (0, 0)]
    up_dev = ((row + 7) % 8, col)
    dn_dev = ((row + 1) % 8, col)
    lt_dev = (row, (col + 15) % 16)
    rt_dev = (row, (col + 1) % 16)
    other = device(0, 0, 0, 1)
    yflip = 1 - 2 * ylo

    partners = [up_dev, dn_dev, lt_dev, rt_dev]
    for dx in range(4):
        for dk in range(2):
            if (dx, dk) != (0, 0):
                partners.append(device(dx, 0, 0, dk))
    for dy, dz in planes:
        partners.append(device(0, dy, dz, 0))
    partners.append(device(0, yflip, 0, 1))
    barrier = pltpu.get_barrier_semaphore()
    for partner in partners:
        pl.semaphore_signal(barrier, inc=1, device_id=partner, device_id_type=MESH)
    diagonal = lax.broadcasted_iota(jnp.int32, (64, 64), 0) == lax.broadcasted_iota(jnp.int32, (64, 64), 1)
    gain = jnp.sum(jnp.where(diagonal, ngain_ref[...].astype(F32), 0.0), axis=1, keepdims=True)
    bias = jnp.sum(jnp.where(diagonal, pbias_ref[...].astype(F32), 0.0), axis=1, keepdims=True)
    eye = jnp.where(diagonal, 1.0, 0.0).astype(BF)
    for n in range(3):
        pt_ref[:, n * 512:n * 512 + 512] = dot_nt(eye, proj_ref[n * 512:n * 512 + 512, :]).astype(BF)
    first_lane = lax.broadcasted_iota(jnp.int32, (64, 128), 1) == 0
    pt_ref[:, CHANNELS:EXT] = jnp.where(first_lane, bias, 0.0).astype(BF)
    for j in range(5):
        gb_ref[j] = (kvw_ref[:, j * 384:j * 384 + 384].astype(F32) * gain).astype(BF)
    gb_ref[5, :, 0:128] = (kvw_ref[:, 1920:2048].astype(F32) * gain).astype(BF)
    gb_ref[5, :, 128:256] = (downw_ref[...].astype(F32) * gain).astype(BF)
    gb_ref[5, :, 256:384] = jnp.zeros((64, 128), BF)
    gb_ref[6:8] = jnp.zeros((2, 64, 384), BF)
    copies0 = [
        pltpu.make_async_copy(x_ref, pad.at[3:7, 16:48], lsem.at[0]),
        pltpu.make_async_copy(w1_ref, wa.at[0], lsem.at[1]),
        pltpu.make_async_copy(w2_ref, wb.at[0], lsem.at[2]),
        pltpu.make_async_copy(b1_ref, ba.at[0], lsem.at[3]),
        pltpu.make_async_copy(pt_ref, pb.at[0, :, 0:EXT], lsem.at[4]),
        pltpu.make_async_copy(gb_ref.at[pair], pb.at[0, :, EXT:2048], lsem.at[5]),
    ]
    for copy in copies0:
        copy.start()
    pl.semaphore_wait(barrier, len(partners))

    h_up = push(x_ref.at[:, 0:16], pad.at[3:7, 48:64], up_dev)
    h_dn = push(x_ref.at[:, 16:32], pad.at[3:7, 0:16], dn_dev)
    h_rt = push(x_ref.at[1:4], pad.at[0:3, 16:48], rt_dev)
    h_lt = push(x_ref.at[0:3], pad.at[7:10, 16:48], lt_dev)
    gb_copies = []
    pt_copies = []
    for dx in (1, 3, 2):
        pt_copies.append(push(pt_ref, pb.at[2 * dx, :, 0:EXT], device(dx, 0, 0, 0)))
    for dx in range(4):
        for dk in range(2):
            if (dx, dk) != (0, 0):
                target_pair = ((x + dx) % 4) * 2 + (core + dk) % 2
                gb_copies.append(
                    push(gb_ref.at[target_pair], pb.at[2 * dx + dk, :, EXT:2048], device(dx, 0, 0, dk))
                )
    fwd_copies = [push(pt_ref, pb.at[1, :, 0:EXT], other)]
    w_core = [
        push(w1_ref, wa.at[1], other), push(w2_ref, wb.at[1], other), push(b1_ref, ba.at[1], other),
    ]
    w_y = [
        push(w1_ref, wa.at[2], device(0, 1, 0, 0)),
        push(w2_ref, wb.at[2], device(0, 3, 0, 0)),
        push(b1_ref, ba.at[2], device(0, 1, 0, 0)),
    ]

    token = lax.broadcasted_iota(jnp.int32, (128, 128), 0)
    later = token >= 64
    start = jnp.where(later, start_ref[core * 2 + 1], start_ref[core * 2])
    position = start + (row * 8 + col // 2) * 64 + jnp.where(later, token - 64, token)
    angle = position.astype(F32) * freq_ref[...]
    cos_ref[...] = jnp.cos(angle)
    upper = lax.broadcasted_iota(jnp.int32, (128, 128), 1) >= 64
    sin_ref[...] = jnp.where(upper, 1.0, -1.0) * jnp.sin(angle)
    up_ref[...] = jnp.zeros((128, 2048), BF)
    up_ref[0:64, 0:1024] = (upw_ref[0].astype(F32) * 0.5).astype(BF)
    up_ref[64:128, 1024:2048] = (upw_ref[1].astype(F32) * 0.5).astype(BF)
    for a in range(7):
        taps_ref[a, 0:7, :] = depth_ref[a].astype(F32)
    cosine = cos_ref[...]
    sine = sin_ref[...]
    for head in range(8):
        lanes = slice(head * 128, head * 128 + 128)
        value = cot_ref[:, lanes].astype(F32)
        grad[:, lanes] = (value * cosine - pltpu.roll(value, 64, 1) * sine).astype(BF)
    grad[:, 1024:2048] = cot_ref[:, 1024:2048]
    adapter_grad = dot_nt(grad[...], up_ref[...]).astype(BF).astype(F32)
    for copy in copies0:
        copy.wait()
    for n in range(3):
        lanes = slice(n * 512, n * 512 + 512)
        feat[:, lanes] = dot(perm_ref[...], x_ref[:, :, lanes].reshape(128, 512))

    h_up.wait()
    h_dn.wait()

    @pl.when(row == 0)
    def _():
        pad[3:7, 0:16] = jnp.zeros((4, 16, CHANNELS), BF)

    @pl.when(row == 7)
    def _():
        pad[3:7, 48:64] = jnp.zeros((4, 16, CHANNELS), BF)

    corners = [
        push(pad.at[4:7, 0:16], pad.at[0:3, 0:16], rt_dev),
        push(pad.at[4:7, 48:64], pad.at[0:3, 48:64], rt_dev),
        push(pad.at[3:6, 0:16], pad.at[7:10, 0:16], lt_dev),
        push(pad.at[3:6, 48:64], pad.at[7:10, 48:64], lt_dev),
    ]

    for n, dx in enumerate((1, 3, 2)):
        pt_copies[n].wait()
        fwd_copies.append(push(pb.at[2 * dx, :, 0:EXT], pb.at[2 * dx + 1, :, 0:EXT], other))
    for copy in gb_copies:
        copy.wait()
    for copy in fwd_copies:
        copy.wait()

    def products(i, carry):
        left = pb[:, :, pl.ds(pl.multiple_of(i * 128, 128), 128)].reshape(512, 128)
        for t in range(3):
            block = pair * 3 + t
            shift = i + block - 17
            around = jnp.where(shift >= 13, shift - 13, shift)
            start = jnp.where(block < 17, 13 + t, around) * 128
            right = pb[:, :, pl.ds(pl.multiple_of(start, 128), 128)].reshape(512, 128)
            value = dot_tn(left, right).astype(BF).reshape(4, 2, 16, 128)
            for r in range(4):
                p = i * 4 + r
                quad[p // 12, p % 12, :, :, t * 128:t * 128 + 128] = value[r]
        return carry

    lax.fori_loop(0, 13, products, 0)
    red_copies = []
    for n, dz in enumerate((1, 3, 2)):
        target = device(0, 0, dz, 0)
        red_copies.append(push(quad.at[0:4, pl.ds(((z + dz) % 4) * 3, 3)], red_z.at[n], target))
        red_copies.append(push(quad.at[4, 0, 0], red_bias.at[n], target))

    h_rt.wait()
    h_lt.wait()
    for copy in corners:
        copy.wait()

    @pl.when(col == 0)
    def _():
        pad[0:3] = jnp.zeros((3, 64, CHANNELS), BF)

    @pl.when(col == 15)
    def _():
        pad[7:10] = jnp.zeros((3, 64, CHANNELS), BF)

    def conv_lanes(n, carry):
        lanes = pl.ds(pl.multiple_of(n * 128, 128), 128)
        sums = [jnp.zeros((32, 128), F32) + dbias_ref[0:1, lanes] for _ in range(4)]
        for wp in range(10):
            full = pad[wp, :, lanes].astype(F32)
            moved = pltpu.roll(full, 60, 0)
            for a in range(7):
                start = 4 * (a + 1)
                window = full[start:start + 32] if a % 2 else moved[start - 4:start + 28]
                for w in range(max(0, wp - 6), min(3, wp) + 1):
                    sums[w] = sums[w] + window * taps_ref[a, wp - w:wp - w + 1, lanes]
        for w in range(4):
            conv[w, :, lanes] = sums[w]
        return carry

    lax.fori_loop(0, BLOCKS, conv_lanes, 0)

    def norm_rows(n, carry):
        w = n // 2
        rows = pl.ds(pl.multiple_of((n % 2) * 16, 16), 16)
        value = conv[w, rows, :]
        center = jnp.sum(value, axis=-1, keepdims=True) * (1.0 / CHANNELS)
        centered = value - center
        variance = jnp.sum(centered * centered, axis=-1, keepdims=True) * (1.0 / CHANNELS)
        value = centered * lax.rsqrt(variance + 1e-06) * lgain_ref[...] + lshift_ref[...]
        part[0, w, rows, :] = value.astype(BF)
        return carry

    lax.fori_loop(0, 8, norm_rows, 0)
    for n in range(3):
        lanes = slice(n * 512, n * 512 + 512)
        tok[0, :, lanes] = dot(perm_ref[...], part[0, :, :, lanes].reshape(128, 512)).astype(BF)
    t_next = push(tok.at[0], tok.at[1], device(0, 0, 1, 0))
    t_prev = push(tok.at[0], tok.at[2], device(0, 0, 3, 0))

    def mlp(slot, count, weights, first):
        rows = 128 * count
        tokens = tok[slot:slot + count].reshape(rows, CHANNELS)
        for index, s in enumerate(weights):
            pre = dot(tokens, wa[s]) + ba[s]
            hidden = (0.5 * pre * (1.0 + lax.erf(pre * (0.5 ** 0.5)))).astype(BF)
            for n in range(3):
                lanes = slice(n * 512, n * 512 + 512)
                term = dot(hidden, wb[s, :, lanes])
                if first and index == 0:
                    acc[0:rows, lanes] = term
                else:
                    acc[0:rows, lanes] += term

    def scatter(slot):
        sent = []
        for tau in (1, 3, 2):
            into = SLOT_OF[(OFFSET[slot] - tau) % 4]
            peer = SLOT_OF[(-tau) % 4] - 1
            sent.append(
                push(part.at[slot, (z + tau) % 4], rs_in.at[peer, into], device(0, 0, tau, 0))
            )
        return sent

    scale = scale_ref[...]
    mlp(0, 1, (0,), True)
    for copy in w_core:
        copy.wait()
    mlp(0, 1, (1,), False)

    for copy in red_copies:
        copy.wait()

    def sum_z(n, carry):
        h, p = n // 3, n % 3
        total = quad[h, z * 3 + p].astype(F32)
        for m in range(3):
            total = total + red_z[m, h, p].astype(F32)
        red_mid[h, p] = total.astype(BF)
        return carry

    lax.fori_loop(0, 12, sum_z, 0)
    total = quad[4, 0, 0].astype(F32)
    for m in range(3):
        total = total + red_bias[m].astype(F32)
    red_bias[6] = total.astype(BF)
    red_copies = []
    for n, dy in enumerate((1, 3, 2)):
        target = device(0, dy, 0, 0)
        red_copies.append(push(red_mid.at[(y + dy) % 4], red_y.at[n], target))
        red_copies.append(push(red_bias.at[6], red_bias.at[3 + n], target))
    t_next.wait()
    t_far0 = push(tok.at[1, 0:64], tok.at[3, 0:64], device(0, 0, 1, 0))
    t_prev.wait()
    t_far1 = push(tok.at[2, 64:128], tok.at[3, 64:128], device(0, 0, 3, 0))
    for copy in red_copies:
        copy.wait()

    def sum_y(p, carry):
        total = red_mid[y, p].astype(F32)
        for m in range(3):
            total = total + red_y[m, p].astype(F32)
        mf[pair, pl.ds(plane * 6 + p * 2, 2)] = total.astype(BF)
        return carry

    lax.fori_loop(0, 3, sum_y, 0)
    total = red_bias[6].astype(F32)
    for m in range(3):
        total = total + red_bias[3 + m].astype(F32)
    mf[pair, 96] = total.astype(BF)
    block = mf.at[pair, pl.ds(plane * 6, 6)]
    all_z = [push(block, block, device(0, 0, dz, 0)) for dz in (1, 3, 2)]
    m_bias = [push(mf.at[pair, 96], mf.at[pair, 96], device(dx, 0, 0, 0)) for dx in (1, 3, 2)]
    for copy in w_y:
        copy.wait()
    w_fwd = [
        push(wa.at[2], wa.at[3], other), push(wb.at[2], wb.at[3], other), push(ba.at[2], ba.at[3], other),
    ]
    mlp(0, 1, (2,), False)
    for copy in w_fwd:
        copy.wait()
    mlp(0, 1, (3,), False)
    part[0] = (acc[0:128, :] * scale + (feat[...] + scale * rbias_ref[...])).astype(BF).reshape(4, 32, CHANNELS)
    scatters = scatter(0)

    x_prev = ((x + 3) % 4) * 2 + core
    x_next = ((x + 1) % 4) * 2 + core
    x_far = ((x + 2) % 4) * 2 + core

    def piece(owner, dy, low=0, count=24):
        return mf.at[owner, pl.ds(((y + dy) % 4) * 24 + low, count)]

    m_core = []

    def send_piece(dy):
        sent = [
            push(piece(pair, dy), piece(pair, dy), device(1, 0, 0, 0)),
            push(piece(pair, dy), piece(pair, dy), device(3, 0, 0, 0)),
        ]
        m_core.append(push(piece(pair, dy), piece(pair, dy), other))
        return sent

    def relay_piece(dy, sent):
        sent[0].wait()
        far = [push(piece(x_prev, dy, 0, 12), piece(x_prev, dy, 0, 12), device(1, 0, 0, 0))]
        m_core.append(push(piece(x_prev, dy), piece(x_prev, dy), other))
        sent[1].wait()
        far.append(push(piece(x_next, dy, 12, 12), piece(x_next, dy, 12, 12), device(3, 0, 0, 0)))
        m_core.append(push(piece(x_next, dy), piece(x_next, dy), other))
        return far

    def finish_piece(dy, far):
        far[0].wait()
        far[1].wait()
        m_core.append(push(piece(x_far, dy), piece(x_far, dy), other))

    for copy in all_z:
        copy.wait()
    all_y = [push(piece(pair, 0), piece(pair, 0), device(0, dy, 0, 0)) for dy in (1, 3, 2)]
    sent_0 = send_piece(0)
    mlp(1, 2, (0, 1, 2, 3), True)
    for slot in (1, 2):
        part[slot] = (acc[128 * slot - 128:128 * slot, :] * scale).astype(BF).reshape(4, 32, CHANNELS)
        scatters += scatter(slot)
    all_y[0].wait()
    sent_3 = send_piece(3)
    far_0 = relay_piece(0, sent_0)
    t_far0.wait()
    t_far1.wait()
    mlp(3, 1, (0, 1, 2, 3), True)
    part[3] = (acc[0:128, :] * scale).astype(BF).reshape(4, 32, CHANNELS)
    scatters += scatter(3)
    all_y[1].wait()
    sent_1 = send_piece(1)
    all_y[2].wait()
    sent_2 = send_piece(2)
    finish_piece(0, far_0)
    far_3 = relay_piece(3, sent_3)
    for copy in scatters:
        copy.wait()

    for slot in range(4):
        for n in range(3):
            lanes = slice(n * 512, n * 512 + 512)
            value = part[slot, z, :, lanes].astype(F32)
            for peer in range(3):
                value = value + rs_in[peer, slot, :, lanes].astype(F32)
            for q in range(4):
                stage_t[q, (z + OFFSET[slot] + 4) % 4, :, lanes] = value[8 * q:8 * q + 8]
    for q in range(4):
        stage_b[q] = stage_t[q].reshape(32, CHANNELS).astype(BF)
    my_q = ylo * 2 + core
    seq_copies = []
    for dy in range(2):
        for dk in range(2):
            if (dy, dk) != (0, 0):
                q = ((ylo + dy) % 2) * 2 + (core + dk) % 2
                seq_copies.append(push(stage_b.at[q], seq_in.at[my_q], device(0, dy * yflip, 0, dk)))
    seq_in[my_q] = stage_b[my_q]

    for copy in seq_copies:
        copy.wait()
    for n in range(3):
        lanes = slice(n * 512, n * 512 + 512)
        tok[0, :, lanes] = dot(seq_ref[...], seq_in[:, :, lanes].reshape(128, 512)).astype(BF)
    for b in range(19):
        if b % 13 == 12:
            ext[:, b * 128:b * 128 + 128] = jnp.where(
                lax.broadcasted_iota(jnp.int32, (128, 128), 1) == 0, 1.0, 0.0
            )
        else:
            lanes = slice((b % 13) * 128, (b % 13) * 128 + 128)
            ext[:, b * 128:b * 128 + 128] = tok[0, :, lanes].astype(F32)
    far_1 = relay_piece(1, sent_1)
    finish_piece(3, far_3)
    far_2 = relay_piece(2, sent_2)
    finish_piece(1, far_1)
    for copy in m_bias:
        copy.wait()
    for owner in (pair, x_prev, x_next, x_far):
        m_core.append(push(mf.at[owner, 96], mf.at[owner, 96], other))
    finish_piece(2, far_2)
    for copy in m_core:
        copy.wait()

    encoded = tok[0]

    def squares_of(i, total):
        cells = tok[0, :, pl.ds(pl.multiple_of(i * 128, 128), 128)]
        groups = pl.ds(i * 8, 8)

        def other_block(d):
            return ext[:, pl.ds(pl.multiple_of((i + d) * 128, 128), 128)]

        total = total + dot(cells, mf[5, groups, :, 256:384].reshape(128, 128)) * other_block(0)
        for j in (6, 7):
            value = 2.0 * dot(cells, mf[j, groups].reshape(128, 384))
            for t in range(3):
                total = total + value[:, t * 128:t * 128 + 128] * other_block((j - 6) * 3 + t + 1)
        return total

    total = lax.fori_loop(0, BLOCKS, squares_of, jnp.zeros((128, 128), F32))
    for d in range(7):
        j, t = (17 + d) // 3, (17 + d) % 3
        weight = mf[j, 96, :, t * 128:t * 128 + 128].astype(F32)[0:1]
        total = total + (1.0 if d == 0 else 2.0) * weight * ext[:, (12 + d) * 128:(13 + d) * 128]
    squares = jnp.maximum(jnp.sum(total, axis=-1, keepdims=True), 0.0)
    inverse = lax.rsqrt(squares * (1.0 / LANGUAGE_WIDTH) + 1e-06)
    for j in range(6):
        offset = mf[j, 96].astype(F32)[0:1]
        lin[:, j * 384:j * 384 + 384] = inverse * (dot(encoded, mf[j, 0:96].reshape(CHANNELS, 384)) + offset)
    adapter_in = lin[:, 2048:2176].astype(BF)
    for n in range(8):
        lanes = slice(n * 256, n * 256 + 256)
        value = lin[:, lanes] + kvb_ref[0:1, lanes] + dot(adapter_in, up_ref[:, lanes])
        if n < 4:
            for h in range(2):
                head = value[:, h * 128:h * 128 + 128]
                turned = head * cosine + pltpu.roll(head, 64, 1) * sine
                kv_ref[:, n * 256 + h * 128:n * 256 + h * 128 + 128] = turned.astype(BF)
        else:
            kv_ref[:, lanes] = value.astype(BF)

    weighted = (inverse * adapter_grad).astype(BF)

    def place(group, value):
        ein[group // 80, group % 80 // 5, group % 5] = value

    for n in range(3):
        value = dot_tn(encoded[:, n * 512:n * 512 + 512], weighted).astype(BF).reshape(32, 16, 128)
        for g in range(32):
            place(n * 32 + g, value[g])
    for n in range(16):
        value = dot_tn(adapter_in, grad[:, n * 128:n * 128 + 128])
        value = value[0:64] if n < 8 else value[64:128]
        value = (0.5 * value).astype(BF).reshape(4, 16, 128)
        for g in range(4):
            place(96 + 4 * n + g, value[g])
    shifted = jnp.sum(weighted.astype(F32), axis=0, keepdims=True)
    shifted = jnp.where(lax.broadcasted_iota(jnp.int32, (16, 128), 0) == 0, shifted, 0.0).astype(BF)
    for half in range(2):
        for p in range(16):
            ein[half, p, 5] = shifted
    push(ein.at[1 - core], e_core, other).wait()

    def sum_cores(p, carry):
        e_mid[p] = (ein[core, p].astype(F32) + e_core[p].astype(F32)).astype(BF)
        return carry

    lax.fori_loop(0, 16, sum_cores, 0)
    sums = []
    for n, (dy, dz) in enumerate(planes):
        target_plane = ((y + dy) % 4) * 4 + (z + dz) % 4
        sums.append(push(e_mid.at[target_plane], e_in1.at[n], device(0, dy, dz, 0)))
    for copy in sums:
        copy.wait()
    value = e_mid[plane].astype(F32)
    for n in range(15):
        value = value + e_in1[n].astype(F32)
    e_in2[x] = value.astype(BF)
    sums = [push(e_in2.at[x], e_in2.at[x], device(dx, 0, 0, 0)) for dx in (1, 3, 2)]
    for copy in sums:
        copy.wait()
    value = e_in2[0].astype(F32)
    for n in range(1, 4):
        value = value + e_in2[n].astype(F32)
    value = value.astype(BF)
    mine = e_all.at[pl.ds(core * 80 + plane * 5, 5)]
    mine[...] = value[0:5]
    sums = [push(mine, mine, device(0, dy, dz, 0)) for dy, dz in planes]
    for copy in sums:
        copy.wait()
    mine = e_all.at[pl.ds(core * 80, 80)]
    push(mine, mine, other).wait()
    total_shift = value[5].astype(F32)[0:1]
    down = dot(pt_ref[:, 0:CHANNELS], e_all[0:96].reshape(CHANNELS, 128))
    down_ref[...] = (down + bias * total_shift) * gain
    for n in range(16):
        lanes = slice((n % 8) * 128, (n % 8) * 128 + 128)
        upg_ref[n // 8, :, lanes] = e_all[96 + 4 * n:100 + 4 * n].reshape(64, 128).astype(F32)


def orders():
    tile = [[0.0] * 128 for _ in range(128)]
    seq = [[0.0] * 128 for _ in range(128)]
    for w in range(4):
        for h in range(8):
            for i in range(4):
                tile[(h % 4) * 32 + (h // 4) * 16 + (i // 2) * 8 + w * 2 + i % 2][w * 32 + h * 4 + i] = 1.0
    for ys in range(2):
        for cs in range(2):
            for zs in range(4):
                for w in range(4):
                    for i in range(2):
                        here = (ys * 2 + cs) * 32 + zs * 8 + w * 2 + i
                        seq[i * 64 + ys * 32 + zs * 8 + cs * 4 + w][here] = 1.0
    return jnp.array(tile, BF), jnp.array(seq, BF)


def local(
    feature_grid, depthwise_kernel, depthwise_bias, layer_norm_gain, layer_norm_shift,
    expansion_weight, expansion_bias, reduction_weight, reduction_bias, layer_branch_scale,
    projector_weight, projector_bias, input_norm_gain, key_value_weight, key_value_bias,
    adapter_down_weight, adapter_up_weight, image_start_positions, key_value_cotangent,
):
    cells = feature_grid.transpose(2, 0, 1, 3).reshape(4, 32, CHANNELS)
    freq = np.exp(np.arange(HEAD_DIM // 2, dtype=np.float32) * np.float32(-2.0 * math.log(ROPE_THETA) / HEAD_DIM))
    freq = jnp.array(np.concatenate([freq, freq])[None, :], F32)
    tile_order, seq_order = orders()
    vmem = pl.BlockSpec(memory_space=pltpu.VMEM)
    kv, down, upg = pl.pallas_call(
        kernel,
        out_shape=(
            jax.ShapeDtypeStruct((128, 2048), BF),
            jax.ShapeDtypeStruct((64, 128), F32),
            jax.ShapeDtypeStruct((2, 64, 1024), F32),
        ),
        in_specs=[vmem] * 17 + [pl.BlockSpec(memory_space=pltpu.SMEM)] + [vmem] * 4,
        out_specs=(vmem, vmem, vmem),
        scratch_shapes=[
            pltpu.VMEM((10, 64, CHANNELS), BF),
            pltpu.VMEM((4, 32, CHANNELS), F32),
            pltpu.VMEM((4, 128, CHANNELS), BF),
            pltpu.VMEM((4, CHANNELS, 384), BF),
            pltpu.VMEM((4, 384, CHANNELS), BF),
            pltpu.VMEM((4, 1, 384), F32),
            pltpu.VMEM((128, CHANNELS), F32),
            pltpu.VMEM((256, CHANNELS), F32),
            pltpu.VMEM((4, 4, 32, CHANNELS), BF),
            pltpu.VMEM((3, 4, 32, CHANNELS), BF),
            pltpu.VMEM((4, 4, 8, CHANNELS), F32),
            pltpu.VMEM((4, 32, CHANNELS), BF),
            pltpu.VMEM((4, 32, CHANNELS), BF),
            pltpu.VMEM((8, 64, 2048), BF),
            pltpu.VMEM((5, 12, 2, 16, 384), BF),
            pltpu.VMEM((3, 4, 3, 2, 16, 384), BF),
            pltpu.VMEM((4, 3, 2, 16, 384), BF),
            pltpu.VMEM((3, 3, 2, 16, 384), BF),
            pltpu.VMEM((7, 16, 384), BF),
            pltpu.VMEM((8, 97, 16, 384), BF),
            pltpu.VMEM((128, 19 * 128), F32),
            pltpu.VMEM((128, 2304), F32),
            pltpu.VMEM((128, 2048), BF),
            pltpu.VMEM((2, 16, 6, 16, 128), BF),
            pltpu.VMEM((16, 6, 16, 128), BF),
            pltpu.VMEM((16, 6, 16, 128), BF),
            pltpu.VMEM((15, 6, 16, 128), BF),
            pltpu.VMEM((4, 6, 16, 128), BF),
            pltpu.VMEM((160, 16, 128), BF),
            pltpu.VMEM((64, EXT), BF),
            pltpu.VMEM((8, 64, 384), BF),
            pltpu.VMEM((128, 2048), BF),
            pltpu.VMEM((7, 8, CHANNELS), F32),
            pltpu.VMEM((128, 128), F32),
            pltpu.VMEM((128, 128), F32),
            pltpu.SemaphoreType.DMA((COPIES,)),
            pltpu.SemaphoreType.DMA((COPIES,)),
            pltpu.SemaphoreType.DMA((6,)),
        ],
        compiler_params=pltpu.CompilerParams(
            collective_id=0, has_side_effects=True, vmem_limit_bytes=62 << 20
        ),
        cost_estimate=pl.CostEstimate(flops=8_000_000_000, bytes_accessed=30_000_000, transcendentals=0),
    )(
        cells, depthwise_kernel, depthwise_bias[None, :], layer_norm_gain[None, :], layer_norm_shift[None, :],
        expansion_weight, reduction_weight, expansion_bias[None, :], reduction_bias[None, :],
        layer_branch_scale[None, :], projector_weight, projector_bias[None, :], input_norm_gain[None, :],
        key_value_weight, key_value_bias[None, :], adapter_down_weight, adapter_up_weight,
        image_start_positions, key_value_cotangent.reshape(128, 2048), freq, tile_order, seq_order,
    )
    return kv.reshape(2, 64, 2048), down, upg


def solution(mesh):
    in_specs = (
        P("row", None, "col", None), P(), P(), P(), P(),
        P(None, "col"), P("col"), P("col", None), P(), P(),
        P(None, ("row", "col")), P(("row", "col")), P(("row", "col")), P(("row", "col"), None), P(),
        P(("row", "col"), None), P(), P(), P(("row", "col"), None, None),
    )
    out_specs = (P(("row", "col"), None, None), P(("row", "col"), None), P())
    return jax.shard_map(local, mesh=mesh, in_specs=in_specs, out_specs=out_specs, check_vma=False)
```

```python
import functools
import math

import jax
import jax.numpy as jnp
import numpy as np
from jax import lax
from jax.experimental import pallas as pl
from jax.experimental.pallas import tpu as pltpu
from jax.sharding import PartitionSpec as P

LANGUAGE_WIDTH = 8192
HEAD_DIM = 128
IMAGES = 4
CHANNELS = 1536
BLOCKS = 12
EXT = 1664
ROPE_THETA = 1000000.0
MESH = pl.DeviceIdType.MESH
BF = jnp.bfloat16
F32 = jnp.float32
COPIES = 240
SLOT_OF = {0: 0, 3: 1, 1: 2, 2: 3}
OFFSET = (0, -1, 1, 2)


def dot(a, b):
    return jnp.dot(a, b, preferred_element_type=F32)


def dot_tn(a, b):
    return lax.dot_general(a, b, (((0,), (0,)), ((), ())), preferred_element_type=F32)


def dot_nt(a, b):
    return lax.dot_general(a, b, (((1,), (1,)), ((), ())), preferred_element_type=F32)


def kernel(
    x_ref, depth_ref, dbias_ref, lgain_ref, lshift_ref, w1_ref, w2_ref, b1_ref, rbias_ref, scale_ref,
    proj_ref, pbias_ref, ngain_ref, kvw_ref, kvb_ref, downw_ref, upw_ref, start_ref, cot_ref,
    freq_ref, perm_ref, seq_ref,
    kv_ref, down_ref, upg_ref,
    pad, conv, tok, wa, wb, ba, feat, acc, part, rs_in, stage_t, stage_b, seq_in,
    pb, quad_a, red_z_a, red_mid_a, red_y_a, red_bias_a, mf_a,
    quad_b, red_z_b, red_mid_b, red_y_b, red_bias_b, mf_b, ext, grad,
    ein, e_core, e_mid, e_in1, e_in2, e_all, pt_ref, gb_ref, up_ref, taps_ref, cos_ref, sin_ref, own_b1,
    send, recv, lsem,
):
    row = lax.axis_index("row")
    col = lax.axis_index("col")
    x = row // 2
    y = (row % 2) * 2 + col // 8
    z = (col % 8) // 2
    core = col % 2
    ylo = y % 2
    plane = y * 4 + z
    pair = x * 2 + core

    def device(dx, dy, dz, dk):
        xx, yy, zz, kk = (x + dx + 4) % 4, (y + dy + 4) % 4, (z + dz + 4) % 4, (core + dk) % 2
        return (xx * 2 + yy // 2, (yy % 2) * 8 + zz * 2 + kk)

    ids = [0]

    def push(src, dst, target):
        n = ids[0]
        ids[0] += 1
        copy = pltpu.make_async_remote_copy(
            src_ref=src, dst_ref=dst, send_sem=send.at[n], recv_sem=recv.at[n],
            device_id=target, device_id_type=MESH,
        )
        copy.start()
        return copy

    planes = [(dy, dz) for dy in range(4) for dz in range(4) if (dy, dz) != (0, 0)]
    up_dev = ((row + 7) % 8, col)
    dn_dev = ((row + 1) % 8, col)
    lt_dev = (row, (col + 15) % 16)
    rt_dev = (row, (col + 1) % 16)
    other = device(0, 0, 0, 1)
    yflip = 1 - 2 * ylo

    partners = [up_dev, dn_dev, lt_dev, rt_dev]
    for dx in range(4):
        for dk in range(2):
            if (dx, dk) != (0, 0):
                partners.append(device(dx, 0, 0, dk))
    for dy, dz in planes:
        partners.append(device(0, dy, dz, 0))
    partners.append(device(0, yflip, 0, 1))
    barrier = pltpu.get_barrier_semaphore()
    for partner in partners:
        pl.semaphore_signal(barrier, inc=1, device_id=partner, device_id_type=MESH)
    diagonal = lax.broadcasted_iota(jnp.int32, (64, 64), 0) == lax.broadcasted_iota(jnp.int32, (64, 64), 1)
    gain = jnp.sum(jnp.where(diagonal, ngain_ref[...].astype(F32), 0.0), axis=1, keepdims=True)
    bias = jnp.sum(jnp.where(diagonal, pbias_ref[...].astype(F32), 0.0), axis=1, keepdims=True)
    pt_ref[:, 0:CHANNELS] = proj_ref[...]
    own_b1[...] = b1_ref[...].reshape(1, 384)
    first_lane = lax.broadcasted_iota(jnp.int32, (64, 128), 1) == 0
    pt_ref[:, CHANNELS:EXT] = jnp.where(first_lane, bias, 0.0).astype(BF)
    for j in range(8):
        gb_ref[j, :, 128:384] = (kvw_ref[:, j * 256:j * 256 + 256].astype(F32) * gain).astype(BF)
    gb_ref[0, :, 0:128] = (downw_ref[...].astype(F32) * gain).astype(BF)
    gb_ref[1:8, :, 0:128] = jnp.zeros((7, 64, 128), BF)
    copies0 = [
        pltpu.make_async_copy(x_ref, pad.at[3:7, 16:48], lsem.at[0]),
        pltpu.make_async_copy(w1_ref, wa.at[0], lsem.at[1]),
        pltpu.make_async_copy(w2_ref, wb.at[0], lsem.at[2]),
        pltpu.make_async_copy(own_b1, ba.at[0], lsem.at[3]),
        pltpu.make_async_copy(pt_ref, pb.at[0, :, 0:EXT], lsem.at[4]),
        pltpu.make_async_copy(gb_ref.at[pair], pb.at[0, :, EXT:2048], lsem.at[5]),
    ]
    for copy in copies0:
        copy.start()
    pl.semaphore_wait(barrier, len(partners))

    h_up = push(x_ref.at[:, 0:16], pad.at[3:7, 48:64], up_dev)
    h_dn = push(x_ref.at[:, 16:32], pad.at[3:7, 0:16], dn_dev)
    h_rt = push(x_ref.at[1:4], pad.at[0:3, 16:48], rt_dev)
    h_lt = push(x_ref.at[0:3], pad.at[7:10, 16:48], lt_dev)
    gb_copies = []
    pt_copies = []
    for dx in (1, 3, 2):
        pt_copies.append(push(pt_ref, pb.at[2 * dx, :, 0:EXT], device(dx, 0, 0, 0)))
    for dx in range(4):
        for dk in range(2):
            if (dx, dk) != (0, 0):
                target_pair = ((x + dx) % 4) * 2 + (core + dk) % 2
                gb_copies.append(
                    push(gb_ref.at[target_pair], pb.at[2 * dx + dk, :, EXT:2048], device(dx, 0, 0, dk))
                )
    fwd_copies = [push(pt_ref, pb.at[1, :, 0:EXT], other)]
    w_core = [
        push(w1_ref, wa.at[1], other), push(w2_ref, wb.at[1], other), push(own_b1, ba.at[1], other),
    ]
    x_half = x % 2

    def w1_rows(half, part_of, count):
        return pl.ds(pl.multiple_of(half * 768 + part_of * 384, 16), count)

    def w2_rows(half, part_of, count):
        return pl.ds(pl.multiple_of(half * 192 + part_of * 96, 16), count)

    w_y = []
    for n in range(2):
        rows1, rows2 = w1_rows(x_half, n, 384), w2_rows(x_half, n, 96)
        w_y.append([
            push(w1_ref.at[rows1], wa.at[2, rows1], device(0, 1, 0, 0)),
            push(w2_ref.at[rows2], wb.at[2, rows2], device(0, 3, 0, 0)),
        ])
    w_y[0].append(push(own_b1, ba.at[2], device(0, 1, 0, 0)))

    w_x = []

    def share_w(n):
        for copy in w_y[n]:
            copy.wait()
        rows1, rows2 = w1_rows(x_half, n, 384), w2_rows(x_half, n, 96)
        w_x.append(push(wa.at[2, rows1], wa.at[2, rows1], device(1, 0, 0, 0)))
        w_x.append(push(wb.at[2, rows2], wb.at[2, rows2], device(3, 0, 0, 0)))

    token = lax.broadcasted_iota(jnp.int32, (128, 128), 0)
    later = token >= 64
    start = jnp.where(later, start_ref[core * 2 + 1], start_ref[core * 2])
    position = start + (row * 8 + col // 2) * 64 + jnp.where(later, token - 64, token)
    angle = position.astype(F32) * freq_ref[...]
    cos_ref[...] = jnp.cos(angle)
    upper = lax.broadcasted_iota(jnp.int32, (128, 128), 1) >= 64
    sin_ref[...] = jnp.where(upper, 1.0, -1.0) * jnp.sin(angle)
    up_ref[...] = jnp.zeros((128, 2048), BF)
    up_ref[0:64, 0:1024] = (upw_ref[0].astype(F32) * 0.5).astype(BF)
    up_ref[64:128, 1024:2048] = (upw_ref[1].astype(F32) * 0.5).astype(BF)
    for a in range(7):
        taps_ref[a, 0:7, :] = depth_ref[a].astype(F32)
    cosine = cos_ref[...]
    sine = sin_ref[...]
    for head in range(8):
        lanes = slice(head * 128, head * 128 + 128)
        value = cot_ref[:, lanes].astype(F32)
        grad[:, lanes] = (value * cosine - pltpu.roll(value, 64, 1) * sine).astype(BF)
    grad[:, 1024:2048] = cot_ref[:, 1024:2048]
    adapter_grad = dot_nt(grad[...], up_ref[...]).astype(BF).astype(F32)
    for copy in copies0:
        copy.wait()
    for n in range(3):
        lanes = slice(n * 512, n * 512 + 512)
        feat[:, lanes] = dot(perm_ref[...], x_ref[:, :, lanes].reshape(128, 512))

    h_up.wait()
    h_dn.wait()

    @pl.when(row == 0)
    def _():
        pad[3:7, 0:16] = jnp.zeros((4, 16, CHANNELS), BF)

    @pl.when(row == 7)
    def _():
        pad[3:7, 48:64] = jnp.zeros((4, 16, CHANNELS), BF)

    corners = [
        push(pad.at[4:7, 0:16], pad.at[0:3, 0:16], rt_dev),
        push(pad.at[4:7, 48:64], pad.at[0:3, 48:64], rt_dev),
        push(pad.at[3:6, 0:16], pad.at[7:10, 0:16], lt_dev),
        push(pad.at[3:6, 48:64], pad.at[7:10, 48:64], lt_dev),
    ]

    for n, dx in enumerate((1, 3, 2)):
        pt_copies[n].wait()
        fwd_copies.append(push(pb.at[2 * dx, :, 0:EXT], pb.at[2 * dx + 1, :, 0:EXT], other))
    for copy in gb_copies:
        copy.wait()
    for copy in fwd_copies:
        copy.wait()

    def products(quad, width, first):
        def body(i, carry):
            left = pb[:, :, pl.ds(pl.multiple_of(i * 128, 128), 128)].reshape(512, 128)
            if first:
                shift = i + pair - 1
                around = jnp.where(shift >= 13, shift - 13, shift)
                start = pl.multiple_of(jnp.where(pair == 0, 13, around) * 128, 128)
            else:
                start = EXT + 128
            right = pb[:, :, pl.ds(start, width)].reshape(512, width)
            value = dot_tn(left, right).astype(BF).reshape(4, 2, 16, width)
            for r in range(4):
                p = i * 4 + r
                quad[p // 12, p % 12] = value[r]
            return carry

        lax.fori_loop(0, 13, body, 0)

    class Chain:
        def __init__(self, quad, red_z, red_mid, red_y, red_bias, mf):
            self.quad, self.red_z, self.red_mid = quad, red_z, red_mid
            self.red_y, self.red_bias, self.mf = red_y, red_bias, mf

        def start(self):
            self.copies = []
            for n, dz in enumerate((1, 3, 2)):
                target = device(0, 0, dz, 0)
                block = self.quad.at[0:4, pl.ds(((z + dz) % 4) * 3, 3)]
                self.copies.append(push(block, self.red_z.at[n], target))
                self.copies.append(push(self.quad.at[4, 0, 0], self.red_bias.at[n], target))

        def middle(self):
            for copy in self.copies:
                copy.wait()

            def body(n, carry):
                h, p = n // 3, n % 3
                total = self.quad[h, z * 3 + p].astype(F32)
                for m in range(3):
                    total = total + self.red_z[m, h, p].astype(F32)
                self.red_mid[h, p] = total.astype(BF)
                return carry

            lax.fori_loop(0, 12, body, 0)
            total = self.quad[4, 0, 0].astype(F32)
            for m in range(3):
                total = total + self.red_bias[m].astype(F32)
            self.red_bias[6] = total.astype(BF)
            self.copies = []
            for n, dy in enumerate((1, 3, 2)):
                target = device(0, dy, 0, 0)
                self.copies.append(push(self.red_mid.at[(y + dy) % 4], self.red_y.at[n], target))
                self.copies.append(push(self.red_bias.at[6], self.red_bias.at[3 + n], target))

        def spread(self):
            for copy in self.copies:
                copy.wait()

            def body(p, carry):
                total = self.red_mid[y, p].astype(F32)
                for m in range(3):
                    total = total + self.red_y[m, p].astype(F32)
                self.mf[pair, pl.ds(plane * 6 + p * 2, 2)] = total.astype(BF)
                return carry

            lax.fori_loop(0, 3, body, 0)
            total = self.red_bias[6].astype(F32)
            for m in range(3):
                total = total + self.red_bias[3 + m].astype(F32)
            self.mf[pair, 96] = total.astype(BF)
            block = self.mf.at[pair, pl.ds(plane * 6, 6)]
            self.copies = [push(block, block, device(0, 0, dz, 0)) for dz in (1, 3, 2)]

        def fan(self):
            for copy in self.copies:
                copy.wait()
            block = self.piece(pair, 0)
            self.copies = [push(block, block, device(0, dy, 0, 0)) for dy in (1, 3, 2)]

        def piece(self, owner, dy, low=0, count=24):
            return self.mf.at[owner, pl.ds(((y + dy) % 4) * 24 + low, count)]

    chain_a = Chain(quad_a, red_z_a, red_mid_a, red_y_a, red_bias_a, mf_a)
    chain_b = Chain(quad_b, red_z_b, red_mid_b, red_y_b, red_bias_b, mf_b)
    x_prev = ((x + 3) % 4) * 2 + core
    x_next = ((x + 1) % 4) * 2 + core
    x_far = ((x + 2) % 4) * 2 + core
    m_core = []

    def send_whole():
        for copy in chain_a.copies:
            copy.wait()
        whole = mf_a.at[pair]
        sent = [push(whole, whole, device(1, 0, 0, 0)), push(whole, whole, device(3, 0, 0, 0))]
        m_core.append(push(whole, whole, other))
        return sent

    def relay_whole(sent):
        sent[0].wait()
        low, high = mf_a.at[x_prev, 0:48], mf_a.at[x_next, 48:97]
        far = [push(low, low, device(1, 0, 0, 0))]
        m_core.append(push(mf_a.at[x_prev], mf_a.at[x_prev], other))
        sent[1].wait()
        far.append(push(high, high, device(3, 0, 0, 0)))
        m_core.append(push(mf_a.at[x_next], mf_a.at[x_next], other))
        return far

    def finish_whole(far):
        for copy in far:
            copy.wait()
        push(mf_a.at[x_far], mf_a.at[x_far], other).wait()
        for copy in m_core:
            copy.wait()
        del m_core[:]

    piece = chain_b.piece

    def send_piece(dy):
        block = piece(pair, dy)
        sent = [push(block, block, device(1, 0, 0, 0)), push(block, block, device(3, 0, 0, 0))]
        m_core.append(push(block, block, other))
        return sent

    def relay_piece(dy, sent):
        sent[0].wait()
        low, high = piece(x_prev, dy, 0, 12), piece(x_next, dy, 12, 12)
        far = [push(low, low, device(1, 0, 0, 0))]
        m_core.append(push(piece(x_prev, dy), piece(x_prev, dy), other))
        sent[1].wait()
        far.append(push(high, high, device(3, 0, 0, 0)))
        m_core.append(push(piece(x_next, dy), piece(x_next, dy), other))
        return far

    def finish_piece(dy, far):
        far[0].wait()
        far[1].wait()
        m_core.append(push(piece(x_far, dy), piece(x_far, dy), other))

    products(quad_a, 128, True)
    chain_a.start()
    share_w(0)
    h_rt.wait()
    h_lt.wait()
    for copy in corners:
        copy.wait()

    @pl.when(col == 0)
    def _():
        pad[0:3] = jnp.zeros((3, 64, CHANNELS), BF)

    @pl.when(col == 15)
    def _():
        pad[7:10] = jnp.zeros((3, 64, CHANNELS), BF)

    def conv_lanes(n, carry):
        lanes = pl.ds(pl.multiple_of(n * 128, 128), 128)
        sums = [jnp.zeros((32, 128), F32) + dbias_ref[lanes].reshape(1, 128) for _ in range(4)]
        for wp in range(10):
            full = pad[wp, :, lanes].astype(F32)
            moved = pltpu.roll(full, 60, 0)
            for a in range(7):
                start = 4 * (a + 1)
                window = full[start:start + 32] if a % 2 else moved[start - 4:start + 28]
                for w in range(max(0, wp - 6), min(3, wp) + 1):
                    sums[w] = sums[w] + window * taps_ref[a, wp - w:wp - w + 1, lanes]
        for w in range(4):
            conv[w, :, lanes] = sums[w]
        return carry

    lax.fori_loop(0, BLOCKS, conv_lanes, 0)

    def norm_rows(n, carry):
        w = n // 2
        rows = pl.ds(pl.multiple_of((n % 2) * 16, 16), 16)
        value = conv[w, rows, :]
        center = jnp.sum(value, axis=-1, keepdims=True) * (1.0 / CHANNELS)
        centered = value - center
        variance = jnp.sum(centered * centered, axis=-1, keepdims=True) * (1.0 / CHANNELS)
        value = centered * lax.rsqrt(variance + 1e-06) * lgain_ref[...].reshape(1, CHANNELS) + lshift_ref[...].reshape(1, CHANNELS)
        part[0, w, rows, :] = value.astype(BF)
        return carry

    lax.fori_loop(0, 8, norm_rows, 0)
    for n in range(3):
        lanes = slice(n * 512, n * 512 + 512)
        tok[0, :, lanes] = dot(perm_ref[...], part[0, :, :, lanes].reshape(128, 512)).astype(BF)
    t_next = push(tok.at[0], tok.at[1], device(0, 0, 1, 0))
    t_prev = push(tok.at[0], tok.at[2], device(0, 0, 3, 0))

    share_w(1)
    products(quad_b, 256, False)
    chain_b.start()
    chain_a.middle()
    def mlp(slot, count, weights, first):
        rows = 128 * count
        tokens = tok[slot:slot + count].reshape(rows, CHANNELS)
        for index, s in enumerate(weights):
            pre = dot(tokens, wa[s]) + ba[s]
            hidden = (0.5 * pre * (1.0 + lax.erf(pre * (0.5 ** 0.5)))).astype(BF)
            for n in range(3):
                lanes = slice(n * 512, n * 512 + 512)
                term = dot(hidden, wb[s, :, lanes])
                if first and index == 0:
                    acc[0:rows, lanes] = term
                else:
                    acc[0:rows, lanes] += term

    def scatter(slot):
        sent = []
        for tau in (1, 3, 2):
            into = SLOT_OF[(OFFSET[slot] - tau) % 4]
            peer = SLOT_OF[(-tau) % 4] - 1
            sent.append(
                push(part.at[slot, (z + tau) % 4], rs_in.at[peer, into], device(0, 0, tau, 0))
            )
        return sent

    scale = scale_ref[...].reshape(1, CHANNELS)
    mlp(0, 1, (0,), True)
    for copy in w_core:
        copy.wait()
    mlp(0, 1, (1,), False)

    chain_a.spread()
    own_half = [(wa, w1_rows(x_half, 0, 768)), (wb, w2_rows(x_half, 0, 192))]
    their_half = [(wa, w1_rows(1 - x_half, 0, 768)), (wb, w2_rows(1 - x_half, 0, 192))]
    w_fwd = [push(ref.at[2, rows], ref.at[3, rows], other) for ref, rows in own_half]
    w_fwd.append(push(ba.at[2], ba.at[3], other))
    t_next.wait()
    t_far0 = push(tok.at[1, 0:64], tok.at[3, 0:64], device(0, 0, 1, 0))
    t_prev.wait()
    t_far1 = push(tok.at[2, 64:128], tok.at[3, 64:128], device(0, 0, 3, 0))
    for copy in w_x:
        copy.wait()
    w_fwd += [push(ref.at[2, rows], ref.at[3, rows], other) for ref, rows in their_half]
    mlp(0, 1, (2,), False)
    for copy in w_fwd:
        copy.wait()
    mlp(0, 1, (3,), False)
    part[0] = (acc[0:128, :] * scale + (feat[...] + scale * rbias_ref[...].reshape(1, CHANNELS))).astype(BF).reshape(4, 32, CHANNELS)
    scatters = scatter(0)
    chain_a.fan()
    mlp(1, 2, (0, 1, 2, 3), True)
    for slot in (1, 2):
        part[slot] = (acc[128 * slot - 128:128 * slot, :] * scale).astype(BF).reshape(4, 32, CHANNELS)
        scatters += scatter(slot)
    sent_a = send_whole()
    chain_b.middle()
    t_far0.wait()
    t_far1.wait()
    mlp(3, 1, (0, 1, 2, 3), True)
    part[3] = (acc[0:128, :] * scale).astype(BF).reshape(4, 32, CHANNELS)
    scatters += scatter(3)
    chain_b.spread()
    far_a = relay_whole(sent_a)
    chain_b.fan()
    b_bias = [push(mf_b.at[pair, 96], mf_b.at[pair, 96], device(dx, 0, 0, 0)) for dx in (1, 3, 2)]
    for copy in scatters:
        copy.wait()

    for slot in range(4):
        for n in range(3):
            lanes = slice(n * 512, n * 512 + 512)
            value = part[slot, z, :, lanes].astype(F32)
            for peer in range(3):
                value = value + rs_in[peer, slot, :, lanes].astype(F32)
            for q in range(4):
                stage_t[q, (z + OFFSET[slot] + 4) % 4, :, lanes] = value[8 * q:8 * q + 8]
    for q in range(4):
        stage_b[q] = stage_t[q].reshape(32, CHANNELS).astype(BF)
    my_q = ylo * 2 + core
    seq_copies = []
    for dy in range(2):
        for dk in range(2):
            if (dy, dk) != (0, 0):
                q = ((ylo + dy) % 2) * 2 + (core + dk) % 2
                seq_copies.append(push(stage_b.at[q], seq_in.at[my_q], device(0, dy * yflip, 0, dk)))
    seq_in[my_q] = stage_b[my_q]

    sent_0 = send_piece(0)
    for copy in seq_copies:
        copy.wait()
    for n in range(3):
        lanes = slice(n * 512, n * 512 + 512)
        tok[0, :, lanes] = dot(seq_ref[...], seq_in[:, :, lanes].reshape(128, 512)).astype(BF)
    for b in range(19):
        if b % 13 == 12:
            ext[:, b * 128:b * 128 + 128] = jnp.where(
                lax.broadcasted_iota(jnp.int32, (128, 128), 1) == 0, 1.0, 0.0
            )
        else:
            lanes = slice((b % 13) * 128, (b % 13) * 128 + 128)
            ext[:, b * 128:b * 128 + 128] = tok[0, :, lanes].astype(F32)
    finish_whole(far_a)
    all_y = chain_b.copies
    all_y[0].wait()
    sent_3 = send_piece(3)

    encoded = tok[0]

    def squares_of(i, total):
        cells = tok[0, :, pl.ds(pl.multiple_of(i * 128, 128), 128)]
        for d in range(7):
            value = dot(cells, mf_a[1 + d, pl.ds(i * 8, 8)].reshape(128, 128))
            turned = ext[:, pl.ds(pl.multiple_of((i + d) * 128, 128), 128)]
            total = total + (1.0 if d == 0 else 2.0) * (value * turned)
        return total

    total = lax.fori_loop(0, BLOCKS, squares_of, jnp.zeros((128, 128), F32))
    for d in range(7):
        weight = mf_a[1 + d, 96].astype(F32)[0:1]
        total = total + (1.0 if d == 0 else 2.0) * weight * ext[:, (12 + d) * 128:(13 + d) * 128]
    squares = jnp.maximum(jnp.sum(total, axis=-1, keepdims=True), 0.0)
    inverse = lax.rsqrt(squares * (1.0 / LANGUAGE_WIDTH) + 1e-06)
    adapter_in = dot(encoded, mf_a[0, 0:96].reshape(CHANNELS, 128)) + mf_a[0, 96].astype(F32)[0:1]
    adapter_in = (inverse * adapter_in).astype(BF)
    weighted = (inverse * adapter_grad).astype(BF)

    def place(group, value):
        ein[group // 80, group % 80 // 5, group % 5] = value

    for n in range(3):
        value = dot_tn(encoded[:, n * 512:n * 512 + 512], weighted).astype(BF).reshape(32, 16, 128)
        for g in range(32):
            place(n * 32 + g, value[g])
    for n in range(16):
        value = dot_tn(adapter_in, grad[:, n * 128:n * 128 + 128])
        value = value[0:64] if n < 8 else value[64:128]
        value = (0.5 * value).astype(BF).reshape(4, 16, 128)
        for g in range(4):
            place(96 + 4 * n + g, value[g])
    shifted = jnp.sum(weighted.astype(F32), axis=0, keepdims=True)
    shifted = jnp.where(lax.broadcasted_iota(jnp.int32, (16, 128), 0) == 0, shifted, 0.0).astype(BF)
    for half in range(2):
        for p in range(16):
            ein[half, p, 5] = shifted
    joined = push(ein.at[1 - core], e_core, other)
    all_y[1].wait()
    sent_1 = send_piece(1)
    all_y[2].wait()
    sent_2 = send_piece(2)
    joined.wait()

    def sum_cores(p, carry):
        e_mid[p] = (ein[core, p].astype(F32) + e_core[p].astype(F32)).astype(BF)
        return carry

    lax.fori_loop(0, 16, sum_cores, 0)
    sums = []
    for n, (dy, dz) in enumerate(planes):
        target_plane = ((y + dy) % 4) * 4 + (z + dz) % 4
        sums.append(push(e_mid.at[target_plane], e_in1.at[n], device(0, dy, dz, 0)))
    far_0 = relay_piece(0, sent_0)
    far_3 = relay_piece(3, sent_3)
    for copy in sums:
        copy.wait()
    value = e_mid[plane].astype(F32)
    for n in range(15):
        value = value + e_in1[n].astype(F32)
    e_in2[x] = value.astype(BF)
    sums = [push(e_in2.at[x], e_in2.at[x], device(dx, 0, 0, 0)) for dx in (1, 3, 2)]
    far_1 = relay_piece(1, sent_1)
    finish_piece(0, far_0)
    for copy in sums:
        copy.wait()
    value = e_in2[0].astype(F32)
    for n in range(1, 4):
        value = value + e_in2[n].astype(F32)
    value = value.astype(BF)
    mine = e_all.at[pl.ds(core * 80 + plane * 5, 5)]
    mine[...] = value[0:5]
    total_shift = value[5].astype(F32)[0:1]
    sums = [push(mine, mine, device(0, dy, dz, 0)) for dy, dz in planes]
    far_2 = relay_piece(2, sent_2)
    finish_piece(3, far_3)
    finish_piece(1, far_1)
    for copy in b_bias:
        copy.wait()
    for owner in (pair, x_prev, x_next, x_far):
        m_core.append(push(mf_b.at[owner, 96], mf_b.at[owner, 96], other))
    finish_piece(2, far_2)
    for copy in sums:
        copy.wait()
    mine = e_all.at[pl.ds(core * 80, 80)]
    joined = push(mine, mine, other)
    for copy in m_core:
        copy.wait()

    for n in range(8):
        lanes = slice(n * 256, n * 256 + 256)
        value = dot(encoded, mf_b[n, 0:96].reshape(CHANNELS, 256)) + mf_b[n, 96].astype(F32)[0:1]
        value = inverse * value + (kvb_ref[0:1, lanes] + dot(adapter_in, up_ref[:, lanes]))
        if n < 4:
            for h in range(2):
                head = value[:, h * 128:h * 128 + 128]
                turned = head * cosine + pltpu.roll(head, 64, 1) * sine
                kv_ref[:, n * 256 + h * 128:n * 256 + h * 128 + 128] = turned.astype(BF)
        else:
            kv_ref[:, lanes] = value.astype(BF)
    joined.wait()
    down = dot(pt_ref[:, 0:CHANNELS], e_all[0:96].reshape(CHANNELS, 128))
    down_ref[...] = (down + bias * total_shift) * gain
    for n in range(16):
        lanes = slice((n % 8) * 128, (n % 8) * 128 + 128)
        upg_ref[n // 8, :, lanes] = e_all[96 + 4 * n:100 + 4 * n].reshape(64, 128).astype(F32)


def orders():
    tile = [[0.0] * 128 for _ in range(128)]
    seq = [[0.0] * 128 for _ in range(128)]
    for w in range(4):
        for h in range(8):
            for i in range(4):
                tile[(h % 4) * 32 + (h // 4) * 16 + (i // 2) * 8 + w * 2 + i % 2][w * 32 + h * 4 + i] = 1.0
    for ys in range(2):
        for cs in range(2):
            for zs in range(4):
                for w in range(4):
                    for i in range(2):
                        here = (ys * 2 + cs) * 32 + zs * 8 + w * 2 + i
                        seq[i * 64 + ys * 32 + zs * 8 + cs * 4 + w][here] = 1.0
    return jnp.array(tile, BF), jnp.array(seq, BF)


def local(
    feature_grid, depthwise_kernel, depthwise_bias, layer_norm_gain, layer_norm_shift,
    expansion_weight, expansion_bias, reduction_weight, reduction_bias, layer_branch_scale,
    projector_weight, projector_bias, input_norm_gain, key_value_weight, key_value_bias,
    adapter_down_weight, adapter_up_weight, image_start_positions, key_value_cotangent,
):
    cells = feature_grid.transpose(2, 0, 1, 3).reshape(4, 32, CHANNELS)
    freq = np.exp(np.arange(HEAD_DIM // 2, dtype=np.float32) * np.float32(-2.0 * math.log(ROPE_THETA) / HEAD_DIM))
    freq = jnp.array(np.concatenate([freq, freq])[None, :], F32)
    tile_order, seq_order = orders()
    vmem = pl.BlockSpec(memory_space=pltpu.VMEM)
    kv, down, upg = pl.pallas_call(
        kernel,
        out_shape=(
            jax.ShapeDtypeStruct((128, 2048), BF),
            jax.ShapeDtypeStruct((64, 128), F32),
            jax.ShapeDtypeStruct((2, 64, 1024), F32),
        ),
        in_specs=[vmem] * 5 + [pl.BlockSpec(memory_space=pl.ANY)] * 2 + [vmem] * 10 + [pl.BlockSpec(memory_space=pltpu.SMEM)] + [vmem] * 4,
        out_specs=(vmem, vmem, vmem),
        scratch_shapes=[
            pltpu.VMEM((10, 64, CHANNELS), BF),
            pltpu.VMEM((4, 32, CHANNELS), F32),
            pltpu.VMEM((4, 128, CHANNELS), BF),
            pltpu.VMEM((4, CHANNELS, 384), BF),
            pltpu.VMEM((4, 384, CHANNELS), BF),
            pltpu.VMEM((4, 1, 384), F32),
            pltpu.VMEM((128, CHANNELS), F32),
            pltpu.VMEM((256, CHANNELS), F32),
            pltpu.VMEM((4, 4, 32, CHANNELS), BF),
            pltpu.VMEM((3, 4, 32, CHANNELS), BF),
            pltpu.VMEM((4, 4, 8, CHANNELS), F32),
            pltpu.VMEM((4, 32, CHANNELS), BF),
            pltpu.VMEM((4, 32, CHANNELS), BF),
            pltpu.VMEM((8, 64, 2048), BF),
            pltpu.VMEM((5, 12, 2, 16, 128), BF),
            pltpu.VMEM((3, 4, 3, 2, 16, 128), BF),
            pltpu.VMEM((4, 3, 2, 16, 128), BF),
            pltpu.VMEM((3, 3, 2, 16, 128), BF),
            pltpu.VMEM((7, 16, 128), BF),
            pltpu.VMEM((8, 97, 16, 128), BF),
            pltpu.VMEM((5, 12, 2, 16, 256), BF),
            pltpu.VMEM((3, 4, 3, 2, 16, 256), BF),
            pltpu.VMEM((4, 3, 2, 16, 256), BF),
            pltpu.VMEM((3, 3, 2, 16, 256), BF),
            pltpu.VMEM((7, 16, 256), BF),
            pltpu.VMEM((8, 97, 16, 256), BF),
            pltpu.VMEM((128, 19 * 128), F32),
            pltpu.VMEM((128, 2048), BF),
            pltpu.VMEM((2, 16, 6, 16, 128), BF),
            pltpu.VMEM((16, 6, 16, 128), BF),
            pltpu.VMEM((16, 6, 16, 128), BF),
            pltpu.VMEM((15, 6, 16, 128), BF),
            pltpu.VMEM((4, 6, 16, 128), BF),
            pltpu.VMEM((160, 16, 128), BF),
            pltpu.VMEM((64, EXT), BF),
            pltpu.VMEM((8, 64, 384), BF),
            pltpu.VMEM((128, 2048), BF),
            pltpu.VMEM((7, 8, CHANNELS), F32),
            pltpu.VMEM((128, 128), F32),
            pltpu.VMEM((128, 128), F32),
            pltpu.VMEM((1, 384), F32),
            pltpu.SemaphoreType.DMA((COPIES,)),
            pltpu.SemaphoreType.DMA((COPIES,)),
            pltpu.SemaphoreType.DMA((6,)),
        ],
        compiler_params=pltpu.CompilerParams(
            collective_id=0, has_side_effects=True, vmem_limit_bytes=62 << 20
        ),
        cost_estimate=pl.CostEstimate(flops=8_000_000_000, bytes_accessed=30_000_000, transcendentals=0),
    )(
        cells, depthwise_kernel, depthwise_bias, layer_norm_gain, layer_norm_shift,
        expansion_weight, reduction_weight, expansion_bias, reduction_bias,
        layer_branch_scale, projector_weight.T, projector_bias[None, :], input_norm_gain[None, :],
        key_value_weight, key_value_bias[None, :], adapter_down_weight, adapter_up_weight,
        image_start_positions, key_value_cotangent.reshape(128, 2048), freq, tile_order, seq_order,
    )
    return kv.reshape(2, 64, 2048), down, upg


def solution(mesh):
    in_specs = (
        P("row", None, "col", None), P(), P(), P(), P(),
        P(None, "col"), P("col"), P("col", None), P(), P(),
        P(None, ("row", "col")), P(("row", "col")), P(("row", "col")), P(("row", "col"), None), P(),
        P(("row", "col"), None), P(), P(), P(("row", "col"), None, None),
    )
    out_specs = (P(("row", "col"), None, None), P(("row", "col"), None), P())
    return jax.shard_map(local, mesh=mesh, in_specs=in_specs, out_specs=out_specs, check_vma=False)
```

```python
import functools
import math

import jax
import jax.numpy as jnp
import numpy as np
from jax import lax
from jax.experimental import pallas as pl
from jax.experimental.pallas import tpu as pltpu
from jax.sharding import PartitionSpec as P

LANGUAGE_WIDTH = 8192
HEAD_DIM = 128
IMAGES = 4
CHANNELS = 1536
BLOCKS = 12
EXT = 1664
ROPE_THETA = 1000000.0
MESH = pl.DeviceIdType.MESH
BF = jnp.bfloat16
F32 = jnp.float32
COPIES = 240
SLOT_OF = {0: 0, 3: 1, 1: 2, 2: 3}
OFFSET = (0, -1, 1, 2)


def dot(a, b):
    return jnp.dot(a, b, preferred_element_type=F32)


def dot_tn(a, b):
    return lax.dot_general(a, b, (((0,), (0,)), ((), ())), preferred_element_type=F32)


def dot_nt(a, b):
    return lax.dot_general(a, b, (((1,), (1,)), ((), ())), preferred_element_type=F32)


def kernel(
    x_ref, depth_ref, dbias_ref, lgain_ref, lshift_ref, w1_ref, w2_ref, b1_ref, rbias_ref, scale_ref,
    proj_ref, pbias_ref, ngain_ref, kvw_ref, kvb_ref, downw_ref, upw_ref, start_ref, cot_ref,
    freq_ref, perm_ref, seq_ref,
    kv_ref, down_ref, upg_ref,
    pad, conv, tok, wa, wb, ba, feat, acc, part, rs_in, stage_t, stage_b, seq_in,
    pb, quad_a, red_z_a, red_mid_a, red_y_a, red_bias_a, mf_a,
    quad_b, red_z_b, red_mid_b, red_y_b, red_bias_b, mf_b, ext, grad,
    ein, e_core, e_mid, e_in1, e_in2, e_all, pt_ref, gb_ref, up_ref, taps_ref, cos_ref, sin_ref, own_b1,
    send, recv, lsem,
):
    row = lax.axis_index("row")
    col = lax.axis_index("col")
    x = row // 2
    y = (row % 2) * 2 + col // 8
    z = (col % 8) // 2
    core = col % 2
    ylo = y % 2
    plane = y * 4 + z
    pair = x * 2 + core

    def device(dx, dy, dz, dk):
        xx, yy, zz, kk = (x + dx + 4) % 4, (y + dy + 4) % 4, (z + dz + 4) % 4, (core + dk) % 2
        return (xx * 2 + yy // 2, (yy % 2) * 8 + zz * 2 + kk)

    ids = [0]

    def push(src, dst, target):
        n = ids[0]
        ids[0] += 1
        copy = pltpu.make_async_remote_copy(
            src_ref=src, dst_ref=dst, send_sem=send.at[n], recv_sem=recv.at[n],
            device_id=target, device_id_type=MESH,
        )
        copy.start()
        return copy

    planes = [(dy, dz) for dy in range(4) for dz in range(4) if (dy, dz) != (0, 0)]
    up_dev = ((row + 7) % 8, col)
    dn_dev = ((row + 1) % 8, col)
    lt_dev = (row, (col + 15) % 16)
    rt_dev = (row, (col + 1) % 16)
    other = device(0, 0, 0, 1)
    yflip = 1 - 2 * ylo

    partners = [up_dev, dn_dev, lt_dev, rt_dev]
    for dx in range(4):
        for dk in range(2):
            if (dx, dk) != (0, 0):
                partners.append(device(dx, 0, 0, dk))
    for dy, dz in planes:
        partners.append(device(0, dy, dz, 0))
    partners.append(device(0, yflip, 0, 1))
    barrier = pltpu.get_barrier_semaphore()
    for partner in partners:
        pl.semaphore_signal(barrier, inc=1, device_id=partner, device_id_type=MESH)
    diagonal = lax.broadcasted_iota(jnp.int32, (64, 64), 0) == lax.broadcasted_iota(jnp.int32, (64, 64), 1)
    gain = jnp.sum(jnp.where(diagonal, ngain_ref[...].astype(F32), 0.0), axis=1, keepdims=True)
    bias = jnp.sum(jnp.where(diagonal, pbias_ref[...].astype(F32), 0.0), axis=1, keepdims=True)
    pt_ref[:, 0:CHANNELS] = proj_ref[...]
    own_b1[...] = b1_ref[...].reshape(1, 384)
    first_lane = lax.broadcasted_iota(jnp.int32, (64, 128), 1) == 0
    pt_ref[:, CHANNELS:EXT] = jnp.where(first_lane, bias, 0.0).astype(BF)
    for j in range(8):
        gb_ref[j, :, 128:384] = (kvw_ref[:, j * 256:j * 256 + 256].astype(F32) * gain).astype(BF)
    gb_ref[0, :, 0:128] = (downw_ref[...].astype(F32) * gain).astype(BF)
    gb_ref[1:8, :, 0:128] = jnp.zeros((7, 64, 128), BF)
    copies0 = [
        pltpu.make_async_copy(x_ref, pad.at[3:7, 16:48], lsem.at[0]),
        pltpu.make_async_copy(w1_ref, wa.at[0], lsem.at[1]),
        pltpu.make_async_copy(w2_ref, wb.at[0], lsem.at[2]),
        pltpu.make_async_copy(own_b1, ba.at[0], lsem.at[3]),
        pltpu.make_async_copy(pt_ref, pb.at[0, :, 0:EXT], lsem.at[4]),
        pltpu.make_async_copy(gb_ref.at[pair], pb.at[0, :, EXT:2048], lsem.at[5]),
    ]
    for copy in copies0:
        copy.start()
    pl.semaphore_wait(barrier, len(partners))

    h_up = push(x_ref.at[:, 0:16], pad.at[3:7, 48:64], up_dev)
    h_dn = push(x_ref.at[:, 16:32], pad.at[3:7, 0:16], dn_dev)
    h_rt = push(x_ref.at[1:4], pad.at[0:3, 16:48], rt_dev)
    h_lt = push(x_ref.at[0:3], pad.at[7:10, 16:48], lt_dev)
    gb_copies = []
    pt_copies = []
    for dx in (1, 3, 2):
        pt_copies.append(push(pt_ref, pb.at[2 * dx, :, 0:EXT], device(dx, 0, 0, 0)))
    for dx in range(4):
        for dk in range(2):
            if (dx, dk) != (0, 0):
                target_pair = ((x + dx) % 4) * 2 + (core + dk) % 2
                gb_copies.append(
                    push(gb_ref.at[target_pair], pb.at[2 * dx + dk, :, EXT:2048], device(dx, 0, 0, dk))
                )
    fwd_copies = [push(pt_ref, pb.at[1, :, 0:EXT], other)]
    w_core = [
        push(w1_ref, wa.at[1], other), push(w2_ref, wb.at[1], other), push(own_b1, ba.at[1], other),
    ]
    x_half = x % 2

    def w1_rows(half, part_of, count):
        return pl.ds(pl.multiple_of(half * 768 + part_of * 384, 16), count)

    def w2_rows(half, part_of, count):
        return pl.ds(pl.multiple_of(half * 192 + part_of * 96, 16), count)

    w_y = []
    for n in range(2):
        rows1, rows2 = w1_rows(x_half, n, 384), w2_rows(x_half, n, 96)
        w_y.append([
            push(w1_ref.at[rows1], wa.at[2, rows1], device(0, 1, 0, 0)),
            push(w2_ref.at[rows2], wb.at[2, rows2], device(0, 3, 0, 0)),
        ])
    w_y[0].append(push(own_b1, ba.at[2], device(0, 1, 0, 0)))

    w_x = []

    def share_w(n):
        for copy in w_y[n]:
            copy.wait()
        rows1, rows2 = w1_rows(x_half, n, 384), w2_rows(x_half, n, 96)
        w_x.append(push(wa.at[2, rows1], wa.at[2, rows1], device(1, 0, 0, 0)))
        w_x.append(push(wb.at[2, rows2], wb.at[2, rows2], device(3, 0, 0, 0)))

    token = lax.broadcasted_iota(jnp.int32, (128, 128), 0)
    later = token >= 64
    start = jnp.where(later, start_ref[core * 2 + 1], start_ref[core * 2])
    position = start + (row * 8 + col // 2) * 64 + jnp.where(later, token - 64, token)
    angle = position.astype(F32) * freq_ref[...]
    cos_ref[...] = jnp.cos(angle)
    upper = lax.broadcasted_iota(jnp.int32, (128, 128), 1) >= 64
    sin_ref[...] = jnp.where(upper, 1.0, -1.0) * jnp.sin(angle)
    up_ref[...] = jnp.zeros((128, 2048), BF)
    up_ref[0:64, 0:1024] = (upw_ref[0].astype(F32) * 0.5).astype(BF)
    up_ref[64:128, 1024:2048] = (upw_ref[1].astype(F32) * 0.5).astype(BF)
    for a in range(7):
        taps_ref[a, 0:7, :] = depth_ref[a].astype(F32)
    cosine = cos_ref[...]
    sine = sin_ref[...]
    for head in range(8):
        lanes = slice(head * 128, head * 128 + 128)
        value = cot_ref[:, lanes].astype(F32)
        grad[:, lanes] = (value * cosine - pltpu.roll(value, 64, 1) * sine).astype(BF)
    grad[:, 1024:2048] = cot_ref[:, 1024:2048]
    adapter_grad = dot_nt(grad[...], up_ref[...]).astype(BF).astype(F32)
    for copy in copies0:
        copy.wait()
    for n in range(3):
        lanes = slice(n * 512, n * 512 + 512)
        feat[:, lanes] = dot(perm_ref[...], x_ref[:, :, lanes].reshape(128, 512))

    h_up.wait()
    h_dn.wait()

    @pl.when(row == 0)
    def _():
        pad[3:7, 0:16] = jnp.zeros((4, 16, CHANNELS), BF)

    @pl.when(row == 7)
    def _():
        pad[3:7, 48:64] = jnp.zeros((4, 16, CHANNELS), BF)

    corners = [
        push(pad.at[4:7, 0:16], pad.at[0:3, 0:16], rt_dev),
        push(pad.at[4:7, 48:64], pad.at[0:3, 48:64], rt_dev),
        push(pad.at[3:6, 0:16], pad.at[7:10, 0:16], lt_dev),
        push(pad.at[3:6, 48:64], pad.at[7:10, 48:64], lt_dev),
    ]

    for n, dx in enumerate((1, 3, 2)):
        pt_copies[n].wait()
        fwd_copies.append(push(pb.at[2 * dx, :, 0:EXT], pb.at[2 * dx + 1, :, 0:EXT], other))
    for copy in gb_copies:
        copy.wait()
    for copy in fwd_copies:
        copy.wait()

    def products(quad, width, first):
        def body(i, carry):
            left = pb[:, :, pl.ds(pl.multiple_of(i * 128, 128), 128)].reshape(512, 128)
            if first:
                shift = i + pair - 1
                around = jnp.where(shift >= 13, shift - 13, shift)
                start = pl.multiple_of(jnp.where(pair == 0, 13, around) * 128, 128)
            else:
                start = EXT + 128
            right = pb[:, :, pl.ds(start, width)].reshape(512, width)
            value = dot_tn(left, right).astype(BF).reshape(4, 2, 16, width)
            for r in range(4):
                p = i * 4 + r
                quad[p // 12, p % 12] = value[r]
            return carry

        lax.fori_loop(0, 13, body, 0)

    class Chain:
        def __init__(self, first, quad, red_1, red_mid, red_2, red_bias, mf):
            self.quad, self.red_1, self.red_mid = quad, red_1, red_mid
            self.red_2, self.red_bias, self.mf = red_2, red_bias, mf
            self.first = first
            self.third = lambda n: pl.ds(((z + n) % 4) * 3, 3)

        def toward(self, axis, n):
            return device(0, n, 0, 0) if axis == 1 else device(0, 0, n, 0)

        def start(self):
            self.copies = []
            for n, step in enumerate((1, 3, 2)):
                target = self.toward(self.first, step)
                if self.first == 2:
                    block = self.quad.at[0:4, self.third(step)]
                else:
                    block = self.quad.at[(y + step) % 4]
                self.copies.append(push(block, self.red_1.at[n], target))
                self.copies.append(push(self.quad.at[4, 0, 0], self.red_bias.at[n], target))

        def middle(self):
            for copy in self.copies:
                copy.wait()

            def body(n, carry):
                if self.first == 2:
                    own, place = (n // 3, z * 3 + n % 3), (n // 3, n % 3)
                else:
                    own, place = (y, n), (n,)
                total = self.quad[own].astype(F32)
                for m in range(3):
                    total = total + self.red_1[(m,) + place].astype(F32)
                self.red_mid[place] = total.astype(BF)
                return carry

            lax.fori_loop(0, 12, body, 0)
            total = self.quad[4, 0, 0].astype(F32)
            for m in range(3):
                total = total + self.red_bias[m].astype(F32)
            self.red_bias[6] = total.astype(BF)
            self.copies = []
            for n, step in enumerate((1, 3, 2)):
                target = self.toward(3 - self.first, step)
                if self.first == 2:
                    block = self.red_mid.at[(y + step) % 4]
                else:
                    block = self.red_mid.at[self.third(step)]
                self.copies.append(push(block, self.red_2.at[n], target))
                self.copies.append(push(self.red_bias.at[6], self.red_bias.at[3 + n], target))

        def spread(self):
            for copy in self.copies:
                copy.wait()

            def body(p, carry):
                own = (y, p) if self.first == 2 else (z * 3 + p,)
                total = self.red_mid[own].astype(F32)
                for m in range(3):
                    total = total + self.red_2[m, p].astype(F32)
                self.mf[pair, pl.ds(plane * 6 + p * 2, 2)] = total.astype(BF)
                return carry

            lax.fori_loop(0, 3, body, 0)
            total = self.red_bias[6].astype(F32)
            for m in range(3):
                total = total + self.red_bias[3 + m].astype(F32)
            self.mf[pair, 96] = total.astype(BF)
            block = self.mf.at[pair, pl.ds(plane * 6, 6)]
            self.copies = [push(block, block, device(0, 0, dz, 0)) for dz in (1, 3, 2)]

        def fan(self):
            for copy in self.copies:
                copy.wait()
            block = self.piece(pair, 0)
            self.copies = [push(block, block, device(0, dy, 0, 0)) for dy in (1, 3, 2)]

        def piece(self, owner, dy, low=0, count=24):
            return self.mf.at[owner, pl.ds(((y + dy) % 4) * 24 + low, count)]

    chain_a = Chain(2, quad_a, red_z_a, red_mid_a, red_y_a, red_bias_a, mf_a)
    chain_b = Chain(1, quad_b, red_z_b, red_mid_b, red_y_b, red_bias_b, mf_b)
    x_prev = ((x + 3) % 4) * 2 + core
    x_next = ((x + 1) % 4) * 2 + core
    x_far = ((x + 2) % 4) * 2 + core
    m_core = []

    def send_whole():
        for copy in chain_a.copies:
            copy.wait()
        whole = mf_a.at[pair]
        sent = [push(whole, whole, device(1, 0, 0, 0)), push(whole, whole, device(3, 0, 0, 0))]
        m_core.append(push(whole, whole, other))
        return sent

    def relay_whole(sent):
        sent[0].wait()
        low, high = mf_a.at[x_prev, 0:48], mf_a.at[x_next, 48:97]
        far = [push(low, low, device(1, 0, 0, 0))]
        m_core.append(push(mf_a.at[x_prev], mf_a.at[x_prev], other))
        sent[1].wait()
        far.append(push(high, high, device(3, 0, 0, 0)))
        m_core.append(push(mf_a.at[x_next], mf_a.at[x_next], other))
        return far

    def finish_whole(far):
        for copy in far:
            copy.wait()
        push(mf_a.at[x_far], mf_a.at[x_far], other).wait()
        for copy in m_core:
            copy.wait()
        del m_core[:]

    piece = chain_b.piece

    def send_piece(dy):
        block = piece(pair, dy)
        sent = [push(block, block, device(1, 0, 0, 0)), push(block, block, device(3, 0, 0, 0))]
        m_core.append(push(block, block, other))
        return sent

    def relay_piece(dy, sent):
        sent[0].wait()
        low, high = piece(x_prev, dy, 0, 12), piece(x_next, dy, 12, 12)
        far = [push(low, low, device(1, 0, 0, 0))]
        m_core.append(push(piece(x_prev, dy), piece(x_prev, dy), other))
        sent[1].wait()
        far.append(push(high, high, device(3, 0, 0, 0)))
        m_core.append(push(piece(x_next, dy), piece(x_next, dy), other))
        return far

    def finish_piece(dy, far):
        far[0].wait()
        far[1].wait()
        m_core.append(push(piece(x_far, dy), piece(x_far, dy), other))

    products(quad_a, 128, True)
    chain_a.start()
    share_w(0)
    h_rt.wait()
    h_lt.wait()
    for copy in corners:
        copy.wait()

    @pl.when(col == 0)
    def _():
        pad[0:3] = jnp.zeros((3, 64, CHANNELS), BF)

    @pl.when(col == 15)
    def _():
        pad[7:10] = jnp.zeros((3, 64, CHANNELS), BF)

    def conv_lanes(n, carry):
        lanes = pl.ds(pl.multiple_of(n * 128, 128), 128)
        sums = [jnp.zeros((32, 128), F32) + dbias_ref[lanes].reshape(1, 128) for _ in range(4)]
        for wp in range(10):
            full = pad[wp, :, lanes].astype(F32)
            moved = pltpu.roll(full, 60, 0)
            for a in range(7):
                start = 4 * (a + 1)
                window = full[start:start + 32] if a % 2 else moved[start - 4:start + 28]
                for w in range(max(0, wp - 6), min(3, wp) + 1):
                    sums[w] = sums[w] + window * taps_ref[a, wp - w:wp - w + 1, lanes]
        for w in range(4):
            conv[w, :, lanes] = sums[w]
        return carry

    lax.fori_loop(0, BLOCKS, conv_lanes, 0)

    def norm_rows(n, carry):
        w = n // 2
        rows = pl.ds(pl.multiple_of((n % 2) * 16, 16), 16)
        value = conv[w, rows, :]
        center = jnp.sum(value, axis=-1, keepdims=True) * (1.0 / CHANNELS)
        centered = value - center
        variance = jnp.sum(centered * centered, axis=-1, keepdims=True) * (1.0 / CHANNELS)
        value = centered * lax.rsqrt(variance + 1e-06) * lgain_ref[...].reshape(1, CHANNELS) + lshift_ref[...].reshape(1, CHANNELS)
        part[0, w, rows, :] = value.astype(BF)
        return carry

    lax.fori_loop(0, 8, norm_rows, 0)
    for n in range(3):
        lanes = slice(n * 512, n * 512 + 512)
        tok[0, :, lanes] = dot(perm_ref[...], part[0, :, :, lanes].reshape(128, 512)).astype(BF)
    t_next = push(tok.at[0], tok.at[1], device(0, 0, 1, 0))
    t_prev = push(tok.at[0], tok.at[2], device(0, 0, 3, 0))

    share_w(1)
    products(quad_b, 256, False)
    chain_b.start()
    chain_a.middle()
    def mlp(slot, count, weights, first):
        rows = 128 * count
        tokens = tok[slot:slot + count].reshape(rows, CHANNELS)
        for index, s in enumerate(weights):
            pre = dot(tokens, wa[s]) + ba[s]
            hidden = (0.5 * pre * (1.0 + lax.erf(pre * (0.5 ** 0.5)))).astype(BF)
            for n in range(3):
                lanes = slice(n * 512, n * 512 + 512)
                term = dot(hidden, wb[s, :, lanes])
                if first and index == 0:
                    acc[0:rows, lanes] = term
                else:
                    acc[0:rows, lanes] += term

    def scatter(slot):
        sent = []
        for tau in (1, 3, 2):
            into = SLOT_OF[(OFFSET[slot] - tau) % 4]
            peer = SLOT_OF[(-tau) % 4] - 1
            sent.append(
                push(part.at[slot, (z + tau) % 4], rs_in.at[peer, into], device(0, 0, tau, 0))
            )
        return sent

    scale = scale_ref[...].reshape(1, CHANNELS)
    mlp(0, 1, (0,), True)
    for copy in w_core:
        copy.wait()
    mlp(0, 1, (1,), False)

    chain_a.spread()
    own_half = [(wa, w1_rows(x_half, 0, 768)), (wb, w2_rows(x_half, 0, 192))]
    their_half = [(wa, w1_rows(1 - x_half, 0, 768)), (wb, w2_rows(1 - x_half, 0, 192))]
    w_fwd = [push(ref.at[2, rows], ref.at[3, rows], other) for ref, rows in own_half]
    w_fwd.append(push(ba.at[2], ba.at[3], other))
    chain_a.fan()
    t_next.wait()
    t_far0 = push(tok.at[1, 0:64], tok.at[3, 0:64], device(0, 0, 1, 0))
    t_prev.wait()
    t_far1 = push(tok.at[2, 64:128], tok.at[3, 64:128], device(0, 0, 3, 0))
    for copy in w_x:
        copy.wait()
    w_fwd += [push(ref.at[2, rows], ref.at[3, rows], other) for ref, rows in their_half]
    mlp(0, 1, (2,), False)
    chain_b.middle()
    for copy in w_fwd:
        copy.wait()
    mlp(0, 1, (3,), False)
    part[0] = (acc[0:128, :] * scale + (feat[...] + scale * rbias_ref[...].reshape(1, CHANNELS))).astype(BF).reshape(4, 32, CHANNELS)
    scatters = scatter(0)
    sent_a = send_whole()
    chain_b.spread()
    mlp(1, 2, (0, 1, 2, 3), True)
    for slot in (1, 2):
        part[slot] = (acc[128 * slot - 128:128 * slot, :] * scale).astype(BF).reshape(4, 32, CHANNELS)
        scatters += scatter(slot)
    chain_b.fan()
    b_bias = [push(mf_b.at[pair, 96], mf_b.at[pair, 96], device(dx, 0, 0, 0)) for dx in (1, 3, 2)]
    t_far0.wait()
    t_far1.wait()
    mlp(3, 1, (0, 1, 2, 3), True)
    part[3] = (acc[0:128, :] * scale).astype(BF).reshape(4, 32, CHANNELS)
    scatters += scatter(3)
    far_a = relay_whole(sent_a)
    sent_0 = send_piece(0)
    all_y = chain_b.copies
    all_y[0].wait()
    sent_3 = send_piece(3)
    all_y[1].wait()
    sent_1 = send_piece(1)
    for copy in scatters:
        copy.wait()

    for slot in range(4):
        for n in range(3):
            lanes = slice(n * 512, n * 512 + 512)
            value = part[slot, z, :, lanes].astype(F32)
            for peer in range(3):
                value = value + rs_in[peer, slot, :, lanes].astype(F32)
            for q in range(4):
                stage_t[q, (z + OFFSET[slot] + 4) % 4, :, lanes] = value[8 * q:8 * q + 8]
    for q in range(4):
        stage_b[q] = stage_t[q].reshape(32, CHANNELS).astype(BF)
    my_q = ylo * 2 + core
    seq_copies = []
    for dy in range(2):
        for dk in range(2):
            if (dy, dk) != (0, 0):
                q = ((ylo + dy) % 2) * 2 + (core + dk) % 2
                seq_copies.append(push(stage_b.at[q], seq_in.at[my_q], device(0, dy * yflip, 0, dk)))
    seq_in[my_q] = stage_b[my_q]

    all_y[2].wait()
    sent_2 = send_piece(2)
    far_0 = relay_piece(0, sent_0)
    for copy in seq_copies:
        copy.wait()
    for n in range(3):
        lanes = slice(n * 512, n * 512 + 512)
        tok[0, :, lanes] = dot(seq_ref[...], seq_in[:, :, lanes].reshape(128, 512)).astype(BF)
    for b in range(19):
        if b % 13 == 12:
            ext[:, b * 128:b * 128 + 128] = jnp.where(
                lax.broadcasted_iota(jnp.int32, (128, 128), 1) == 0, 1.0, 0.0
            )
        else:
            lanes = slice((b % 13) * 128, (b % 13) * 128 + 128)
            ext[:, b * 128:b * 128 + 128] = tok[0, :, lanes].astype(F32)
    finish_whole(far_a)

    encoded = tok[0]

    def squares_of(i, total):
        cells = tok[0, :, pl.ds(pl.multiple_of(i * 128, 128), 128)]
        for d in range(7):
            value = dot(cells, mf_a[1 + d, pl.ds(i * 8, 8)].reshape(128, 128))
            turned = ext[:, pl.ds(pl.multiple_of((i + d) * 128, 128), 128)]
            total = total + (1.0 if d == 0 else 2.0) * (value * turned)
        return total

    total = lax.fori_loop(0, BLOCKS, squares_of, jnp.zeros((128, 128), F32))
    for d in range(7):
        weight = mf_a[1 + d, 96].astype(F32)[0:1]
        total = total + (1.0 if d == 0 else 2.0) * weight * ext[:, (12 + d) * 128:(13 + d) * 128]
    squares = jnp.maximum(jnp.sum(total, axis=-1, keepdims=True), 0.0)
    inverse = lax.rsqrt(squares * (1.0 / LANGUAGE_WIDTH) + 1e-06)
    adapter_in = dot(encoded, mf_a[0, 0:96].reshape(CHANNELS, 128)) + mf_a[0, 96].astype(F32)[0:1]
    adapter_in = (inverse * adapter_in).astype(BF)
    weighted = (inverse * adapter_grad).astype(BF)

    def place(group, value):
        ein[group // 80, group % 80 // 5, group % 5] = value

    for n in range(3):
        value = dot_tn(encoded[:, n * 512:n * 512 + 512], weighted).astype(BF).reshape(32, 16, 128)
        for g in range(32):
            place(n * 32 + g, value[g])
    for n in range(16):
        value = dot_tn(adapter_in, grad[:, n * 128:n * 128 + 128])
        value = value[0:64] if n < 8 else value[64:128]
        value = (0.5 * value).astype(BF).reshape(4, 16, 128)
        for g in range(4):
            place(96 + 4 * n + g, value[g])
    shifted = jnp.sum(weighted.astype(F32), axis=0, keepdims=True)
    shifted = jnp.where(lax.broadcasted_iota(jnp.int32, (16, 128), 0) == 0, shifted, 0.0).astype(BF)
    for half in range(2):
        for p in range(16):
            ein[half, p, 5] = shifted
    joined = push(ein.at[1 - core], e_core, other)
    far_3 = relay_piece(3, sent_3)
    joined.wait()

    def sum_cores(p, carry):
        e_mid[p] = (ein[core, p].astype(F32) + e_core[p].astype(F32)).astype(BF)
        return carry

    lax.fori_loop(0, 16, sum_cores, 0)
    sums = []
    for n, (dy, dz) in enumerate(planes):
        target_plane = ((y + dy) % 4) * 4 + (z + dz) % 4
        sums.append(push(e_mid.at[target_plane], e_in1.at[n], device(0, dy, dz, 0)))
    far_1 = relay_piece(1, sent_1)
    finish_piece(0, far_0)
    for copy in sums:
        copy.wait()
    value = e_mid[plane].astype(F32)
    for n in range(15):
        value = value + e_in1[n].astype(F32)
    e_in2[x] = value.astype(BF)
    sums = [push(e_in2.at[x], e_in2.at[x], device(dx, 0, 0, 0)) for dx in (1, 3, 2)]
    far_2 = relay_piece(2, sent_2)
    finish_piece(3, far_3)
    for copy in sums:
        copy.wait()
    value = e_in2[0].astype(F32)
    for n in range(1, 4):
        value = value + e_in2[n].astype(F32)
    value = value.astype(BF)
    mine = e_all.at[pl.ds(core * 80 + plane * 5, 5)]
    mine[...] = value[0:5]
    total_shift = value[5].astype(F32)[0:1]
    sums = [push(mine, mine, device(0, dy, dz, 0)) for dy, dz in planes]
    finish_piece(1, far_1)
    for copy in b_bias:
        copy.wait()
    for owner in (pair, x_prev, x_next, x_far):
        m_core.append(push(mf_b.at[owner, 96], mf_b.at[owner, 96], other))
    finish_piece(2, far_2)
    for copy in sums:
        copy.wait()
    mine = e_all.at[pl.ds(core * 80, 80)]
    joined = push(mine, mine, other)
    for copy in m_core:
        copy.wait()

    for n in range(8):
        lanes = slice(n * 256, n * 256 + 256)
        value = dot(encoded, mf_b[n, 0:96].reshape(CHANNELS, 256)) + mf_b[n, 96].astype(F32)[0:1]
        value = inverse * value + (kvb_ref[0:1, lanes] + dot(adapter_in, up_ref[:, lanes]))
        if n < 4:
            for h in range(2):
                head = value[:, h * 128:h * 128 + 128]
                turned = head * cosine + pltpu.roll(head, 64, 1) * sine
                kv_ref[:, n * 256 + h * 128:n * 256 + h * 128 + 128] = turned.astype(BF)
        else:
            kv_ref[:, lanes] = value.astype(BF)
    joined.wait()
    down = dot(pt_ref[:, 0:CHANNELS], e_all[0:96].reshape(CHANNELS, 128))
    down_ref[...] = (down + bias * total_shift) * gain
    for n in range(16):
        lanes = slice((n % 8) * 128, (n % 8) * 128 + 128)
        upg_ref[n // 8, :, lanes] = e_all[96 + 4 * n:100 + 4 * n].reshape(64, 128).astype(F32)


def orders():
    tile = [[0.0] * 128 for _ in range(128)]
    seq = [[0.0] * 128 for _ in range(128)]
    for w in range(4):
        for h in range(8):
            for i in range(4):
                tile[(h % 4) * 32 + (h // 4) * 16 + (i // 2) * 8 + w * 2 + i % 2][w * 32 + h * 4 + i] = 1.0
    for ys in range(2):
        for cs in range(2):
            for zs in range(4):
                for w in range(4):
                    for i in range(2):
                        here = (ys * 2 + cs) * 32 + zs * 8 + w * 2 + i
                        seq[i * 64 + ys * 32 + zs * 8 + cs * 4 + w][here] = 1.0
    return jnp.array(tile, BF), jnp.array(seq, BF)


def local(
    feature_grid, depthwise_kernel, depthwise_bias, layer_norm_gain, layer_norm_shift,
    expansion_weight, expansion_bias, reduction_weight, reduction_bias, layer_branch_scale,
    projector_weight, projector_bias, input_norm_gain, key_value_weight, key_value_bias,
    adapter_down_weight, adapter_up_weight, image_start_positions, key_value_cotangent,
):
    cells = feature_grid.transpose(2, 0, 1, 3).reshape(4, 32, CHANNELS)
    freq = np.exp(np.arange(HEAD_DIM // 2, dtype=np.float32) * np.float32(-2.0 * math.log(ROPE_THETA) / HEAD_DIM))
    freq = jnp.array(np.concatenate([freq, freq])[None, :], F32)
    tile_order, seq_order = orders()
    vmem = pl.BlockSpec(memory_space=pltpu.VMEM)
    kv, down, upg = pl.pallas_call(
        kernel,
        out_shape=(
            jax.ShapeDtypeStruct((128, 2048), BF),
            jax.ShapeDtypeStruct((64, 128), F32),
            jax.ShapeDtypeStruct((2, 64, 1024), F32),
        ),
        in_specs=[vmem] * 5 + [pl.BlockSpec(memory_space=pl.ANY)] * 2 + [vmem] * 10 + [pl.BlockSpec(memory_space=pltpu.SMEM)] + [vmem] * 4,
        out_specs=(vmem, vmem, vmem),
        scratch_shapes=[
            pltpu.VMEM((10, 64, CHANNELS), BF),
            pltpu.VMEM((4, 32, CHANNELS), F32),
            pltpu.VMEM((4, 128, CHANNELS), BF),
            pltpu.VMEM((4, CHANNELS, 384), BF),
            pltpu.VMEM((4, 384, CHANNELS), BF),
            pltpu.VMEM((4, 1, 384), F32),
            pltpu.VMEM((128, CHANNELS), F32),
            pltpu.VMEM((256, CHANNELS), F32),
            pltpu.VMEM((4, 4, 32, CHANNELS), BF),
            pltpu.VMEM((3, 4, 32, CHANNELS), BF),
            pltpu.VMEM((4, 4, 8, CHANNELS), F32),
            pltpu.VMEM((4, 32, CHANNELS), BF),
            pltpu.VMEM((4, 32, CHANNELS), BF),
            pltpu.VMEM((8, 64, 2048), BF),
            pltpu.VMEM((5, 12, 2, 16, 128), BF),
            pltpu.VMEM((3, 4, 3, 2, 16, 128), BF),
            pltpu.VMEM((4, 3, 2, 16, 128), BF),
            pltpu.VMEM((3, 3, 2, 16, 128), BF),
            pltpu.VMEM((7, 16, 128), BF),
            pltpu.VMEM((8, 97, 16, 128), BF),
            pltpu.VMEM((5, 12, 2, 16, 256), BF),
            pltpu.VMEM((3, 12, 2, 16, 256), BF),
            pltpu.VMEM((12, 2, 16, 256), BF),
            pltpu.VMEM((3, 3, 2, 16, 256), BF),
            pltpu.VMEM((7, 16, 256), BF),
            pltpu.VMEM((8, 97, 16, 256), BF),
            pltpu.VMEM((128, 19 * 128), F32),
            pltpu.VMEM((128, 2048), BF),
            pltpu.VMEM((2, 16, 6, 16, 128), BF),
            pltpu.VMEM((16, 6, 16, 128), BF),
            pltpu.VMEM((16, 6, 16, 128), BF),
            pltpu.VMEM((15, 6, 16, 128), BF),
            pltpu.VMEM((4, 6, 16, 128), BF),
            pltpu.VMEM((160, 16, 128), BF),
            pltpu.VMEM((64, EXT), BF),
            pltpu.VMEM((8, 64, 384), BF),
            pltpu.VMEM((128, 2048), BF),
            pltpu.VMEM((7, 8, CHANNELS), F32),
            pltpu.VMEM((128, 128), F32),
            pltpu.VMEM((128, 128), F32),
            pltpu.VMEM((1, 384), F32),
            pltpu.SemaphoreType.DMA((COPIES,)),
            pltpu.SemaphoreType.DMA((COPIES,)),
            pltpu.SemaphoreType.DMA((6,)),
        ],
        compiler_params=pltpu.CompilerParams(
            collective_id=0, has_side_effects=True, vmem_limit_bytes=62 << 20
        ),
        cost_estimate=pl.CostEstimate(flops=8_000_000_000, bytes_accessed=30_000_000, transcendentals=0),
    )(
        cells, depthwise_kernel, depthwise_bias, layer_norm_gain, layer_norm_shift,
        expansion_weight, reduction_weight, expansion_bias, reduction_bias,
        layer_branch_scale, projector_weight.T, projector_bias[None, :], input_norm_gain[None, :],
        key_value_weight, key_value_bias[None, :], adapter_down_weight, adapter_up_weight,
        image_start_positions, key_value_cotangent.reshape(128, 2048), freq, tile_order, seq_order,
    )
    return kv.reshape(2, 64, 2048), down, upg


def solution(mesh):
    in_specs = (
        P("row", None, "col", None), P(), P(), P(), P(),
        P(None, "col"), P("col"), P("col", None), P(), P(),
        P(None, ("row", "col")), P(("row", "col")), P(("row", "col")), P(("row", "col"), None), P(),
        P(("row", "col"), None), P(), P(), P(("row", "col"), None, None),
    )
    out_specs = (P(("row", "col"), None, None), P(("row", "col"), None), P())
    return jax.shard_map(local, mesh=mesh, in_specs=in_specs, out_specs=out_specs, check_vma=False)
```

```python
import functools
import math

import jax
import jax.numpy as jnp
import numpy as np
from jax import lax
from jax.experimental import pallas as pl
from jax.experimental.pallas import tpu as pltpu
from jax.sharding import PartitionSpec as P

LANGUAGE_WIDTH = 8192
HEAD_DIM = 128
IMAGES = 4
CHANNELS = 1536
BLOCKS = 12
EXT = 1664
ROPE_THETA = 1000000.0
MESH = pl.DeviceIdType.MESH
BF = jnp.bfloat16
F32 = jnp.float32
COPIES = 240
SLOT_OF = {0: 0, 3: 1, 1: 2, 2: 3}
OFFSET = (0, -1, 1, 2)


def dot(a, b):
    return jnp.dot(a, b, preferred_element_type=F32)


def dot_tn(a, b):
    return lax.dot_general(a, b, (((0,), (0,)), ((), ())), preferred_element_type=F32)


def dot_nt(a, b):
    return lax.dot_general(a, b, (((1,), (1,)), ((), ())), preferred_element_type=F32)


def kernel(
    x_hbm, depth_hbm, dbias_hbm, lgain_hbm, lshift_hbm, w1_hbm, w2_hbm, b1_hbm, rbias_hbm, scale_hbm, proj_hbm, pbias_hbm, ngain_hbm, kvw_hbm, kvb_hbm, downw_hbm, upw_hbm, start_ref, cot_hbm, freq_hbm, perm_hbm,
    kv_hbm, down_hbm, upg_hbm,
    pad, conv, tok, wa, wb, ba, feat, acc, part, rs_in, stage_t, stage_b, seq_in,
    pb, quad_a, red_z_a, red_mid_a, red_y_a, red_bias_a, mf_a,
    quad_b, red_z_b, red_mid_b, red_y_b, red_bias_b, mf_b, ext, grad,
    ein, e_core, e_mid, e_in1, e_in2, e_all, pt_ref, gb_ref, gb_in, up_ref, taps_ref, cos_ref, sin_ref, own_b1,
    kv_ref, down_ref, upg_ref, x_ref, depth_ref, dbias_ref, lgain_ref, lshift_ref, b1_ref, rbias_ref, scale_ref, proj_ref, pbias_ref, ngain_ref, kvw_ref, kvb_ref, downw_ref, upw_ref, cot_ref, freq_ref, perm_ref,
    send, recv, lsem,
):
    ids = [0, 0]
    loads = {}

    def load(name, source, target):
        loads[name] = pltpu.make_async_copy(source, target, lsem.at[ids[1]])
        ids[1] += 1
        loads[name].start()

    load("proj", proj_hbm, proj_ref)
    load("pbias", pbias_hbm, pbias_ref)
    load("ngain", ngain_hbm, ngain_ref)
    load("kvw", kvw_hbm, kvw_ref)
    load("downw", downw_hbm, downw_ref)
    load("b1", b1_hbm, b1_ref)
    load("x", x_hbm, x_ref)
    load("depth", depth_hbm, depth_ref)
    load("dbias", dbias_hbm, dbias_ref)
    load("lgain", lgain_hbm, lgain_ref)
    load("lshift", lshift_hbm, lshift_ref)
    load("rbias", rbias_hbm, rbias_ref)
    load("scale", scale_hbm, scale_ref)
    load("kvb", kvb_hbm, kvb_ref)
    load("upw", upw_hbm, upw_ref)
    load("cot", cot_hbm, cot_ref)
    load("freq", freq_hbm, freq_ref)
    load("perm", perm_hbm, perm_ref)
    row = lax.axis_index("row")
    col = lax.axis_index("col")
    x = row // 2
    y = (row % 2) * 2 + col // 8
    z = (col % 8) // 2
    core = col % 2
    ylo = y % 2
    plane = y * 4 + z
    pair = x * 2 + core

    def device(dx, dy, dz, dk):
        xx, yy, zz, kk = (x + dx + 4) % 4, (y + dy + 4) % 4, (z + dz + 4) % 4, (core + dk) % 2
        return (xx * 2 + yy // 2, (yy % 2) * 8 + zz * 2 + kk)


    def push(src, dst, target):
        n = ids[0]
        ids[0] += 1
        copy = pltpu.make_async_remote_copy(
            src_ref=src, dst_ref=dst, send_sem=send.at[n], recv_sem=recv.at[n],
            device_id=target, device_id_type=MESH,
        )
        copy.start()
        return copy

    planes = [(dy, dz) for dy in range(4) for dz in range(4) if (dy, dz) != (0, 0)]
    up_dev = ((row + 7) % 8, col)
    dn_dev = ((row + 1) % 8, col)
    lt_dev = (row, (col + 15) % 16)
    rt_dev = (row, (col + 1) % 16)
    other = device(0, 0, 0, 1)
    yflip = 1 - 2 * ylo

    partners = [up_dev, dn_dev, lt_dev, rt_dev, other]
    for step in (1, 2, 3):
        partners += [device(step, 0, 0, 0), device(0, step, 0, 0), device(0, 0, step, 0)]
    barrier = pltpu.get_barrier_semaphore()
    for partner in partners:
        pl.semaphore_signal(barrier, inc=1, device_id=partner, device_id_type=MESH)
    for name in ("proj", "pbias", "ngain", "kvw", "downw", "b1"):
        loads.pop(name).wait()
    diagonal = lax.broadcasted_iota(jnp.int32, (64, 64), 0) == lax.broadcasted_iota(jnp.int32, (64, 64), 1)
    gain = jnp.sum(jnp.where(diagonal, ngain_ref[...].astype(F32), 0.0), axis=1, keepdims=True)
    bias = jnp.sum(jnp.where(diagonal, pbias_ref[...].astype(F32), 0.0), axis=1, keepdims=True)
    pt_ref[:, 0:CHANNELS] = proj_ref[...]
    own_b1[...] = b1_ref[...].reshape(1, 384)
    first_lane = lax.broadcasted_iota(jnp.int32, (64, 128), 1) == 0
    pt_ref[:, CHANNELS:EXT] = jnp.where(first_lane, bias, 0.0).astype(BF)
    for j in range(8):
        gb_ref[j, :, 128:384] = (kvw_ref[:, j * 256:j * 256 + 256].astype(F32) * gain).astype(BF)
    gb_ref[0, :, 0:128] = (downw_ref[...].astype(F32) * gain).astype(BF)
    gb_ref[1:8, :, 0:128] = jnp.zeros((7, 64, 128), BF)
    copies0 = [
        pltpu.make_async_copy(x_hbm, pad.at[3:7, 16:48], lsem.at[20]),
        pltpu.make_async_copy(w1_hbm, wa.at[0], lsem.at[21]),
        pltpu.make_async_copy(w2_hbm, wb.at[0], lsem.at[22]),
        pltpu.make_async_copy(own_b1, ba.at[0], lsem.at[23]),
        pltpu.make_async_copy(pt_ref, pb.at[0, :, 0:EXT], lsem.at[24]),
        pltpu.make_async_copy(gb_ref.at[pair], pb.at[0, :, EXT:2048], lsem.at[25]),
    ]
    for copy in copies0:
        copy.start()
    pl.semaphore_wait(barrier, len(partners))

    h_up = push(x_hbm.at[:, 0:16], pad.at[3:7, 48:64], up_dev)
    h_dn = push(x_hbm.at[:, 16:32], pad.at[3:7, 0:16], dn_dev)
    h_rt = push(x_hbm.at[1:4], pad.at[0:3, 16:48], rt_dev)
    h_lt = push(x_hbm.at[0:3], pad.at[7:10, 16:48], lt_dev)
    gb_copies = []
    pt_copies = []
    for dx in (1, 3, 2):
        pt_copies.append(push(pt_ref, pb.at[2 * dx, :, 0:EXT], device(dx, 0, 0, 0)))
    for dx in (1, 3, 2):
        target_x = ((x + dx) % 4) * 2
        target = device(dx, 0, 0, 0)
        gb_copies.append(push(gb_ref.at[target_x + core], pb.at[2 * dx, :, EXT:2048], target))
        gb_copies.append(push(gb_ref.at[target_x + 1 - core], gb_in.at[dx - 1], target))
    fwd_copies = [
        push(pt_ref, pb.at[1, :, 0:EXT], other),
        push(gb_ref.at[x * 2 + 1 - core], pb.at[1, :, EXT:2048], other),
    ]
    w_core = [
        push(w1_hbm, wa.at[1], other), push(w2_hbm, wb.at[1], other), push(own_b1, ba.at[1], other),
    ]
    x_half = x % 2

    def w1_rows(half, part_of, count):
        return pl.ds(pl.multiple_of(half * 768 + part_of * 384, 16), count)

    def w2_rows(half, part_of, count):
        return pl.ds(pl.multiple_of(half * 192 + part_of * 96, 16), count)

    w_y = []
    for n in range(2):
        rows1, rows2 = w1_rows(x_half, n, 384), w2_rows(x_half, n, 96)
        w_y.append([
            push(w1_hbm.at[rows1], wa.at[2, rows1], device(0, 1, 0, 0)),
            push(w2_hbm.at[rows2], wb.at[2, rows2], device(0, 3, 0, 0)),
        ])
    w_y[0].append(push(own_b1, ba.at[2], device(0, 1, 0, 0)))

    w_x = []

    def share_w(n):
        for copy in w_y[n]:
            copy.wait()
        rows1, rows2 = w1_rows(x_half, n, 384), w2_rows(x_half, n, 96)
        w_x.append(push(wa.at[2, rows1], wa.at[2, rows1], device(1, 0, 0, 0)))
        w_x.append(push(wb.at[2, rows2], wb.at[2, rows2], device(3, 0, 0, 0)))

    for name in list(loads):
        loads.pop(name).wait()
    token = lax.broadcasted_iota(jnp.int32, (128, 128), 0)
    later = token >= 64
    start = jnp.where(later, start_ref[core * 2 + 1], start_ref[core * 2])
    position = start + (row * 8 + col // 2) * 64 + jnp.where(later, token - 64, token)
    angle = position.astype(F32) * freq_ref[...]
    cos_ref[...] = jnp.cos(angle)
    upper = lax.broadcasted_iota(jnp.int32, (128, 128), 1) >= 64
    sin_ref[...] = jnp.where(upper, 1.0, -1.0) * jnp.sin(angle)
    up_ref[...] = jnp.zeros((128, 2048), BF)
    up_ref[0:64, 0:1024] = (upw_ref[0].astype(F32) * 0.5).astype(BF)
    up_ref[64:128, 1024:2048] = (upw_ref[1].astype(F32) * 0.5).astype(BF)
    for a in range(7):
        taps_ref[a, 0:7, :] = depth_ref[a].astype(F32)
    cosine = cos_ref[...]
    sine = sin_ref[...]
    for head in range(8):
        lanes = slice(head * 128, head * 128 + 128)
        value = cot_ref[:, lanes].astype(F32)
        grad[:, lanes] = (value * cosine - pltpu.roll(value, 64, 1) * sine).astype(BF)
    grad[:, 1024:2048] = cot_ref[:, 1024:2048]
    adapter_grad = dot_nt(grad[...], up_ref[...]).astype(BF).astype(F32)
    for copy in copies0:
        copy.wait()
    for n in range(3):
        lanes = slice(n * 512, n * 512 + 512)
        feat[:, lanes] = dot(perm_ref[0], x_ref[:, :, lanes].reshape(128, 512))

    h_up.wait()
    h_dn.wait()

    @pl.when(row == 0)
    def _():
        pad[3:7, 0:16] = jnp.zeros((4, 16, CHANNELS), BF)

    @pl.when(row == 7)
    def _():
        pad[3:7, 48:64] = jnp.zeros((4, 16, CHANNELS), BF)

    corners = [
        push(pad.at[4:7, 0:16], pad.at[0:3, 0:16], rt_dev),
        push(pad.at[4:7, 48:64], pad.at[0:3, 48:64], rt_dev),
        push(pad.at[3:6, 0:16], pad.at[7:10, 0:16], lt_dev),
        push(pad.at[3:6, 48:64], pad.at[7:10, 48:64], lt_dev),
    ]

    for n, dx in enumerate((1, 3, 2)):
        pt_copies[n].wait()
        fwd_copies.append(push(pb.at[2 * dx, :, 0:EXT], pb.at[2 * dx + 1, :, 0:EXT], other))
        gb_copies[2 * n].wait()
        gb_copies[2 * n + 1].wait()
        fwd_copies.append(push(gb_in.at[dx - 1], pb.at[2 * dx + 1, :, EXT:2048], other))
    for copy in fwd_copies:
        copy.wait()

    def products(quad, width, first):
        def body(i, carry):
            left = pb[:, :, pl.ds(pl.multiple_of(i * 128, 128), 128)].reshape(512, 128)
            if first:
                shift = i + pair - 1
                around = jnp.where(shift >= 13, shift - 13, shift)
                start = pl.multiple_of(jnp.where(pair == 0, 13, around) * 128, 128)
            else:
                start = EXT + 128
            right = pb[:, :, pl.ds(start, width)].reshape(512, width)
            value = dot_tn(left, right).astype(BF).reshape(4, 2, 16, width)
            for r in range(4):
                p = i * 4 + r
                quad[p // 12, p % 12] = value[r]
            return carry

        lax.fori_loop(0, 13, body, 0)

    class Chain:
        def __init__(self, first, quad, red_1, red_mid, red_2, red_bias, mf):
            self.quad, self.red_1, self.red_mid = quad, red_1, red_mid
            self.red_2, self.red_bias, self.mf = red_2, red_bias, mf
            self.first = first
            self.third = lambda n: pl.ds(((z + n) % 4) * 3, 3)

        def toward(self, axis, n):
            return device(0, n, 0, 0) if axis == 1 else device(0, 0, n, 0)

        def start(self):
            self.copies = []
            for n, step in enumerate((1, 3, 2)):
                target = self.toward(self.first, step)
                if self.first == 2:
                    block = self.quad.at[0:4, self.third(step)]
                else:
                    block = self.quad.at[(y + step) % 4]
                self.copies.append(push(block, self.red_1.at[n], target))
                self.copies.append(push(self.quad.at[4, 0, 0], self.red_bias.at[n], target))

        def middle(self):
            for copy in self.copies:
                copy.wait()

            def body(n, carry):
                if self.first == 2:
                    own, place = (n // 3, z * 3 + n % 3), (n // 3, n % 3)
                else:
                    own, place = (y, n), (n,)
                total = self.quad[own].astype(F32)
                for m in range(3):
                    total = total + self.red_1[(m,) + place].astype(F32)
                self.red_mid[place] = total.astype(BF)
                return carry

            lax.fori_loop(0, 12, body, 0)
            total = self.quad[4, 0, 0].astype(F32)
            for m in range(3):
                total = total + self.red_bias[m].astype(F32)
            self.red_bias[6] = total.astype(BF)
            self.copies = []
            for n, step in enumerate((1, 3, 2)):
                target = self.toward(3 - self.first, step)
                if self.first == 2:
                    block = self.red_mid.at[(y + step) % 4]
                else:
                    block = self.red_mid.at[self.third(step)]
                self.copies.append(push(block, self.red_2.at[n], target))
                self.copies.append(push(self.red_bias.at[6], self.red_bias.at[3 + n], target))

        def spread(self):
            for copy in self.copies:
                copy.wait()

            def body(p, carry):
                own = (y, p) if self.first == 2 else (z * 3 + p,)
                total = self.red_mid[own].astype(F32)
                for m in range(3):
                    total = total + self.red_2[m, p].astype(F32)
                self.mf[pair, pl.ds(plane * 6 + p * 2, 2)] = total.astype(BF)
                return carry

            lax.fori_loop(0, 3, body, 0)
            total = self.red_bias[6].astype(F32)
            for m in range(3):
                total = total + self.red_bias[3 + m].astype(F32)
            self.mf[pair, 96] = total.astype(BF)
            block = self.mf.at[pair, pl.ds(plane * 6, 6)]
            self.copies = [push(block, block, device(0, 0, dz, 0)) for dz in (1, 3, 2)]

        def fan(self):
            for copy in self.copies:
                copy.wait()
            block = self.piece(pair, 0)
            self.copies = [push(block, block, device(0, dy, 0, 0)) for dy in (1, 3, 2)]

        def piece(self, owner, dy, low=0, count=24):
            return self.mf.at[owner, pl.ds(((y + dy) % 4) * 24 + low, count)]

    chain_a = Chain(2, quad_a, red_z_a, red_mid_a, red_y_a, red_bias_a, mf_a)
    chain_b = Chain(1, quad_b, red_z_b, red_mid_b, red_y_b, red_bias_b, mf_b)
    x_prev = ((x + 3) % 4) * 2 + core
    x_next = ((x + 1) % 4) * 2 + core
    x_far = ((x + 2) % 4) * 2 + core
    m_core = []

    def send_whole():
        for copy in chain_a.copies:
            copy.wait()
        whole = mf_a.at[pair]
        sent = [push(whole, whole, device(1, 0, 0, 0)), push(whole, whole, device(3, 0, 0, 0))]
        m_core.append(push(whole, whole, other))
        return sent

    def relay_whole(sent):
        sent[0].wait()
        low, high = mf_a.at[x_prev, 0:48], mf_a.at[x_next, 48:97]
        far = [push(low, low, device(1, 0, 0, 0))]
        m_core.append(push(mf_a.at[x_prev], mf_a.at[x_prev], other))
        sent[1].wait()
        far.append(push(high, high, device(3, 0, 0, 0)))
        m_core.append(push(mf_a.at[x_next], mf_a.at[x_next], other))
        return far

    def finish_whole(far):
        for copy in far:
            copy.wait()
        push(mf_a.at[x_far], mf_a.at[x_far], other).wait()
        for copy in m_core:
            copy.wait()
        del m_core[:]

    piece = chain_b.piece

    def send_piece(dy):
        block = piece(pair, dy)
        sent = [push(block, block, device(1, 0, 0, 0)), push(block, block, device(3, 0, 0, 0))]
        m_core.append(push(block, block, other))
        return sent

    def relay_piece(dy, sent):
        sent[0].wait()
        low, high = piece(x_prev, dy, 0, 12), piece(x_next, dy, 12, 12)
        far = [push(low, low, device(1, 0, 0, 0))]
        m_core.append(push(piece(x_prev, dy), piece(x_prev, dy), other))
        sent[1].wait()
        far.append(push(high, high, device(3, 0, 0, 0)))
        m_core.append(push(piece(x_next, dy), piece(x_next, dy), other))
        return far

    def finish_piece(dy, far):
        far[0].wait()
        far[1].wait()
        m_core.append(push(piece(x_far, dy), piece(x_far, dy), other))

    products(quad_a, 128, True)
    chain_a.start()
    share_w(0)
    h_rt.wait()
    h_lt.wait()
    for copy in corners:
        copy.wait()

    @pl.when(col == 0)
    def _():
        pad[0:3] = jnp.zeros((3, 64, CHANNELS), BF)

    @pl.when(col == 15)
    def _():
        pad[7:10] = jnp.zeros((3, 64, CHANNELS), BF)

    def conv_lanes(n, carry):
        lanes = pl.ds(pl.multiple_of(n * 128, 128), 128)
        sums = [jnp.zeros((32, 128), F32) + dbias_ref[lanes].reshape(1, 128) for _ in range(4)]
        for wp in range(10):
            full = pad[wp, :, lanes].astype(F32)
            moved = pltpu.roll(full, 60, 0)
            for a in range(7):
                start = 4 * (a + 1)
                window = full[start:start + 32] if a % 2 else moved[start - 4:start + 28]
                for w in range(max(0, wp - 6), min(3, wp) + 1):
                    sums[w] = sums[w] + window * taps_ref[a, wp - w:wp - w + 1, lanes]
        for w in range(4):
            conv[w, :, lanes] = sums[w]
        return carry

    lax.fori_loop(0, BLOCKS, conv_lanes, 0)

    def norm_rows(n, carry):
        w = n // 2
        rows = pl.ds(pl.multiple_of((n % 2) * 16, 16), 16)
        value = conv[w, rows, :]
        center = jnp.sum(value, axis=-1, keepdims=True) * (1.0 / CHANNELS)
        centered = value - center
        variance = jnp.sum(centered * centered, axis=-1, keepdims=True) * (1.0 / CHANNELS)
        value = centered * lax.rsqrt(variance + 1e-06) * lgain_ref[...].reshape(1, CHANNELS) + lshift_ref[...].reshape(1, CHANNELS)
        part[0, w, rows, :] = value.astype(BF)
        return carry

    lax.fori_loop(0, 8, norm_rows, 0)
    for n in range(3):
        lanes = slice(n * 512, n * 512 + 512)
        tok[0, :, lanes] = dot(perm_ref[0], part[0, :, :, lanes].reshape(128, 512)).astype(BF)
    t_next = push(tok.at[0], tok.at[1], device(0, 0, 1, 0))
    t_prev = push(tok.at[0], tok.at[2], device(0, 0, 3, 0))

    share_w(1)
    products(quad_b, 256, False)
    chain_b.start()
    chain_a.middle()
    def mlp(slot, count, weights, first):
        rows = 128 * count
        tokens = tok[slot:slot + count].reshape(rows, CHANNELS)
        for index, s in enumerate(weights):
            pre = dot(tokens, wa[s]) + ba[s]
            hidden = (0.5 * pre * (1.0 + lax.erf(pre * (0.5 ** 0.5)))).astype(BF)
            for n in range(3):
                lanes = slice(n * 512, n * 512 + 512)
                term = dot(hidden, wb[s, :, lanes])
                if first and index == 0:
                    acc[0:rows, lanes] = term
                else:
                    acc[0:rows, lanes] += term

    def scatter(slot):
        sent = []
        for tau in (1, 3, 2):
            into = SLOT_OF[(OFFSET[slot] - tau) % 4]
            peer = SLOT_OF[(-tau) % 4] - 1
            sent.append(
                push(part.at[slot, (z + tau) % 4], rs_in.at[peer, into], device(0, 0, tau, 0))
            )
        return sent

    scale = scale_ref[...].reshape(1, CHANNELS)
    mlp(0, 1, (0,), True)
    for copy in w_core:
        copy.wait()
    mlp(0, 1, (1,), False)

    chain_a.spread()
    own_half = [(wa, w1_rows(x_half, 0, 768)), (wb, w2_rows(x_half, 0, 192))]
    their_half = [(wa, w1_rows(1 - x_half, 0, 768)), (wb, w2_rows(1 - x_half, 0, 192))]
    w_fwd = [push(ref.at[2, rows], ref.at[3, rows], other) for ref, rows in own_half]
    w_fwd.append(push(ba.at[2], ba.at[3], other))
    chain_a.fan()
    t_next.wait()
    t_far0 = push(tok.at[1, 0:64], tok.at[3, 0:64], device(0, 0, 1, 0))
    t_prev.wait()
    t_far1 = push(tok.at[2, 64:128], tok.at[3, 64:128], device(0, 0, 3, 0))
    for copy in w_x:
        copy.wait()
    w_fwd += [push(ref.at[2, rows], ref.at[3, rows], other) for ref, rows in their_half]
    mlp(0, 1, (2,), False)
    chain_b.middle()
    for copy in w_fwd:
        copy.wait()
    mlp(0, 1, (3,), False)
    part[0] = (acc[0:128, :] * scale + (feat[...] + scale * rbias_ref[...].reshape(1, CHANNELS))).astype(BF).reshape(4, 32, CHANNELS)
    scatters = scatter(0)
    sent_a = send_whole()
    chain_b.spread()
    mlp(1, 2, (0, 1, 2, 3), True)
    for slot in (1, 2):
        part[slot] = (acc[128 * slot - 128:128 * slot, :] * scale).astype(BF).reshape(4, 32, CHANNELS)
        scatters += scatter(slot)
    chain_b.fan()
    b_bias = [push(mf_b.at[pair, 96], mf_b.at[pair, 96], device(dx, 0, 0, 0)) for dx in (1, 3, 2)]
    t_far0.wait()
    t_far1.wait()
    mlp(3, 1, (0, 1, 2, 3), True)
    part[3] = (acc[0:128, :] * scale).astype(BF).reshape(4, 32, CHANNELS)
    scatters += scatter(3)
    far_a = relay_whole(sent_a)
    sent_0 = send_piece(0)
    all_y = chain_b.copies
    all_y[0].wait()
    sent_3 = send_piece(3)
    all_y[1].wait()
    sent_1 = send_piece(1)
    for copy in scatters:
        copy.wait()

    for slot in range(4):
        for n in range(3):
            lanes = slice(n * 512, n * 512 + 512)
            value = part[slot, z, :, lanes].astype(F32)
            for peer in range(3):
                value = value + rs_in[peer, slot, :, lanes].astype(F32)
            for q in range(4):
                stage_t[q, (z + OFFSET[slot] + 4) % 4, :, lanes] = value[8 * q:8 * q + 8]
    for q in range(4):
        stage_b[q] = stage_t[q].reshape(32, CHANNELS).astype(BF)
    my_q = ylo * 2 + core
    seq_copies = []
    for dy in range(2):
        for dk in range(2):
            if (dy, dk) != (0, 0):
                q = ((ylo + dy) % 2) * 2 + (core + dk) % 2
                seq_copies.append(push(stage_b.at[q], seq_in.at[my_q], device(0, dy * yflip, 0, dk)))
    seq_in[my_q] = stage_b[my_q]

    all_y[2].wait()
    sent_2 = send_piece(2)
    far_0 = relay_piece(0, sent_0)
    for copy in seq_copies:
        copy.wait()
    for n in range(3):
        lanes = slice(n * 512, n * 512 + 512)
        tok[0, :, lanes] = dot(perm_ref[1], seq_in[:, :, lanes].reshape(128, 512)).astype(BF)
    for b in range(19):
        if b % 13 == 12:
            ext[:, b * 128:b * 128 + 128] = jnp.where(
                lax.broadcasted_iota(jnp.int32, (128, 128), 1) == 0, 1.0, 0.0
            )
        else:
            lanes = slice((b % 13) * 128, (b % 13) * 128 + 128)
            ext[:, b * 128:b * 128 + 128] = tok[0, :, lanes].astype(F32)
    finish_whole(far_a)

    encoded = tok[0]

    def squares_of(i, total):
        cells = tok[0, :, pl.ds(pl.multiple_of(i * 128, 128), 128)]
        for d in range(7):
            value = dot(cells, mf_a[1 + d, pl.ds(i * 8, 8)].reshape(128, 128))
            turned = ext[:, pl.ds(pl.multiple_of((i + d) * 128, 128), 128)]
            total = total + (1.0 if d == 0 else 2.0) * (value * turned)
        return total

    total = lax.fori_loop(0, BLOCKS, squares_of, jnp.zeros((128, 128), F32))
    for d in range(7):
        weight = mf_a[1 + d, 96].astype(F32)[0:1]
        total = total + (1.0 if d == 0 else 2.0) * weight * ext[:, (12 + d) * 128:(13 + d) * 128]
    squares = jnp.maximum(jnp.sum(total, axis=-1, keepdims=True), 0.0)
    inverse = lax.rsqrt(squares * (1.0 / LANGUAGE_WIDTH) + 1e-06)
    adapter_in = dot(encoded, mf_a[0, 0:96].reshape(CHANNELS, 128)) + mf_a[0, 96].astype(F32)[0:1]
    adapter_in = (inverse * adapter_in).astype(BF)
    weighted = (inverse * adapter_grad).astype(BF)

    def place(group, value):
        ein[group // 80, group % 80 // 5, group % 5] = value

    for n in range(3):
        value = dot_tn(encoded[:, n * 512:n * 512 + 512], weighted).astype(BF).reshape(32, 16, 128)
        for g in range(32):
            place(n * 32 + g, value[g])
    for n in range(16):
        value = dot_tn(adapter_in, grad[:, n * 128:n * 128 + 128])
        value = value[0:64] if n < 8 else value[64:128]
        value = (0.5 * value).astype(BF).reshape(4, 16, 128)
        for g in range(4):
            place(96 + 4 * n + g, value[g])
    shifted = jnp.sum(weighted.astype(F32), axis=0, keepdims=True)
    shifted = jnp.where(lax.broadcasted_iota(jnp.int32, (16, 128), 0) == 0, shifted, 0.0).astype(BF)
    for half in range(2):
        for p in range(16):
            ein[half, p, 5] = shifted
    joined = push(ein.at[1 - core], e_core, other)
    far_3 = relay_piece(3, sent_3)
    joined.wait()

    def sum_cores(p, carry):
        e_mid[p] = (ein[core, p].astype(F32) + e_core[p].astype(F32)).astype(BF)
        return carry

    lax.fori_loop(0, 16, sum_cores, 0)
    sums = []
    for n, (dy, dz) in enumerate(planes):
        target_plane = ((y + dy) % 4) * 4 + (z + dz) % 4
        sums.append(push(e_mid.at[target_plane], e_in1.at[n], device(0, dy, dz, 0)))
    far_1 = relay_piece(1, sent_1)
    finish_piece(0, far_0)
    for copy in sums:
        copy.wait()
    value = e_mid[plane].astype(F32)
    for n in range(15):
        value = value + e_in1[n].astype(F32)
    e_in2[x] = value.astype(BF)
    sums = [push(e_in2.at[x], e_in2.at[x], device(dx, 0, 0, 0)) for dx in (1, 3, 2)]
    far_2 = relay_piece(2, sent_2)
    finish_piece(3, far_3)
    for copy in sums:
        copy.wait()
    value = e_in2[0].astype(F32)
    for n in range(1, 4):
        value = value + e_in2[n].astype(F32)
    value = value.astype(BF)
    mine = e_all.at[pl.ds(core * 80 + plane * 5, 5)]
    mine[...] = value[0:5]
    total_shift = value[5].astype(F32)[0:1]
    sums = [push(mine, mine, device(0, dy, dz, 0)) for dy, dz in planes]
    finish_piece(1, far_1)
    for copy in b_bias:
        copy.wait()
    for owner in (pair, x_prev, x_next, x_far):
        m_core.append(push(mf_b.at[owner, 96], mf_b.at[owner, 96], other))
    finish_piece(2, far_2)
    for copy in sums:
        copy.wait()
    mine = e_all.at[pl.ds(core * 80, 80)]
    joined = push(mine, mine, other)
    for copy in m_core:
        copy.wait()

    for n in range(8):
        lanes = slice(n * 256, n * 256 + 256)
        value = dot(encoded, mf_b[n, 0:96].reshape(CHANNELS, 256)) + mf_b[n, 96].astype(F32)[0:1]
        value = inverse * value + (kvb_ref[0:1, lanes] + dot(adapter_in, up_ref[:, lanes]))
        if n < 4:
            for h in range(2):
                head = value[:, h * 128:h * 128 + 128]
                turned = head * cosine + pltpu.roll(head, 64, 1) * sine
                kv_ref[:, n * 256 + h * 128:n * 256 + h * 128 + 128] = turned.astype(BF)
        else:
            kv_ref[:, lanes] = value.astype(BF)
    kv_out = pltpu.make_async_copy(kv_ref, kv_hbm, lsem.at[26])
    kv_out.start()
    joined.wait()
    down = dot(pt_ref[:, 0:CHANNELS], e_all[0:96].reshape(CHANNELS, 128))
    down_ref[...] = (down + bias * total_shift) * gain
    for n in range(16):
        lanes = slice((n % 8) * 128, (n % 8) * 128 + 128)
        upg_ref[n // 8, :, lanes] = e_all[96 + 4 * n:100 + 4 * n].reshape(64, 128).astype(F32)
    outs = [
        pltpu.make_async_copy(upg_ref, upg_hbm, lsem.at[27]),
        pltpu.make_async_copy(down_ref, down_hbm, lsem.at[28]),
    ]
    for copy in outs:
        copy.start()
    kv_out.wait()
    for copy in outs:
        copy.wait()


def orders():
    tile = [[0.0] * 128 for _ in range(128)]
    seq = [[0.0] * 128 for _ in range(128)]
    for w in range(4):
        for h in range(8):
            for i in range(4):
                tile[(h % 4) * 32 + (h // 4) * 16 + (i // 2) * 8 + w * 2 + i % 2][w * 32 + h * 4 + i] = 1.0
    for ys in range(2):
        for cs in range(2):
            for zs in range(4):
                for w in range(4):
                    for i in range(2):
                        here = (ys * 2 + cs) * 32 + zs * 8 + w * 2 + i
                        seq[i * 64 + ys * 32 + zs * 8 + cs * 4 + w][here] = 1.0
    return jnp.array([tile, seq], BF)


def local(
    feature_grid, depthwise_kernel, depthwise_bias, layer_norm_gain, layer_norm_shift,
    expansion_weight, expansion_bias, reduction_weight, reduction_bias, layer_branch_scale,
    projector_weight, projector_bias, input_norm_gain, key_value_weight, key_value_bias,
    adapter_down_weight, adapter_up_weight, image_start_positions, key_value_cotangent,
):
    cells = feature_grid.transpose(2, 0, 1, 3).reshape(4, 32, CHANNELS)
    freq = np.exp(np.arange(HEAD_DIM // 2, dtype=np.float32) * np.float32(-2.0 * math.log(ROPE_THETA) / HEAD_DIM))
    freq = jnp.array(np.concatenate([freq, freq])[None, :], F32)
    any_space = pl.BlockSpec(memory_space=pl.ANY)
    kv, down, upg = pl.pallas_call(
        kernel,
        out_shape=(
            jax.ShapeDtypeStruct((128, 2048), BF),
            jax.ShapeDtypeStruct((64, 128), F32),
            jax.ShapeDtypeStruct((2, 64, 1024), F32),
        ),
        in_specs=[any_space] * 17 + [pl.BlockSpec(memory_space=pltpu.SMEM)] + [any_space] * 3,
        out_specs=(any_space, any_space, any_space),
        scratch_shapes=[
            pltpu.VMEM((10, 64, CHANNELS), BF),
            pltpu.VMEM((4, 32, CHANNELS), F32),
            pltpu.VMEM((4, 128, CHANNELS), BF),
            pltpu.VMEM((4, CHANNELS, 384), BF),
            pltpu.VMEM((4, 384, CHANNELS), BF),
            pltpu.VMEM((4, 1, 384), F32),
            pltpu.VMEM((128, CHANNELS), F32),
            pltpu.VMEM((256, CHANNELS), F32),
            pltpu.VMEM((4, 4, 32, CHANNELS), BF),
            pltpu.VMEM((3, 4, 32, CHANNELS), BF),
            pltpu.VMEM((4, 4, 8, CHANNELS), F32),
            pltpu.VMEM((4, 32, CHANNELS), BF),
            pltpu.VMEM((4, 32, CHANNELS), BF),
            pltpu.VMEM((8, 64, 2048), BF),
            pltpu.VMEM((5, 12, 2, 16, 128), BF),
            pltpu.VMEM((3, 4, 3, 2, 16, 128), BF),
            pltpu.VMEM((4, 3, 2, 16, 128), BF),
            pltpu.VMEM((3, 3, 2, 16, 128), BF),
            pltpu.VMEM((7, 16, 128), BF),
            pltpu.VMEM((8, 97, 16, 128), BF),
            pltpu.VMEM((5, 12, 2, 16, 256), BF),
            pltpu.VMEM((3, 12, 2, 16, 256), BF),
            pltpu.VMEM((12, 2, 16, 256), BF),
            pltpu.VMEM((3, 3, 2, 16, 256), BF),
            pltpu.VMEM((7, 16, 256), BF),
            pltpu.VMEM((8, 97, 16, 256), BF),
            pltpu.VMEM((128, 19 * 128), F32),
            pltpu.VMEM((128, 2048), BF),
            pltpu.VMEM((2, 16, 6, 16, 128), BF),
            pltpu.VMEM((16, 6, 16, 128), BF),
            pltpu.VMEM((16, 6, 16, 128), BF),
            pltpu.VMEM((15, 6, 16, 128), BF),
            pltpu.VMEM((4, 6, 16, 128), BF),
            pltpu.VMEM((160, 16, 128), BF),
            pltpu.VMEM((64, EXT), BF),
            pltpu.VMEM((8, 64, 384), BF),
            pltpu.VMEM((3, 64, 384), BF),
            pltpu.VMEM((128, 2048), BF),
            pltpu.VMEM((7, 8, CHANNELS), F32),
            pltpu.VMEM((128, 128), F32),
            pltpu.VMEM((128, 128), F32),
            pltpu.VMEM((1, 384), F32),
            pltpu.VMEM((128, 2048), BF),
            pltpu.VMEM((64, 128), F32),
            pltpu.VMEM((2, 64, 1024), F32),
            pltpu.VMEM((4, 32, CHANNELS), BF),
            pltpu.VMEM((7, 7, CHANNELS), BF),
            pltpu.VMEM((CHANNELS,), F32),
            pltpu.VMEM((CHANNELS,), F32),
            pltpu.VMEM((CHANNELS,), F32),
            pltpu.VMEM((384,), F32),
            pltpu.VMEM((CHANNELS,), F32),
            pltpu.VMEM((CHANNELS,), F32),
            pltpu.VMEM((64, CHANNELS), BF),
            pltpu.VMEM((1, 64), BF),
            pltpu.VMEM((1, 64), BF),
            pltpu.VMEM((64, 2048), BF),
            pltpu.VMEM((1, 2048), F32),
            pltpu.VMEM((64, 128), BF),
            pltpu.VMEM((2, 64, 1024), BF),
            pltpu.VMEM((128, 2048), BF),
            pltpu.VMEM((1, 128), F32),
            pltpu.VMEM((2, 128, 128), BF),
            pltpu.SemaphoreType.DMA((COPIES,)),
            pltpu.SemaphoreType.DMA((COPIES,)),
            pltpu.SemaphoreType.DMA((32,)),
        ],
        compiler_params=pltpu.CompilerParams(
            collective_id=0, has_side_effects=True, vmem_limit_bytes=62 << 20
        ),
        cost_estimate=pl.CostEstimate(flops=8_000_000_000, bytes_accessed=30_000_000, transcendentals=0),
    )(
        cells, depthwise_kernel, depthwise_bias, layer_norm_gain, layer_norm_shift,
        expansion_weight, reduction_weight, expansion_bias, reduction_bias,
        layer_branch_scale, projector_weight.T, projector_bias[None, :], input_norm_gain[None, :],
        key_value_weight, key_value_bias[None, :], adapter_down_weight, adapter_up_weight,
        image_start_positions, key_value_cotangent.reshape(128, 2048), freq, orders(),
    )
    return kv.reshape(2, 64, 2048), down, upg


def solution(mesh):
    in_specs = (
        P("row", None, "col", None), P(), P(), P(), P(),
        P(None, "col"), P("col"), P("col", None), P(), P(),
        P(None, ("row", "col")), P(("row", "col")), P(("row", "col")), P(("row", "col"), None), P(),
        P(("row", "col"), None), P(), P(), P(("row", "col"), None, None),
    )
    out_specs = (P(("row", "col"), None, None), P(("row", "col"), None), P())
    return jax.shard_map(local, mesh=mesh, in_specs=in_specs, out_specs=out_specs, check_vma=False)
```
